256 devices in a mesh: seq: 32 (over x_hi, z, core), head: 8 (over x_lo, y).
Axes of the slice: x: 4 (x_hi: 2, x_lo: 2; x = x_hi * 2 + x_lo), y: 4, z: 8, core: 2. Of those that a mesh axis runs over, the one named last changes fastest.
Arguments:
- signal: bfloat16 [32768, 2048], P('seq', 'head'), may hold values from -6 to 6
- write_keys: bfloat16 [32768, 128], P('seq'), may hold values from -1.5 to 1.5
- read_queries: bfloat16 [32768, 128], P('seq'), may hold values from -1.5 to 1.5
- step_sizes: float32 [32, 32768], P('head', 'seq'), may hold values from 0.005 to 0.02
- log_decay: float32 [32, 32768], P('head', 'seq'), as said below
- mirror_heads: int32 [32], replicated, may hold values from 0 to 31, each once
- contig_starts: int32 [4], replicated, may hold values from 1 to 32767
- out_grad: bfloat16 [32768, 2048], P('seq', 'head'), may hold values from -6 to 6
Outputs:
- signal_grad: float32 [32768, 2048], P('seq', 'head')
- write_grad: float32 [32768, 128], P('seq')
- read_grad: float32 [32768, 128], P('seq')
- step_grad: float32 [32, 32768], P('head', 'seq')
- decay_grad: float32 [32, 32768], P('head', 'seq')
The draws below stay inside these ranges and needn't reach their ends.
Inputs may be any that keep to these rules, and one draw needn't show every extreme that they name: `mirror_heads`: a permutation of the 32 heads. `contig_starts`: start positions of contigs, in no particular order, repeats possible. `log_decay`: every entry is negative.
All inputs are finite; a program needn't handle non-finite values.
Results may differ from the reference program's by a relative error of at most 0.0003.
Values sent between devices are 32-bit elements; how exact they have to be, the bound alone decides.
A program may use at most 128 MiB of HBM per device.

```python
import math
import jax
import jax.numpy as jnp
from jax import lax

HEADS = 32
HEAD_DIM = 64
STATE = 128
BLOCK = 256
CONTIG_RESETS = 4
TOK_DEV = 1024
WINDOW_TOKENS = 32768


contig_total = 3


def draw_log_decay(key, part):
    key = jax.random.fold_in(key, 7)
    every_key = jax.random.split(key, 10)
    slow_share = 0.5
    shard_count = WINDOW_TOKENS // TOK_DEV
    forced = jax.random.randint(every_key[8], (), 0, HEADS)
    slow = jax.random.bernoulli(every_key[0], slow_share, (HEADS,)) & (jnp.arange(HEADS) != forced)
    slow_rate = jnp.exp(jax.random.uniform(every_key[1], (HEADS,), jnp.float32, math.log(0.2), math.log(1.0))) / WINDOW_TOKENS
    fast_rate = jax.random.uniform(every_key[2], (HEADS,), jnp.float32, 1.0 / 50.0, 1.0 / 30.0)
    shard_scale = jnp.exp(jax.random.uniform(every_key[3], (HEADS, shard_count, 1), jnp.float32, -0.7, 0.7))
    rough = jax.random.uniform(every_key[4], (HEADS, shard_count, TOK_DEV), jnp.float32, 0.5, 1.5)
    quiet = jax.random.bernoulli(every_key[7], 0.25, (HEADS, shard_count, 1))
    flip = jax.random.bernoulli(every_key[9], 0.5, (HEADS, shard_count, 1))
    ramp = (jnp.arange(TOK_DEV).astype(jnp.float32) + 0.5) / TOK_DEV
    ramp_dir = jnp.where(flip, 1.0 - ramp[None, None, :], ramp[None, None, :])
    slow_part = slow_rate[:, None, None] * shard_scale * 2.0 * ramp_dir * rough
    fast_part = fast_rate[:, None, None] * jnp.where(quiet, 0.001, shard_scale) * rough
    base = -jnp.where(slow[:, None, None], slow_part, fast_part).reshape(HEADS, WINDOW_TOKENS)
    reset_locations = jax.random.randint(every_key[5], (contig_total,), 0, WINDOW_TOKENS)
    hits = jnp.any(jnp.arange(WINDOW_TOKENS)[None, :] == reset_locations[:, None], axis=0).astype(jnp.float32)
    depth = jax.random.uniform(every_key[6], (HEADS,), jnp.float32, 0.22, 0.5)
    return (base - hits[None, :] * depth[:, None]).astype(jnp.float32)


def plant(values, rng, low, top_value):
    place = [jax.random.randint(jax.random.fold_in(rng, axis), (), 0, length) for axis, length in enumerate(values.shape)]
    widest = values.shape.index(max(values.shape))
    beside = place[:widest] + [(place[widest] + 1) % values.shape[widest]] + place[widest + 1:]
    return values.at[tuple(place)].set(low).at[tuple(beside)].set(top_value)


def steps_of(rng, extent, cuts, smallest, largest):
    def one(position, blocks):
        heights = jax.random.uniform(jax.random.fold_in(jax.random.fold_in(rng, 6), position), (blocks,), jnp.float32, smallest / len(cuts), largest / len(cuts))
        return jnp.repeat(jnp.exp(heights), extent[position] // blocks).reshape((-1,) + (1,) * (len(extent) - position - 1))

    gain = one(*cuts[0])
    for cut in cuts[1:]:
        gain = gain * one(*cut)
    return gain


def noise(rng, shape, scale, limit, cuts=(), kind=jnp.bfloat16):
    result = scale * jax.random.normal(rng, shape, jnp.float32)
    if cuts:
        result = result * steps_of(rng, shape, cuts, -0.22, 0.18)
    return jnp.clip(result, -limit, limit).astype(kind)


def setup_inputs(seed: int = 0) -> dict:
    key_list = jax.random.split(jax.random.key(seed), 9)
    signal = noise(key_list[0], (WINDOW_TOKENS, HEADS * HEAD_DIM), 1.0, 6.0, ((0, 32), (1, 8)))
    write_keys = noise(key_list[1], (WINDOW_TOKENS, STATE), 0.25, 1.5, ((0, 32),))
    read_queries = noise(key_list[2], (WINDOW_TOKENS, STATE), 0.25, 1.5, ((0, 32),))
    step_sizes = jnp.clip(0.005 + 0.015 * jax.random.uniform(key_list[3], (HEADS, WINDOW_TOKENS), jnp.float32) ** steps_of(key_list[3], (HEADS, WINDOW_TOKENS), ((0, 8), (1, 32)), -0.2, 0.2), 0.005, 0.02)
    log_decay = draw_log_decay(jax.random.fold_in(key_list[8], 71), 0)
    mirror_heads = jax.random.permutation(key_list[5], HEADS).astype(jnp.int32)
    contig_starts = plant(jax.random.randint(key_list[6], (CONTIG_RESETS,), 1, WINDOW_TOKENS), jax.random.fold_in(key_list[6], 1), 1, WINDOW_TOKENS - 1).astype(jnp.int32)
    out_grad = noise(key_list[7], (WINDOW_TOKENS, HEADS * HEAD_DIM), 1.0, 6.0, ((0, 32), (1, 8)))
    return {"signal": signal, "write_keys": write_keys, "read_queries": read_queries, "step_sizes": step_sizes, "log_decay": log_decay, "mirror_heads": mirror_heads, "contig_starts": contig_starts, "out_grad": out_grad}


highest = lax.Precision.HIGHEST

def block_step(carried_pair, block_data):
    state_in, seg_last = carried_pair
    values, write_rows, read_rows, step_rows, decays, segments = block_data
    cumulative = jnp.cumsum(decays, axis=1)
    places = jnp.arange(segments.shape[0])
    allowed = (places[:, None] >= places[None, :]) & (segments[:, None] == segments[None, :])
    log_gap = cumulative[:, :, None] - cumulative[:, None, :]
    decay_mat = jnp.where(allowed[None], jnp.exp(jnp.where(allowed[None], log_gap, 0.0)), 0.0)
    scores = jnp.dot(read_rows, write_rows.T, precision=highest)
    weights = decay_mat * scores[None] * step_rows[:, None, :]
    inside = jnp.einsum('hts,shp->thp', weights, values, precision=highest)
    entering = jnp.exp(cumulative) * (segments == seg_last).astype(cumulative.dtype)[None, :]
    carried = jnp.einsum('tn,hpn->thp', read_rows, state_in, precision=highest) * entering.T[:, :, None]
    leaving = jnp.exp(cumulative[:, -1:] - cumulative) * (segments == segments[-1]).astype(cumulative.dtype)[None, :] * step_rows
    written = jnp.einsum('shp,sn->hpn', values * leaving.T[:, :, None], write_rows, precision=highest)
    new_state = state_in * entering[:, -1][:, None, None] + written
    return ((new_state, segments[-1]), inside + carried)

def strand(values, write_rows, read_rows, step_rows, decays, segments, seg_before, state_in):
    length, head_count, head_width = values.shape
    block_count = length // BLOCK
    state_dim = write_rows.shape[1]
    blocks = (values.reshape(block_count, BLOCK, head_count, head_width), write_rows.reshape(block_count, BLOCK, state_dim), read_rows.reshape(block_count, BLOCK, state_dim), step_rows.reshape(head_count, block_count, BLOCK).transpose(1, 0, 2), decays.reshape(head_count, block_count, BLOCK).transpose(1, 0, 2), segments.reshape(block_count, BLOCK))
    finale, outputs = lax.scan(jax.checkpoint(block_step), (state_in, seg_before), blocks)
    return (outputs.reshape(length, head_count, head_width), finale[0])

def reference(signal, write_keys, read_queries, step_sizes, log_decay, mirror_heads, contig_starts, out_grad):
    values = signal.astype(jnp.float32).reshape(WINDOW_TOKENS, HEADS, HEAD_DIM)
    write_rows = write_keys.astype(jnp.float32)
    read_rows = read_queries.astype(jnp.float32)
    token_positions = jnp.arange(WINDOW_TOKENS).astype(jnp.int32)
    segments = lax.optimization_barrier(jnp.sum(contig_starts[None, :] <= token_positions[:, None], axis=1)).astype(jnp.int32)
    seg_before = jnp.array(-1, jnp.int32)
    zero_state = jnp.zeros((HEADS, HEAD_DIM, STATE), jnp.float32)

    def strands(values, write_rows, read_rows, step_rows, decays):
        front_out, front_end = strand(values, write_rows, read_rows, step_rows, decays, segments, seg_before, zero_state)
        back_out, back_end = strand(values[::-1], write_rows[::-1], read_rows[::-1], step_rows[mirror_heads][:, ::-1], decays[mirror_heads][:, ::-1], segments[::-1], seg_before, zero_state)
        return front_out + back_out[::-1]
    output, pullback = jax.vjp(strands, values, write_rows, read_rows, step_sizes, log_decay)
    gradients = pullback(out_grad.astype(jnp.float32).reshape(WINDOW_TOKENS, HEADS, HEAD_DIM))
    return (gradients[0].reshape(WINDOW_TOKENS, HEADS * HEAD_DIM), gradients[1], gradients[2], gradients[3], gradients[4])
```

```python
import functools

import jax
import jax.numpy as jnp
from jax import lax
from jax.experimental import pallas as pl
from jax.experimental.pallas import tpu as pltpu
from jax.sharding import PartitionSpec as P

Q = 256
STRIP = 32
LOG2E = 1.4426950408889634
F32, BF16 = jnp.float32, jnp.bfloat16
MESH = pl.DeviceIdType.MESH
VMEM_LIMIT = 56 * 1024 * 1024


def iota(shape, dim):
    return lax.broadcasted_iota(jnp.int32, shape, dim)


def split2(v):
    hi = v.astype(BF16)
    return hi, (v - hi.astype(F32)).astype(BF16)


def split3(v):
    hi = v.astype(BF16)
    rest = v - hi.astype(F32)
    mid = rest.astype(BF16)
    return hi, mid, (rest - mid.astype(F32)).astype(BF16)


def dot(a, b):
    return lax.dot_general(a, b, (((1,), (0,)), ((), ())), preferred_element_type=F32)


def dot_nt(a, b):
    return lax.dot_general(a, b, (((1,), (1,)), ((), ())), preferred_element_type=F32)


def dot_sum(parts, b, how=dot):
    total = how(parts[0], b)
    for part in parts[1:]:
        total = total + how(part, b)
    return total


def greet(peers):
    barrier = pltpu.get_barrier_semaphore()
    for axis, count in peers:
        me = lax.axis_index(axis)

        def one(k, carry, axis=axis, count=count, me=me):
            pl.semaphore_signal(
                barrier, inc=1, device_id={axis: lax.rem(me + k, count)}, device_id_type=MESH
            )
            return carry

        lax.fori_loop(1, count, one, 0)
    pl.semaphore_wait(barrier, sum(count - 1 for _, count in peers))


def push_all(axis, count, source, target, send, recv):
    me = lax.axis_index(axis)

    def copy(k):
        peer = lax.rem(me + k, count)
        return pltpu.make_async_remote_copy(
            src_ref=source(peer),
            dst_ref=target(me),
            send_sem=send.at[k],
            recv_sem=recv.at[k],
            device_id={axis: peer},
            device_id_type=MESH,
        )

    def begin(k, carry):
        copy(k).start()
        return carry

    def end(k, carry):
        copy(k).wait()
        return carry

    lax.fori_loop(1, count, begin, 0)
    return lambda: lax.fori_loop(1, count, end, 0)


def gather_kernel(nh, step_ref, decay_ref, all_ref, send, recv):
    me = lax.axis_index("head")
    all_ref[me, 0:4, :] = step_ref[...]
    all_ref[me, 4:8, :] = decay_ref[...]
    greet([("head", nh)])
    push_all("head", nh, lambda peer: all_ref.at[me], lambda me: all_ref.at[me], send, recv)()


def segment_at(starts_ref, t):
    total = (starts_ref[0] <= t).astype(jnp.int32)
    for k in range(1, 4):
        total = total + (starts_ref[k] <= t).astype(jnp.int32)
    return total


def prep_kernel(
    ns,
    heads_ref,
    starts_ref,
    x_ref,
    g_ref,
    b_ref,
    c_ref,
    all_ref,
    snd_ref,
    rows_ref,
    cols_ref,
    xhi_ref,
    xlo_ref,
    ghi_ref,
    glo_ref,
    el_ref,
    ends_ref,
    seeds_ref,
    gain_ref,
):
    length = x_ref.shape[0]
    chunks = length // Q
    me = lax.axis_index("head")
    offset = lax.axis_index("seq") * length
    lower = iota((Q, Q), 0) >= iota((Q, Q), 1)
    upper = iota((Q, Q), 0) <= iota((Q, Q), 1)
    low_one = jnp.where(lower, 1.0, 0.0).astype(BF16)
    up_one = jnp.where(upper, 1.0, 0.0).astype(BF16)
    front8 = iota((8, Q), 0) < 4
    lane = iota((32, 1024), 1)
    quantity = lane // 256
    source = jnp.where(quantity < 2, 16, 8) + (quantity % 2) * 4 + (lane % 256) // 64
    spread = jnp.where(iota((32, 1024), 0) == source, 1.0, 0.0).astype(BF16)
    pick8 = jnp.where(iota((8, 512), 0) == iota((8, 512), 1) // 64, 1.0, 0.0)

    def chunk(c, carry):
        base = pl.multiple_of(c * Q, Q)
        span = pl.ds(base, Q)
        own = all_ref[me, :, span]
        others = []
        for h in range(4):
            head = heads_ref[me * 4 + h]
            others.append(
                (all_ref[head // 4, pl.ds(head % 4, 1), span], all_ref[head // 4, pl.ds(head % 4 + 4, 1), span])
            )
        s8 = jnp.concatenate([own[0:4]] + [o[0] for o in others], axis=0)
        d8 = jnp.concatenate([own[4:8]] + [o[1] for o in others], axis=0)
        d3 = split3(d8)
        cum8 = jnp.where(front8, dot_sum(d3, up_one), dot_sum(d3, low_one)) * LOG2E
        total8 = jnp.where(front8[:, 0:1], cum8[:, Q - 1 : Q], cum8[:, 0:1])
        first = offset + base
        seg = segment_at(starts_ref, first + iota((8, Q), 1))
        seg_first, seg_last = segment_at(starts_ref, first), segment_at(starts_ref, first + Q - 1)
        seg_before = jnp.where(first == 0, -1, segment_at(starts_ref, first - 1))
        seg_after = segment_at(starts_ref, first + Q)
        enters = jnp.where(front8, seg_before, seg_after) == seg
        leaves = jnp.where(front8, seg_last, seg_first) == seg
        e8 = jnp.where(enters, jnp.exp2(cum8), 0.0)
        l8 = jnp.where(leaves, jnp.exp2(total8 - cum8) * s8, 0.0)
        through = jnp.where(
            front8[:, 0:1],
            (seg_before == seg_last).astype(F32),
            (seg_after == seg_first).astype(F32),
        )
        gain8 = jnp.exp2(total8) * through
        gain = jnp.sum(pick8 * gain8, axis=0, keepdims=True)
        gain_ref[c] = jnp.broadcast_to(gain, (8, 512))
        rows = jnp.concatenate([cum8, e8, l8, s8], axis=0)
        rows_ref[c] = rows
        cols = rows.T
        cols_ref[span, :] = cols
        wide = dot_sum(split3(cols), spread)
        el_ref[span, :] = wide[:, 0:512]
        x2 = jnp.concatenate([x_ref[span, :]] * 2, axis=1).astype(F32) * wide[:, 0:512]
        g2 = jnp.concatenate([g_ref[span, :]] * 2, axis=1).astype(F32) * wide[:, 512:1024]
        xhi, xlo = split2(x2)
        ghi, glo = split2(g2)
        xhi_ref[span, :] = xhi
        xlo_ref[span, :] = xlo
        ghi_ref[span, :] = ghi
        glo_ref[span, :] = glo
        bt, ct = b_ref[span, :].T, c_ref[span, :].T
        ends_ref[c] = dot(bt, xhi) + dot(bt, xlo)
        seeds_ref[c] = dot(ct, ghi) + dot(ct, glo)
        return carry

    lax.fori_loop(0, chunks, chunk, 0)

    front, mirror = slice(0, 256), slice(256, 512)
    rows_of_slice = 256 // ns
    half_count = ns // 2

    def put(q, value):
        for k in range(2):
            snd_ref[k * half_count : (k + 1) * half_count, q] = value[:, k * 128 : (k + 1) * 128].reshape(
                half_count, rows_of_slice, 128
            )

    for q, terms, lanes, order in (
        (0, ends_ref, front, range(chunks)),
        (1, seeds_ref, mirror, range(chunks)),
        (2, ends_ref, mirror, range(chunks - 1, -1, -1)),
        (3, seeds_ref, front, range(chunks - 1, -1, -1)),
    ):
        run = None
        for c in order:
            run = terms[c, :, lanes] if run is None else run * gain_ref[c, 0:1, lanes] + terms[c, :, lanes]
        put(q, run)
    whole = gain_ref[0]
    for c in range(1, chunks):
        whole = whole * gain_ref[c]
    for k in range(2):
        both = jnp.where(
            iota((8, 128), 0) < 4, whole[:, k * 128 : (k + 1) * 128], whole[:, 256 + k * 128 : 256 + (k + 1) * 128]
        )
        snd_ref[k * half_count : (k + 1) * half_count, 4, 0:8] = jnp.broadcast_to(both[None], (half_count, 8, 128))


def scan_kernel(ns, snd_ref, in_ref, got, out, send1, recv1, send2, recv2):
    me = lax.axis_index("seq")
    got[me] = snd_ref[me]
    greet([("seq", ns)])
    push_all("seq", ns, lambda peer: snd_ref.at[peer], lambda me: got.at[me], send1, recv1)()

    zero = jnp.zeros(got.shape[2:], F32)

    def up(k, runs):
        front, mirror = runs
        out[k, 0] = front
        out[k, 1] = mirror
        return (got[k, 4, 0:1] * front + got[k, 0], got[k, 4, 4:5] * mirror + got[k, 1])

    def down(i, runs):
        k = ns - 1 - i
        mirror, front = runs
        out[k, 2] = mirror
        out[k, 3] = front
        return (got[k, 4, 4:5] * mirror + got[k, 2], got[k, 4, 0:1] * front + got[k, 3])

    lax.fori_loop(0, ns, up, (zero, zero))
    lax.fori_loop(0, ns, down, (zero, zero))
    in_ref[me] = out[me]
    push_all("seq", ns, lambda peer: out.at[peer], lambda me: in_ref.at[me], send2, recv2)()


def main_kernel(
    ns,
    starts_ref,
    x_ref,
    g_ref,
    b_ref,
    c_ref,
    in_ref,
    rows_ref,
    cols_ref,
    xhi_ref,
    xlo_ref,
    ghi_ref,
    glo_ref,
    el_ref,
    ends_ref,
    seeds_ref,
    gain_ref,
    dx_ref,
    db_ref,
    dc_ref,
    own_ref,
    other_ref,
    states,
    adjoints,
    gm,
    pt,
    whi,
    wlo,
    dghi,
    dglo,
    csum,
):
    length = x_ref.shape[0]
    chunks = length // Q
    offset = lax.axis_index("seq") * length
    half_count = ns // 2
    front, mirror = slice(0, 256), slice(256, 512)

    def incoming(q):
        return jnp.concatenate(
            [in_ref[k * half_count : (k + 1) * half_count, q].reshape(128, 128) for k in range(2)], axis=1
        )

    run = incoming(0)
    for c in range(chunks):
        states[c, :, front] = run
        run = run * gain_ref[c, 0:1, front] + ends_ref[c, :, front]
    states[chunks, :, front] = run
    run = incoming(2)
    for c in range(chunks - 1, -1, -1):
        states[c, :, mirror] = run
        run = run * gain_ref[c, 0:1, mirror] + ends_ref[c, :, mirror]
    states[chunks, :, mirror] = run
    run = incoming(3)
    for c in range(chunks - 1, -1, -1):
        adjoints[c, :, front] = run
        run = run * gain_ref[c, 0:1, front] + seeds_ref[c, :, front]
    run = incoming(1)
    for c in range(chunks):
        adjoints[c, :, mirror] = run
        run = run * gain_ref[c, 0:1, mirror] + seeds_ref[c, :, mirror]

    lower = iota((Q, Q), 0) >= iota((Q, Q), 1)
    upper = iota((Q, Q), 0) <= iota((Q, Q), 1)
    low_one = jnp.where(lower, 1.0, 0.0).astype(BF16)
    up_one = jnp.where(upper, 1.0, 0.0).astype(BF16)
    front8 = iota((8, Q), 0) < 4
    pick = jnp.where(iota((8, 512), 0) == iota((8, 512), 1) // 64, 1.0, 0.0)
    pick_bf = pick.astype(BF16)
    pick2_bf = jnp.where(iota((8, 256), 0) % 4 == iota((8, 256), 1) // 64, 1.0, 0.0).astype(BF16)
    ones_bf = jnp.ones((8, 128), BF16)
    half_mask = [
        jnp.where(iota((1, 128), 1) // 64 == k, 1.0, 0.0).astype(BF16) for k in range(2)
    ]
    zero_row = jnp.zeros((8, 128), F32)

    def chunk(c, carry):
        base = pl.multiple_of(c * Q, Q)
        span = pl.ds(base, Q)
        first = offset + base
        bc, cc = b_ref[span, :], c_ref[span, :]
        xs = [x_ref[span, k * 128 : (k + 1) * 128] for k in range(2)]
        gs = [g_ref[span, k * 128 : (k + 1) * 128] for k in range(2)]

        seg_s = segment_at(starts_ref, first + iota((Q, 1), 0))
        seg_t = segment_at(starts_ref, first + iota((1, Q), 1))
        gm[...] = jnp.where(seg_s == seg_t, dot_nt(bc, cc), 0.0)
        for h in range(4):
            pt[h] = dot_nt(xs[h // 2] * half_mask[h % 2], gs[h // 2])
        row_sums = []
        for i in range(2):

            def strip(r, sums, i=i):
                start = pl.multiple_of(i * 128 + r * STRIP, STRIP)
                at = pl.ds(start, STRIP)
                col = cols_ref[pl.ds(pl.multiple_of(base + start, STRIP), STRIP), :]
                lane128 = iota((STRIP, 128), 1)
                s_index = r * STRIP + iota((STRIP, 128), 0)
                ahead = lane128 > s_index
                behind = lane128 < s_index
                sums = list(sums)
                collected = jnp.zeros((STRIP, 128), F32)
                dg = [jnp.zeros((STRIP, 128), F32) for _ in range(2)]
                for h in range(4):
                    cum_f, cum_m = col[:, h : h + 1], col[:, 4 + h : 5 + h]
                    step_f, step_m = col[:, 24 + h : 25 + h], col[:, 28 + h : 29 + h]
                    lane_sums = [None, None]
                    for j in range(2):
                        t = slice(j * 128, (j + 1) * 128)
                        row_f = rows_ref[c, h : h + 1, t]
                        row_m = rows_ref[c, 4 + h : 5 + h, t]
                        if i == j:
                            gap = jnp.where(behind, row_m - cum_m, row_f - cum_f)
                            step = jnp.where(behind, step_m, jnp.where(ahead, step_f, step_f + step_m))
                        elif j > i:
                            gap, step = row_f - cum_f, step_f
                        else:
                            gap, step = row_m - cum_m, step_m
                        d = jnp.exp2(gap) * step
                        w = d * gm[at, t]
                        p = pt[h, at, t]
                        dg[j] = dg[j] + d * p
                        e = w * p
                        hi, lo = split2(w)
                        whi[h, at, t] = hi
                        wlo[h, at, t] = lo
                        if i == j:
                            parts = [jnp.where(ahead, e, 0.0), jnp.where(behind, e, 0.0)]
                        else:
                            parts = [e, None] if j > i else [None, e]
                        for strand in range(2):
                            part = parts[strand]
                            if part is None:
                                continue
                            slot = (h * 2 + j) * 2 + strand
                            add = part[0:8]
                            for u in range(1, STRIP // 8):
                                add = add + part[u * 8 : (u + 1) * 8]
                            sums[slot] = sums[slot] + add
                            old = lane_sums[strand]
                            lane_sums[strand] = part if old is None else old + part
                    for strand in range(2):
                        total = jnp.sum(lane_sums[strand], axis=1, keepdims=True)
                        collected = jnp.where(lane128 == strand * 4 + h, total, collected)
                csum[at, :] = collected
                for j in range(2):
                    t = slice(j * 128, (j + 1) * 128)
                    same = seg_mask(at, t, r, i, j)
                    hi, lo = split2(jnp.where(same, dg[j], 0.0))
                    dghi[at, t] = hi
                    dglo[at, t] = lo
                return tuple(sums)

            def seg_mask(at, t, r, i, j):
                rows_at = first + i * 128 + r * STRIP + iota((STRIP, 1), 0)
                cols_at = first + j * 128 + iota((1, 128), 1)
                return segment_at(starts_ref, rows_at) == segment_at(starts_ref, cols_at)

            row_sums.append(lax.fori_loop(0, 128 // STRIP, strip, (zero_row,) * 16))
        rows_in = []
        for strand in range(2):
            for h in range(4):
                lanes = []
                for j in range(2):
                    slot = (h * 2 + j) * 2 + strand
                    lanes.append(jnp.sum(row_sums[0][slot] + row_sums[1][slot], axis=0, keepdims=True))
                rows_in.append(jnp.concatenate(lanes, axis=1))
        row8 = jnp.concatenate(rows_in, axis=0)
        col8 = csum[...].T[0:8]

        state_hi, state_lo = split2(states[c])
        adj_hi, adj_lo = split2(adjoints[c])
        xhi, xlo, ghi, glo = xhi_ref[span, :], xlo_ref[span, :], ghi_ref[span, :], glo_ref[span, :]
        v = dot(bc, adj_hi) + dot(bc, adj_lo)
        y = dot(cc, state_hi) + dot(cc, state_lo)
        scaled = el_ref[span, :] * v
        db = dot_nt(xhi, adj_hi) + dot_nt(xlo, adj_hi) + dot_nt(xhi, adj_lo)
        dc = dot_nt(ghi, state_hi) + dot_nt(glo, state_hi) + dot_nt(ghi, state_lo)
        x_prod = split2((xhi.astype(F32) + xlo.astype(F32)) * v)
        g_prod = split2((ghi.astype(F32) + glo.astype(F32)) * y)
        col8 = col8 + dot_nt(pick_bf, x_prod[0]) + dot_nt(pick_bf, x_prod[1])
        row8 = row8 + dot_nt(pick_bf, g_prod[0]) + dot_nt(pick_bf, g_prod[1])

        for k in range(2):
            lanes = slice(k * 128, (k + 1) * 128)
            total = scaled[:, k * 128 : (k + 1) * 128] + scaled[:, 256 + k * 128 : 256 + (k + 1) * 128]
            for h in (2 * k, 2 * k + 1):
                masked = gs[k] * half_mask[h % 2]
                total = total + dot(whi[h], masked) + dot(wlo[h], masked)
            dx_ref[span, lanes] = total
        db_ref[span, :] = db + dot(dghi[...], cc) + dot(dglo[...], cc)
        dgt_hi, dgt_lo = dghi[...].T, dglo[...].T
        dc_ref[span, :] = dc + dot(dgt_hi, bc) + dot(dgt_lo, bc)

        bc_prod = split2(bc.astype(F32) * cc.astype(F32))
        score8 = dot_nt(ones_bf, bc_prod[0]) + dot_nt(ones_bf, bc_prod[1])
        xg = split2(x_ref[span, :].astype(F32) * g_ref[span, :].astype(F32))
        pair8 = dot_nt(pick2_bf, xg[0]) + dot_nt(pick2_bf, xg[1])
        step8 = col8 / rows_ref[c, 24:32, :] + score8 * pair8
        flow_f = jnp.sum(states[c + 1, :, front] * adjoints[c, :, front], axis=0, keepdims=True)
        under = jnp.where(c == 0, chunks, c - 1)
        flow_m = jnp.sum(states[under, :, mirror] * adjoints[c, :, mirror], axis=0, keepdims=True)
        flow = jnp.concatenate([flow_f, flow_m], axis=1)
        flow8 = jnp.sum(pick * flow, axis=1, keepdims=True)
        diff = split3(row8 - col8)
        decay8 = jnp.where(front8, dot_sum(diff, low_one), dot_sum(diff, up_one)) + flow8
        own_ref[0:4, span] = step8[0:4]
        own_ref[4:8, span] = decay8[0:4]
        other_ref[0:4, span] = step8[4:8]
        other_ref[4:8, span] = decay8[4:8]
        return carry

    lax.fori_loop(0, chunks, chunk, 0)


def reduce_kernel(
    nh, heads_ref, db_ref, dc_ref, own_ref, other_ref, bout_ref, cout_ref, step_ref, decay_ref, got, mine, others, sems
):
    me = lax.axis_index("head")
    others[me] = other_ref[...]
    greet([("head", nh)])
    sent_b = push_all("head", nh, lambda peer: db_ref.at[peer], lambda me: got.at[me, 0], sems.at[0], sems.at[1])
    sent_c = push_all("head", nh, lambda peer: dc_ref.at[peer], lambda me: got.at[me, 1], sems.at[2], sems.at[3])
    sent_o = push_all("head", nh, lambda peer: other_ref, lambda me: others.at[me], sems.at[4], sems.at[5])
    got[me, 0] = db_ref[me]
    got[me, 1] = dc_ref[me]
    sent_b()
    total = got[0, 0]
    for k in range(1, nh):
        total = total + got[k, 0]
    mine[0] = total
    bout_ref[me] = total
    back_b = push_all("head", nh, lambda peer: mine.at[0], lambda me: bout_ref.at[me], sems.at[6], sems.at[7])
    sent_c()
    total = got[0, 1]
    for k in range(1, nh):
        total = total + got[k, 1]
    mine[1] = total
    cout_ref[me] = total
    back_c = push_all("head", nh, lambda peer: mine.at[1], lambda me: cout_ref.at[me], sems.at[8], sems.at[9])
    sent_o()
    for h in range(4):
        place = 0 * me
        for k in range(nh * 4):
            place = jnp.where(heads_ref[k] == me * 4 + h, k, place)
        step_ref[h : h + 1, :] = own_ref[h : h + 1, :] + others[place // 4, pl.ds(place % 4, 1), :]
        decay_ref[h : h + 1, :] = own_ref[4 + h : 5 + h, :] + others[place // 4, pl.ds(place % 4 + 4, 1), :]
    back_b()
    back_c()


def on_device(signal, write_keys, read_queries, step_sizes, log_decay, mirror_heads, contig_starts, out_grad):
    nh, ns = lax.axis_size("head"), lax.axis_size("seq")
    length = signal.shape[0]
    chunks = length // Q
    rows_of_slice = 256 // ns
    vmem = pl.BlockSpec(memory_space=pltpu.VMEM)
    smem = pl.BlockSpec(memory_space=pltpu.SMEM)

    def shape(*dims, dtype=F32):
        return jax.ShapeDtypeStruct(dims, dtype)

    def params(**more):
        return pltpu.CompilerParams(vmem_limit_bytes=VMEM_LIMIT, **more)

    gathered = pl.pallas_call(
        functools.partial(gather_kernel, nh),
        out_shape=shape(nh, 8, length),
        in_specs=[vmem] * 2,
        out_specs=vmem,
        scratch_shapes=[pltpu.SemaphoreType.DMA((nh,)), pltpu.SemaphoreType.DMA((nh,))],
        compiler_params=params(collective_id=0, has_side_effects=True),
        name="gather",
    )(step_sizes, log_decay)

    prepared = pl.pallas_call(
        functools.partial(prep_kernel, ns),
        out_shape=[
            shape(ns, 5, rows_of_slice, 128),
            shape(chunks, 32, Q),
            shape(length, 32),
            shape(length, 512, dtype=BF16),
            shape(length, 512, dtype=BF16),
            shape(length, 512, dtype=BF16),
            shape(length, 512, dtype=BF16),
            shape(length, 512),
            shape(chunks, 128, 512),
            shape(chunks, 128, 512),
            shape(chunks, 8, 512),
        ],
        in_specs=[smem] * 2 + [vmem] * 5,
        out_specs=[vmem] * 11,
        compiler_params=params(),
        name="prep",
    )(mirror_heads, contig_starts, signal, out_grad, write_keys, read_queries, gathered)
    slices, kept = prepared[0], prepared[1:]

    incoming = pl.pallas_call(
        functools.partial(scan_kernel, ns),
        out_shape=shape(ns, 4, rows_of_slice, 128),
        in_specs=[vmem],
        out_specs=vmem,
        scratch_shapes=[pltpu.VMEM((ns, 5, rows_of_slice, 128), F32), pltpu.VMEM((ns, 4, rows_of_slice, 128), F32)]
        + [pltpu.SemaphoreType.DMA((ns,))] * 4,
        compiler_params=params(collective_id=1, has_side_effects=True),
        name="scan",
    )(slices)

    dx, db, dc, own, other = pl.pallas_call(
        functools.partial(main_kernel, ns),
        out_shape=[shape(length, 256), shape(length, 128), shape(length, 128), shape(8, length), shape(8, length)],
        in_specs=[smem] + [vmem] * 15,
        out_specs=[vmem] * 5,
        scratch_shapes=[
            pltpu.VMEM((chunks + 1, 128, 512), F32),
            pltpu.VMEM((chunks, 128, 512), F32),
            pltpu.VMEM((Q, Q), F32),
            pltpu.VMEM((4, Q, Q), F32),
            pltpu.VMEM((4, Q, Q), BF16),
            pltpu.VMEM((4, Q, Q), BF16),
            pltpu.VMEM((Q, Q), BF16),
            pltpu.VMEM((Q, Q), BF16),
            pltpu.VMEM((Q, 128), F32),
        ],
        compiler_params=params(),
        name="main",
    )(contig_starts, signal, out_grad, write_keys, read_queries, incoming, *kept)

    part = length // nh
    bsum, csum, step_grad, decay_grad = pl.pallas_call(
        functools.partial(reduce_kernel, nh),
        out_shape=[shape(nh, part, 128), shape(nh, part, 128), shape(4, length), shape(4, length)],
        in_specs=[smem] + [vmem] * 4,
        out_specs=[vmem] * 4,
        scratch_shapes=[
            pltpu.VMEM((nh, 2, part, 128), F32),
            pltpu.VMEM((2, part, 128), F32),
            pltpu.VMEM((nh, 8, length), F32),
            pltpu.SemaphoreType.DMA((10, nh)),
        ],
        compiler_params=params(collective_id=2, has_side_effects=True),
        name="reduce",
    )(mirror_heads, db.reshape(nh, part, 128), dc.reshape(nh, part, 128), own, other)
    return dx, bsum.reshape(length, 128), csum.reshape(length, 128), step_grad, decay_grad


def solution(mesh):
    return jax.shard_map(
        on_device,
        mesh=mesh,
        in_specs=(
            P("seq", "head"),
            P("seq", None),
            P("seq", None),
            P("head", "seq"),
            P("head", "seq"),
            P(),
            P(),
            P("seq", "head"),
        ),
        out_specs=(
            P("seq", "head"),
            P("seq", None),
            P("seq", None),
            P("head", "seq"),
            P("head", "seq"),
        ),
        check_vma=False,
    )
```

```python
import functools

import jax
import jax.numpy as jnp
from jax import lax
from jax.experimental import pallas as pl
from jax.experimental.pallas import tpu as pltpu
from jax.sharding import PartitionSpec as P

Q = 256
STRIP = 32
LOG2E = 1.4426950408889634
F32, BF16 = jnp.float32, jnp.bfloat16
MESH = pl.DeviceIdType.MESH
VMEM_LIMIT = 56 * 1024 * 1024


def iota(shape, dim):
    return lax.broadcasted_iota(jnp.int32, shape, dim)


def split2(v):
    hi = v.astype(BF16)
    return hi, (v - hi.astype(F32)).astype(BF16)


def split3(v):
    hi = v.astype(BF16)
    rest = v - hi.astype(F32)
    mid = rest.astype(BF16)
    return hi, mid, (rest - mid.astype(F32)).astype(BF16)


def dot(a, b):
    return lax.dot_general(a, b, (((1,), (0,)), ((), ())), preferred_element_type=F32)


def dot_nt(a, b):
    return lax.dot_general(a, b, (((1,), (1,)), ((), ())), preferred_element_type=F32)


def dot_sum(parts, b, how=dot):
    total = how(parts[0], b)
    for part in parts[1:]:
        total = total + how(part, b)
    return total


def segment_at(starts_ref, t):
    total = (starts_ref[0] <= t).astype(jnp.int32)
    for k in range(1, 4):
        total = total + (starts_ref[k] <= t).astype(jnp.int32)
    return total


FRONT, MIRROR = slice(0, 256), slice(256, 512)
STRANDS = (FRONT, MIRROR)


def kernel(
    nh,
    ns,
    heads_ref,
    starts_ref,
    x_ref,
    g_ref,
    b_ref,
    c_ref,
    step_ref,
    decay_ref,
    dx_ref,
    sums_ref,
    dstep_ref,
    ddecay_ref,
    all_ref,
    rows_ref,
    cols_ref,
    xhi_ref,
    xlo_ref,
    ghi_ref,
    glo_ref,
    el_ref,
    ends_ref,
    seeds_ref,
    gain_ref,
    pair_out,
    pair_in,
    slice_out,
    slice_in,
    scan_out,
    total_out,
    total_in,
    back_in,
    next_out,
    entering,
    states,
    adjoints,
    gm,
    pt,
    whi,
    wlo,
    dghi,
    dglo,
    csum,
    row_keep,
    col_keep,
    part,
    got,
    own_ref,
    other_ref,
    others,
    gather_sems,
    pair_sems,
    z_sems,
    head_sems,
    other_sems,
):
    length = x_ref.shape[0]
    chunks = length // Q
    head_me = lax.axis_index("head")
    seq_me = lax.axis_index("seq")
    offset = seq_me * length
    core = lax.rem(seq_me, 2)
    zs = ns // 4
    z_me = lax.rem(seq_me // 2, zs)
    x_me = seq_me // (2 * zs)
    core_peer = seq_me + 1 - 2 * core
    x_peer = lax.rem(seq_me + ns // 2, ns)

    def z_peer(k):
        z = lax.rem(z_me + k, zs)
        return z, x_me * 2 * zs + z * 2 + core

    all_ref[head_me, 0:4, :] = step_ref[...]
    all_ref[head_me, 4:8, :] = decay_ref[...]
    barrier = pltpu.get_barrier_semaphore()

    def greet_head(k, carry):
        peer = lax.rem(head_me + k, nh)
        pl.semaphore_signal(barrier, inc=1, device_id={"head": peer}, device_id_type=MESH)
        return carry

    def greet_z(k, carry):
        pl.semaphore_signal(barrier, inc=1, device_id={"seq": z_peer(k)[1]}, device_id_type=MESH)
        return carry

    lax.fori_loop(1, nh, greet_head, 0)
    lax.fori_loop(1, zs, greet_z, 0)
    pl.semaphore_signal(barrier, inc=1, device_id={"seq": core_peer}, device_id_type=MESH)
    pl.semaphore_signal(barrier, inc=1, device_id={"seq": x_peer}, device_id_type=MESH)
    pl.semaphore_wait(barrier, nh + zs)

    def remote(source, target, send, recv, axis, peer):
        return pltpu.make_async_remote_copy(
            src_ref=source,
            dst_ref=target,
            send_sem=send,
            recv_sem=recv,
            device_id={axis: peer},
            device_id_type=MESH,
        )

    def every(count, copy):
        def begin(k, carry):
            copy(k).start()
            return carry

        def end(k, carry):
            copy(k).wait()
            return carry

        lax.fori_loop(1, count, begin, 0)
        return lambda: lax.fori_loop(1, count, end, 0)

    def head_copies(source, target, send, recv):
        def copy(k):
            peer = lax.rem(head_me + k, nh)
            return remote(source(peer), target, send.at[k], recv.at[k], "head", peer)

        return every(nh, copy)

    def z_copies(source, target, send, recv):
        def copy(k):
            z, peer = z_peer(k)
            return remote(source(z), target, send.at[k], recv.at[k], "seq", peer)

        return every(zs, copy)

    gathered = head_copies(
        lambda peer: all_ref.at[head_me], all_ref.at[head_me], gather_sems.at[0], gather_sems.at[1]
    )

    lower = iota((Q, Q), 0) >= iota((Q, Q), 1)
    upper = iota((Q, Q), 0) <= iota((Q, Q), 1)
    low_one = jnp.where(lower, 1.0, 0.0).astype(BF16)
    up_one = jnp.where(upper, 1.0, 0.0).astype(BF16)
    lane = iota((16, 512), 1)
    source = jnp.where(lane < 256, 8, 4) + (lane % 256) // 64
    spread = jnp.where(iota((16, 512), 0) == source, 1.0, 0.0).astype(BF16)
    pick8 = jnp.where(iota((8, 256), 0) == iota((8, 256), 1) // 64, 1.0, 0.0)


    def prepare(strand):
        def chunk(c, carry):
            base = pl.multiple_of(c * Q, Q)
            span = pl.ds(base, Q)
            if strand == 0:
                s4 = all_ref[head_me, 0:4, span]
                d4 = all_ref[head_me, 4:8, span]
            else:
                heads = [heads_ref[head_me * 4 + h] for h in range(4)]
                s4 = jnp.concatenate([all_ref[i // 4, pl.ds(i % 4, 1), span] for i in heads], axis=0)
                d4 = jnp.concatenate([all_ref[i // 4, pl.ds(i % 4 + 4, 1), span] for i in heads], axis=0)
            s8 = jnp.concatenate([s4, s4], axis=0)
            d8 = jnp.concatenate([d4, d4], axis=0)
            cum8 = dot_sum(split3(d8), low_one if strand else up_one) * LOG2E
            total8 = cum8[:, 0:1] if strand else cum8[:, Q - 1 : Q]
            first = offset + base
            seg = segment_at(starts_ref, first + iota((8, Q), 1))
            seg_first, seg_last = segment_at(starts_ref, first), segment_at(starts_ref, first + Q - 1)
            if strand:
                seg_in, seg_near, seg_far = segment_at(starts_ref, first + Q), seg_last, seg_first
            else:
                seg_in = jnp.where(first == 0, -1, segment_at(starts_ref, first - 1))
                seg_near, seg_far = seg_first, seg_last
            del seg_near
            e8 = jnp.where(seg == seg_in, jnp.exp2(cum8), 0.0)
            l8 = jnp.where(seg == seg_far, jnp.exp2(total8 - cum8) * s8, 0.0)
            gain8 = jnp.exp2(total8) * (seg_in == seg_far).astype(F32)
            gain = jnp.sum(pick8 * gain8, axis=0, keepdims=True)
            gain_ref[c, :, STRANDS[strand]] = jnp.broadcast_to(gain, (8, 256))
            rows = jnp.concatenate([cum8[0:4], e8[0:4], l8[0:4], s8[0:4]], axis=0)
            rows_ref[c, strand] = rows
            cols = rows.T
            cols_ref[strand, span, :] = cols
            wide = dot_sum(split3(cols), spread)
            lanes = STRANDS[strand]
            el_ref[span, lanes] = wide[:, 0:256]
            xhi, xlo = split2(x_ref[span, :].astype(F32) * wide[:, 0:256])
            ghi, glo = split2(g_ref[span, :].astype(F32) * wide[:, 256:512])
            xhi_ref[span, lanes] = xhi
            xlo_ref[span, lanes] = xlo
            ghi_ref[span, lanes] = ghi
            glo_ref[span, lanes] = glo
            bt, ct = b_ref[span, :].T, c_ref[span, :].T
            ends_ref[c, :, lanes] = dot(bt, xhi) + dot(bt, xlo)
            seeds_ref[c, :, lanes] = dot(ct, ghi) + dot(ct, glo)
            return carry

        lax.fori_loop(0, chunks, chunk, 0)

    prepare(0)
    gathered()
    prepare(1)

    whole = gain_ref[0]
    for c in range(1, chunks):
        whole = whole * gain_ref[c]
    ascending, descending = range(chunks), range(chunks - 1, -1, -1)
    quantities = (
        (ends_ref, FRONT, ascending),
        (seeds_ref, MIRROR, ascending),
        (ends_ref, MIRROR, descending),
        (seeds_ref, FRONT, descending),
    )
    for q, (terms, lanes, order) in enumerate(quantities):
        run = None
        for c in order:
            run = terms[c, :, lanes] if run is None else run * gain_ref[c, 0:1, lanes] + terms[c, :, lanes]
        for k in range(2):
            pair_out[q // 2, (q % 2) * 256 + k * 128 : (q % 2) * 256 + (k + 1) * 128] = run[:, k * 128 : (k + 1) * 128]
    for p in range(2):
        for a in range(2):
            lanes = STRANDS[(p + a) % 2]
            gains = whole[:, lanes]
            for k in range(2):
                pair_out[p, 512 + (a * 2 + k) * 8 : 512 + (a * 2 + k + 1) * 8] = gains[:, k * 128 : (k + 1) * 128]


    half_mask = [jnp.where(iota((1, 128), 1) // 64 == k, 1.0, 0.0).astype(BF16) for k in range(2)]
    zero_row = jnp.zeros((8, 128), F32)
    part_rows = Q // nh

    def put_part(c, lanes, value):
        part[c, :, :, lanes] = value.reshape(nh, part_rows, 128)

    def inside(c):
        base = c * Q
        span = slice(base, base + Q)
        first = offset + base
        bc, cc = b_ref[span, :], c_ref[span, :]
        xs = [x_ref[span, k * 128 : (k + 1) * 128] for k in range(2)]
        gs = [g_ref[span, k * 128 : (k + 1) * 128] for k in range(2)]
        seg_s = segment_at(starts_ref, first + iota((Q, 1), 0))
        seg_t = segment_at(starts_ref, first + iota((1, Q), 1))
        gm[...] = jnp.where(seg_s == seg_t, dot_nt(bc, cc), 0.0)
        for h in range(4):
            pt[h] = dot_nt(xs[h // 2] * half_mask[h % 2], gs[h // 2])
        row_sums = []
        for i in range(2):

            def strip(r, sums, i=i):
                start = pl.multiple_of(i * 128 + r * STRIP, STRIP)
                at = pl.ds(start, STRIP)
                at_cols = pl.ds(pl.multiple_of(base + start, STRIP), STRIP)
                col_f, col_m = cols_ref[0, at_cols, :], cols_ref[1, at_cols, :]
                lane128 = iota((STRIP, 128), 1)
                s_index = r * STRIP + iota((STRIP, 128), 0)
                ahead = lane128 > s_index
                behind = lane128 < s_index
                sums = list(sums)
                collected = jnp.zeros((STRIP, 128), F32)
                dg = [jnp.zeros((STRIP, 128), F32) for _ in range(2)]
                for h in range(4):
                    cum_f, cum_m = col_f[:, h : h + 1], col_m[:, h : h + 1]
                    step_f, step_m = col_f[:, 12 + h : 13 + h], col_m[:, 12 + h : 13 + h]
                    lane_sums = [None, None]
                    for j in range(2):
                        t = slice(j * 128, (j + 1) * 128)
                        row_f = rows_ref[c, 0, h : h + 1, t]
                        row_m = rows_ref[c, 1, h : h + 1, t]
                        if i == j:
                            gap = jnp.where(behind, row_m - cum_m, row_f - cum_f)
                            step = jnp.where(behind, step_m, jnp.where(ahead, step_f, step_f + step_m))
                        elif j > i:
                            gap, step = row_f - cum_f, step_f
                        else:
                            gap, step = row_m - cum_m, step_m
                        d = jnp.exp2(gap) * step
                        w = d * gm[at, t]
                        p = pt[h, at, t]
                        dg[j] = dg[j] + d * p
                        e = w * p
                        hi, lo = split2(w)
                        whi[h, at, t] = hi
                        wlo[h, at, t] = lo
                        if i == j:
                            parts = [jnp.where(ahead, e, 0.0), jnp.where(behind, e, 0.0)]
                        else:
                            parts = [e, None] if j > i else [None, e]
                        for strand in range(2):
                            piece = parts[strand]
                            if piece is None:
                                continue
                            slot = (h * 2 + j) * 2 + strand
                            add = piece[0:8]
                            for u in range(1, STRIP // 8):
                                add = add + piece[u * 8 : (u + 1) * 8]
                            sums[slot] = sums[slot] + add
                            old = lane_sums[strand]
                            lane_sums[strand] = piece if old is None else old + piece
                    for strand in range(2):
                        total = jnp.sum(lane_sums[strand], axis=1, keepdims=True)
                        collected = jnp.where(lane128 == strand * 4 + h, total, collected)
                csum[at, :] = collected
                rows_at = segment_at(starts_ref, first + start + iota((STRIP, 1), 0))
                for j in range(2):
                    t = slice(j * 128, (j + 1) * 128)
                    cols_at = segment_at(starts_ref, first + j * 128 + iota((1, 128), 1))
                    hi, lo = split2(jnp.where(rows_at == cols_at, dg[j], 0.0))
                    dghi[at, t] = hi
                    dglo[at, t] = lo
                return tuple(sums)

            row_sums.append(lax.fori_loop(0, 128 // STRIP, strip, (zero_row,) * 16))
        rows_in = []
        for strand in range(2):
            for h in range(4):
                lanes = []
                for j in range(2):
                    slot = (h * 2 + j) * 2 + strand
                    lanes.append(jnp.sum(row_sums[0][slot] + row_sums[1][slot], axis=0, keepdims=True))
                rows_in.append(jnp.concatenate(lanes, axis=1))
        row_keep[c] = jnp.concatenate(rows_in, axis=0)
        col_keep[c] = csum[...].T[0:8]
        for k in range(2):
            total = None
            for h in (2 * k, 2 * k + 1):
                masked = gs[k] * half_mask[h % 2]
                term = dot(whi[h], masked) + dot(wlo[h], masked)
                total = term if total is None else total + term
            dx_ref[span, k * 128 : (k + 1) * 128] = total
        put_part(c, slice(0, 128), dot(dghi[...], cc) + dot(dglo[...], cc))
        dgt_hi, dgt_lo = dghi[...].T, dglo[...].T
        put_part(c, slice(128, 256), dot(dgt_hi, bc) + dot(dgt_lo, bc))


    other = 1 - core
    trade = remote(pair_out.at[other], pair_in, pair_sems.at[0], pair_sems.at[1], "seq", core_peer)
    trade.start()
    inside(0)
    trade.wait()

    def gain_of(ref, a, k):
        return ref[512 + (a * 2 + k) * 8 : 512 + (a * 2 + k + 1) * 8][0:1]

    mine = pair_out.at[core]
    slice_rows = 256 // zs
    for a in range(2):
        for k in range(2):
            rows = slice(a * 256 + k * 128, a * 256 + (k + 1) * 128)
            chip = gain_of(pair_in, a, k) * mine[rows] + pair_in[rows]
            slices = slice(k * (zs // 2), (k + 1) * (zs // 2))
            slice_out[slices, a * slice_rows : (a + 1) * slice_rows] = chip.reshape(zs // 2, slice_rows, 128)
    for k in range(2):
        gains = [gain_of(pair_in, a, k) * gain_of(mine, a, k) for a in range(2)]
        both = jnp.where(iota((8, 128), 0) < 4, gains[0], gains[1])
        slices = slice(k * (zs // 2), (k + 1) * (zs // 2))
        slice_out[slices, 2 * slice_rows : 2 * slice_rows + 8] = jnp.broadcast_to(both[None], (zs // 2, 8, 128))
    slice_in[z_me] = slice_out[z_me]
    sliced = z_copies(lambda z: slice_out.at[z], slice_in.at[z_me], z_sems.at[0], z_sems.at[1])
    inside(1)
    sliced()

    def order(i):
        return i + core * (zs - 1 - 2 * i)

    runs = [jnp.zeros((slice_rows, 128), F32) for _ in range(2)]
    for i in range(zs):
        z = order(i)
        for a in range(2):
            rows = slice(a * slice_rows, (a + 1) * slice_rows)
            scan_out[z, rows] = runs[a]
            gain = slice_in[z, 2 * slice_rows + a * 4 : 2 * slice_rows + a * 4 + 1]
            runs[a] = gain * runs[a] + slice_in[z, rows]
    for a in range(2):
        total_out[a * slice_rows : (a + 1) * slice_rows] = runs[a]
    swap = remote(total_out, total_in, pair_sems.at[2], pair_sems.at[3], "seq", x_peer)
    swap.start()
    inside(2)
    swap.wait()
    second = jnp.where(x_me == 1 - core, 1.0, 0.0)
    runs = [total_in[a * slice_rows : (a + 1) * slice_rows] * second for a in range(2)]
    for i in range(zs):
        z = order(i)
        for a in range(2):
            rows = slice(a * slice_rows, (a + 1) * slice_rows)
            scan_out[z, rows] = scan_out[z, rows] + runs[a]
            gain = slice_in[z, 2 * slice_rows + a * 4 : 2 * slice_rows + a * 4 + 1]
            runs[a] = gain * runs[a]
    back_in[z_me] = scan_out[z_me]
    returned = z_copies(lambda z: scan_out.at[z], back_in.at[z_me], z_sems.at[2], z_sems.at[3])
    inside(3)
    returned()
    for a in range(2):
        for k in range(2):
            rows = slice(a * 256 + k * 128, a * 256 + (k + 1) * 128)
            slices = slice(k * (zs // 2), (k + 1) * (zs // 2))
            enter = back_in[slices, a * slice_rows : (a + 1) * slice_rows].reshape(128, 128)
            entering[core, rows] = enter
            next_out[rows] = gain_of(mine, a, k) * enter + mine[rows]
    passed = remote(next_out, entering.at[core], pair_sems.at[4], pair_sems.at[5], "seq", core_peer)
    passed.start()

    pick = jnp.where(iota((8, 512), 0) == iota((8, 512), 1) // 64, 1.0, 0.0)
    pick_bf = pick.astype(BF16)
    pick2_bf = jnp.where(iota((8, 256), 0) % 4 == iota((8, 256), 1) // 64, 1.0, 0.0).astype(BF16)
    ones_bf = jnp.ones((8, 128), BF16)

    def same_place(c, carry):
        span = pl.ds(pl.multiple_of(c * Q, Q), Q)
        bc_prod = split2(b_ref[span, :].astype(F32) * c_ref[span, :].astype(F32))
        score8 = dot_nt(ones_bf, bc_prod[0]) + dot_nt(ones_bf, bc_prod[1])
        xg = split2(x_ref[span, :].astype(F32) * g_ref[span, :].astype(F32))
        pair8 = dot_nt(pick2_bf, xg[0]) + dot_nt(pick2_bf, xg[1])
        other_ref[:, span] = score8 * pair8
        return carry

    lax.fori_loop(0, chunks, same_place, 0)
    passed.wait()


    def incoming(q):
        at = (q % 2) * 256
        return jnp.concatenate([entering[q // 2, at + k * 128 : at + (k + 1) * 128] for k in range(2)], axis=1)

    for q, (terms, lanes, way) in enumerate(quantities):
        target = states if terms is ends_ref else adjoints
        run = incoming(q)
        for c in way:
            target[c, :, lanes] = run
            run = run * gain_ref[c, 0:1, lanes] + terms[c, :, lanes]
        if target is states:
            target[chunks, :, lanes] = run

    sent = []
    for c in range(chunks):
        span = slice(c * Q, (c + 1) * Q)
        state_hi, state_lo = split2(states[c])
        adj_hi, adj_lo = split2(adjoints[c])
        xhi, xlo, ghi, glo = xhi_ref[span, :], xlo_ref[span, :], ghi_ref[span, :], glo_ref[span, :]
        db = dot_nt(xhi, adj_hi) + dot_nt(xlo, adj_hi) + dot_nt(xhi, adj_lo)
        dc = dot_nt(ghi, state_hi) + dot_nt(glo, state_hi) + dot_nt(ghi, state_lo)
        part[c, :, :, 0:128] = part[c, :, :, 0:128] + db.reshape(nh, part_rows, 128)
        part[c, :, :, 128:256] = part[c, :, :, 128:256] + dc.reshape(nh, part_rows, 128)
        sent.append(
            head_copies(
                lambda peer, c=c: part.at[c, peer], got.at[c, head_me], head_sems.at[0, c], head_sems.at[1, c]
            )
        )

    def across(c, carry):
        span = pl.ds(pl.multiple_of(c * Q, Q), Q)
        state_hi, state_lo = split2(states[c])
        adj_hi, adj_lo = split2(adjoints[c])
        bc, cc = b_ref[span, :], c_ref[span, :]
        v = dot(bc, adj_hi) + dot(bc, adj_lo)
        y = dot(cc, state_hi) + dot(cc, state_lo)
        scaled = el_ref[span, :] * v
        dx_ref[span, :] = dx_ref[span, :] + scaled[:, FRONT] + scaled[:, MIRROR]
        x_prod = split2((xhi_ref[span, :].astype(F32) + xlo_ref[span, :].astype(F32)) * v)
        g_prod = split2((ghi_ref[span, :].astype(F32) + glo_ref[span, :].astype(F32)) * y)
        col8 = col_keep[c] + dot_nt(pick_bf, x_prod[0]) + dot_nt(pick_bf, x_prod[1])
        row8 = row_keep[c] + dot_nt(pick_bf, g_prod[0]) + dot_nt(pick_bf, g_prod[1])
        s8 = jnp.concatenate([rows_ref[c, 0, 12:16, :], rows_ref[c, 1, 12:16, :]], axis=0)
        step8 = col8 / s8 + other_ref[:, span]
        flow_f = jnp.sum(states[c + 1, :, FRONT] * adjoints[c, :, FRONT], axis=0, keepdims=True)
        under = lax.rem(c + chunks, chunks + 1)
        flow_m = jnp.sum(states[under, :, MIRROR] * adjoints[c, :, MIRROR], axis=0, keepdims=True)
        flow8 = jnp.sum(pick * jnp.concatenate([flow_f, flow_m], axis=1), axis=1, keepdims=True)
        diff = split3(row8 - col8)
        front8 = iota((8, Q), 0) < 4
        decay8 = jnp.where(front8, dot_sum(diff, low_one), dot_sum(diff, up_one)) + flow8
        own_ref[0:4, span] = step8[0:4]
        own_ref[4:8, span] = decay8[0:4]
        other_ref[0:4, span] = step8[4:8]
        other_ref[4:8, span] = decay8[4:8]
        return carry

    def add_up(c):
        sent[c]()
        total = part[c, head_me]
        for k in range(1, nh):
            total = total + got[c, lax.rem(head_me + k, nh)]
        sums_ref[c, head_me] = total
        return head_copies(
            lambda peer: sums_ref.at[c, head_me], sums_ref.at[c, head_me], head_sems.at[2, c], head_sems.at[3, c]
        )

    lax.fori_loop(0, chunks, across, 0)
    others[head_me] = other_ref[...]
    shared = head_copies(lambda peer: other_ref, others.at[head_me], other_sems.at[0], other_sems.at[1])
    ended = [add_up(c) for c in range(chunks)]
    shared()
    for h in range(4):
        place = 0 * head_me
        for k in range(nh * 4):
            place = jnp.where(heads_ref[k] == head_me * 4 + h, k, place)
        dstep_ref[h : h + 1, :] = own_ref[h : h + 1, :] + others[place // 4, pl.ds(place % 4, 1), :]
        ddecay_ref[h : h + 1, :] = own_ref[4 + h : 5 + h, :] + others[place // 4, pl.ds(place % 4 + 4, 1), :]
    for wait in ended:
        wait()


def hand_on(dx_ref, sums_ref, step_ref, decay_ref, dx_out, db_out, dc_out, step_out, decay_out, sems):
    copies = [
        (dx_ref, dx_out),
        (sums_ref.at[:, 0:128], db_out),
        (sums_ref.at[:, 128:256], dc_out),
        (step_ref, step_out),
        (decay_ref, decay_out),
    ]
    started = [pltpu.make_async_copy(a, b, sems.at[i]) for i, (a, b) in enumerate(copies)]
    for copy in started:
        copy.start()
    for copy in started:
        copy.wait()


def on_device(signal, write_keys, read_queries, step_sizes, log_decay, mirror_heads, contig_starts, out_grad):
    nh, ns = lax.axis_size("head"), lax.axis_size("seq")
    length = signal.shape[0]
    chunks = length // Q
    zs = ns // 4
    slice_rows = 256 // zs
    part_rows = Q // nh
    vmem = pl.BlockSpec(memory_space=pltpu.VMEM)
    smem = pl.BlockSpec(memory_space=pltpu.SMEM)
    hbm = pl.BlockSpec(memory_space=pl.ANY)

    def shape(*dims, dtype=F32):
        return jax.ShapeDtypeStruct(dims, dtype)

    def room(*dims, dtype=F32):
        return pltpu.VMEM(dims, dtype)

    dx, sums, dstep, ddecay = pl.pallas_call(
        functools.partial(kernel, nh, ns),
        out_shape=[shape(length, 256), shape(chunks, nh, part_rows, 256), shape(4, length), shape(4, length)],
        in_specs=[smem] * 2 + [vmem] * 6,
        out_specs=[vmem] * 4,
        scratch_shapes=[
            room(nh, 8, length),
            room(chunks, 2, 16, Q),
            room(2, length, 16),
            room(length, 512, dtype=BF16),
            room(length, 512, dtype=BF16),
            room(length, 512, dtype=BF16),
            room(length, 512, dtype=BF16),
            room(length, 512),
            room(chunks, 128, 512),
            room(chunks, 128, 512),
            room(chunks, 8, 512),
            room(2, 544, 128),
            room(544, 128),
            room(zs, 2 * slice_rows + 8, 128),
            room(zs, 2 * slice_rows + 8, 128),
            room(zs, 2 * slice_rows, 128),
            room(2 * slice_rows, 128),
            room(2 * slice_rows, 128),
            room(zs, 2 * slice_rows, 128),
            room(512, 128),
            room(2, 512, 128),
            room(chunks + 1, 128, 512),
            room(chunks, 128, 512),
            room(Q, Q),
            room(4, Q, Q),
            room(4, Q, Q, dtype=BF16),
            room(4, Q, Q, dtype=BF16),
            room(Q, Q, dtype=BF16),
            room(Q, Q, dtype=BF16),
            room(Q, 128),
            room(chunks, 8, Q),
            room(chunks, 8, Q),
            room(chunks, nh, part_rows, 256),
            room(chunks, nh, part_rows, 256),
            room(8, length),
            room(8, length),
            room(nh, 8, length),
            pltpu.SemaphoreType.DMA((2, nh)),
            pltpu.SemaphoreType.DMA((6,)),
            pltpu.SemaphoreType.DMA((4, zs)),
            pltpu.SemaphoreType.DMA((4, chunks, nh)),
            pltpu.SemaphoreType.DMA((2, nh)),
        ],
        compiler_params=pltpu.CompilerParams(
            vmem_limit_bytes=VMEM_LIMIT, collective_id=0, has_side_effects=True
        ),
        name="mixer_backward",
    )(mirror_heads, contig_starts, signal, out_grad, write_keys, read_queries, step_sizes, log_decay)

    return pl.pallas_call(
        hand_on,
        out_shape=[shape(length, 256), shape(length, 128), shape(length, 128), shape(4, length), shape(4, length)],
        in_specs=[hbm] * 4,
        out_specs=[hbm] * 5,
        scratch_shapes=[pltpu.SemaphoreType.DMA((5,))],
        name="hand_on",
    )(dx, sums.reshape(length, 256), dstep, ddecay)


def solution(mesh):
    return jax.shard_map(
        on_device,
        mesh=mesh,
        in_specs=(
            P("seq", "head"),
            P("seq", None),
            P("seq", None),
            P("head", "seq"),
            P("head", "seq"),
            P(),
            P(),
            P("seq", "head"),
        ),
        out_specs=(
            P("seq", "head"),
            P("seq", None),
            P("seq", None),
            P("head", "seq"),
            P("head", "seq"),
        ),
        check_vma=False,
    )
```

```python
import functools

import jax
import jax.numpy as jnp
from jax import lax
from jax.experimental import pallas as pl
from jax.experimental.pallas import tpu as pltpu
from jax.sharding import PartitionSpec as P

Q = 256
STRIP = 32
LOG2E = 1.4426950408889634
F32, BF16 = jnp.float32, jnp.bfloat16
MESH = pl.DeviceIdType.MESH
VMEM_LIMIT = 56 * 1024 * 1024


def iota(shape, dim):
    return lax.broadcasted_iota(jnp.int32, shape, dim)


def split2(v):
    hi = v.astype(BF16)
    return hi, (v - hi.astype(F32)).astype(BF16)


def split3(v):
    hi = v.astype(BF16)
    rest = v - hi.astype(F32)
    mid = rest.astype(BF16)
    return hi, mid, (rest - mid.astype(F32)).astype(BF16)


def dot(a, b):
    return lax.dot_general(a, b, (((1,), (0,)), ((), ())), preferred_element_type=F32)


def dot_nt(a, b):
    return lax.dot_general(a, b, (((1,), (1,)), ((), ())), preferred_element_type=F32)


def dot_sum(parts, b, how=dot):
    total = how(parts[0], b)
    for part in parts[1:]:
        total = total + how(part, b)
    return total


def segment_at(starts_ref, t):
    total = (starts_ref[0] <= t).astype(jnp.int32)
    for k in range(1, 4):
        total = total + (starts_ref[k] <= t).astype(jnp.int32)
    return total


FRONT, MIRROR = slice(0, 256), slice(256, 512)
STRANDS = (FRONT, MIRROR)


def kernel(
    nh,
    ns,
    heads_ref,
    starts_ref,
    x_ref,
    g_ref,
    b_ref,
    c_ref,
    step_ref,
    decay_ref,
    dx_ref,
    sums_ref,
    dstep_ref,
    ddecay_ref,
    all_ref,
    rows_ref,
    cols_ref,
    xhi_ref,
    xlo_ref,
    ghi_ref,
    glo_ref,
    el_ref,
    ends_ref,
    seeds_ref,
    gain_ref,
    pair_out,
    pair_in,
    slice_out,
    slice_in,
    scan_out,
    total_out,
    total_in,
    back_in,
    next_out,
    entering,
    states,
    adjoints,
    gm,
    pt,
    whi,
    wlo,
    dghi,
    dglo,
    csum,
    row_keep,
    col_keep,
    part,
    got,
    own_ref,
    other_ref,
    others,
    gather_sems,
    pair_sems,
    z_sems,
    head_sems,
    other_sems,
):
    length = x_ref.shape[0]
    chunks = length // Q
    head_me = lax.axis_index("head")
    seq_me = lax.axis_index("seq")
    offset = seq_me * length
    core = lax.rem(seq_me, 2)
    zs = ns // 4
    z_me = lax.rem(seq_me // 2, zs)
    x_me = seq_me // (2 * zs)
    core_peer = seq_me + 1 - 2 * core
    x_peer = lax.rem(seq_me + ns // 2, ns)

    def z_peer(k):
        z = lax.rem(z_me + k, zs)
        return z, x_me * 2 * zs + z * 2 + core

    all_ref[head_me, 0:4, :] = step_ref[...]
    all_ref[head_me, 4:8, :] = decay_ref[...]
    barrier = pltpu.get_barrier_semaphore()

    def greet_head(k, carry):
        peer = lax.rem(head_me + k, nh)
        pl.semaphore_signal(barrier, inc=1, device_id={"head": peer}, device_id_type=MESH)
        return carry

    def greet_z(k, carry):
        pl.semaphore_signal(barrier, inc=1, device_id={"seq": z_peer(k)[1]}, device_id_type=MESH)
        return carry

    lax.fori_loop(1, nh, greet_head, 0)
    lax.fori_loop(1, zs, greet_z, 0)
    pl.semaphore_signal(barrier, inc=1, device_id={"seq": core_peer}, device_id_type=MESH)
    pl.semaphore_signal(barrier, inc=1, device_id={"seq": x_peer}, device_id_type=MESH)
    pl.semaphore_wait(barrier, nh + zs)

    def remote(source, target, send, recv, axis, peer):
        return pltpu.make_async_remote_copy(
            src_ref=source,
            dst_ref=target,
            send_sem=send,
            recv_sem=recv,
            device_id={axis: peer},
            device_id_type=MESH,
        )

    def every(count, copy):
        def begin(k, carry):
            copy(k).start()
            return carry

        def end(k, carry):
            copy(k).wait()
            return carry

        lax.fori_loop(1, count, begin, 0)
        return lambda: lax.fori_loop(1, count, end, 0)

    def head_copies(source, target, send, recv):
        def copy(k):
            peer = lax.rem(head_me + k, nh)
            return remote(source(peer), target, send.at[k], recv.at[k], "head", peer)

        return every(nh, copy)

    def z_copies(source, target, send, recv):
        def copy(k):
            z, peer = z_peer(k)
            return remote(source(z), target, send.at[k], recv.at[k], "seq", peer)

        return every(zs, copy)

    gathered = head_copies(
        lambda peer: all_ref.at[head_me], all_ref.at[head_me], gather_sems.at[0], gather_sems.at[1]
    )

    lower = iota((Q, Q), 0) >= iota((Q, Q), 1)
    upper = iota((Q, Q), 0) <= iota((Q, Q), 1)
    low_one = jnp.where(lower, 1.0, 0.0).astype(BF16)
    up_one = jnp.where(upper, 1.0, 0.0).astype(BF16)
    lane = iota((16, 512), 1)
    source = jnp.where(lane < 256, 8, 4) + (lane % 256) // 64
    spread = jnp.where(iota((16, 512), 0) == source, 1.0, 0.0).astype(BF16)
    pick8 = jnp.where(iota((8, 256), 0) == iota((8, 256), 1) // 64, 1.0, 0.0)


    def prepare(strand):
        def chunk(c, carry):
            base = pl.multiple_of(c * Q, Q)
            span = pl.ds(base, Q)
            if strand == 0:
                s4 = all_ref[head_me, 0:4, span]
                d4 = all_ref[head_me, 4:8, span]
            else:
                heads = [heads_ref[head_me * 4 + h] for h in range(4)]
                s4 = jnp.concatenate([all_ref[i // 4, pl.ds(i % 4, 1), span] for i in heads], axis=0)
                d4 = jnp.concatenate([all_ref[i // 4, pl.ds(i % 4 + 4, 1), span] for i in heads], axis=0)
            s8 = jnp.concatenate([s4, s4], axis=0)
            d8 = jnp.concatenate([d4, d4], axis=0)
            cum8 = dot_sum(split3(d8), low_one if strand else up_one) * LOG2E
            total8 = cum8[:, 0:1] if strand else cum8[:, Q - 1 : Q]
            first = offset + base
            seg = segment_at(starts_ref, first + iota((8, Q), 1))
            seg_first, seg_last = segment_at(starts_ref, first), segment_at(starts_ref, first + Q - 1)
            if strand:
                seg_in, seg_far = segment_at(starts_ref, first + Q), seg_first
            else:
                seg_in = jnp.where(first == 0, -1, segment_at(starts_ref, first - 1))
                seg_far = seg_last
            e8 = jnp.where(seg == seg_in, jnp.exp2(cum8), 0.0)
            l8 = jnp.where(seg == seg_far, jnp.exp2(total8 - cum8) * s8, 0.0)
            gain8 = jnp.exp2(total8) * (seg_in == seg_far).astype(F32)
            gain = jnp.sum(pick8 * gain8, axis=0, keepdims=True)
            gain_ref[c, :, STRANDS[strand]] = jnp.broadcast_to(gain, (8, 256))
            rows = jnp.concatenate([cum8[0:4], e8[0:4], l8[0:4], s8[0:4]], axis=0)
            rows_ref[c, strand] = rows
            cols = rows.T
            cols_ref[strand, span, :] = cols
            wide = dot_sum(split3(cols), spread)
            lanes = STRANDS[strand]
            el_ref[span, lanes] = wide[:, 0:256]
            xhi, xlo = split2(x_ref[span, :].astype(F32) * wide[:, 0:256])
            ghi, glo = split2(g_ref[span, :].astype(F32) * wide[:, 256:512])
            xhi_ref[span, lanes] = xhi
            xlo_ref[span, lanes] = xlo
            ghi_ref[span, lanes] = ghi
            glo_ref[span, lanes] = glo
            bt, ct = b_ref[span, :].T, c_ref[span, :].T
            ends_ref[c, :, lanes] = dot(bt, xhi) + dot(bt, xlo)
            seeds_ref[c, :, lanes] = dot(ct, ghi) + dot(ct, glo)
            return carry

        lax.fori_loop(0, chunks, chunk, 0)

    prepare(0)
    gathered()
    prepare(1)

    whole = gain_ref[0]
    for c in range(1, chunks):
        whole = whole * gain_ref[c]
    ascending, descending = range(chunks), range(chunks - 1, -1, -1)
    quantities = (
        (ends_ref, FRONT, ascending),
        (seeds_ref, MIRROR, ascending),
        (ends_ref, MIRROR, descending),
        (seeds_ref, FRONT, descending),
    )
    for q, (terms, lanes, order) in enumerate(quantities):
        run = None
        for c in order:
            run = terms[c, :, lanes] if run is None else run * gain_ref[c, 0:1, lanes] + terms[c, :, lanes]
        for k in range(2):
            pair_out[q // 2, (q % 2) * 256 + k * 128 : (q % 2) * 256 + (k + 1) * 128] = run[:, k * 128 : (k + 1) * 128]
    for p in range(2):
        for a in range(2):
            lanes = STRANDS[(p + a) % 2]
            gains = whole[:, lanes]
            for k in range(2):
                pair_out[p, 512 + (a * 2 + k) * 8 : 512 + (a * 2 + k + 1) * 8] = gains[:, k * 128 : (k + 1) * 128]


    half_mask = [jnp.where(iota((1, 128), 1) // 64 == k, 1.0, 0.0).astype(BF16) for k in range(2)]
    zero_row = jnp.zeros((8, 128), F32)
    part_rows = Q // nh

    def put_part(c, lanes, value):
        part[c, :, :, lanes] = value.reshape(nh, part_rows, 128)

    def inside(c):
        base = c * Q
        span = slice(base, base + Q)
        first = offset + base
        bc, cc = b_ref[span, :], c_ref[span, :]
        xs = [x_ref[span, k * 128 : (k + 1) * 128] for k in range(2)]
        gs = [g_ref[span, k * 128 : (k + 1) * 128] for k in range(2)]
        seg_s = segment_at(starts_ref, first + iota((Q, 1), 0))
        seg_t = segment_at(starts_ref, first + iota((1, Q), 1))
        gm[...] = jnp.where(seg_s == seg_t, dot_nt(bc, cc), 0.0)
        for h in range(4):
            pt[h] = dot_nt(xs[h // 2] * half_mask[h % 2], gs[h // 2])
        row_sums = []
        for i in range(2):

            def strip(r, sums, i=i):
                start = pl.multiple_of(i * 128 + r * STRIP, STRIP)
                at = pl.ds(start, STRIP)
                at_cols = pl.ds(pl.multiple_of(base + start, STRIP), STRIP)
                col_f, col_m = cols_ref[0, at_cols, :], cols_ref[1, at_cols, :]
                lane128 = iota((STRIP, 128), 1)
                s_index = r * STRIP + iota((STRIP, 128), 0)
                ahead = lane128 > s_index
                behind = lane128 < s_index
                sums = list(sums)
                collected = jnp.zeros((STRIP, 128), F32)
                dg = [jnp.zeros((STRIP, 128), F32) for _ in range(2)]
                for h in range(4):
                    cum_f, cum_m = col_f[:, h : h + 1], col_m[:, h : h + 1]
                    step_f, step_m = col_f[:, 12 + h : 13 + h], col_m[:, 12 + h : 13 + h]
                    lane_sums = [None, None]
                    for j in range(2):
                        t = slice(j * 128, (j + 1) * 128)
                        row_f = rows_ref[c, 0, h : h + 1, t]
                        row_m = rows_ref[c, 1, h : h + 1, t]
                        if i == j:
                            gap = jnp.where(behind, row_m - cum_m, row_f - cum_f)
                            step = jnp.where(behind, step_m, jnp.where(ahead, step_f, step_f + step_m))
                        elif j > i:
                            gap, step = row_f - cum_f, step_f
                        else:
                            gap, step = row_m - cum_m, step_m
                        d = jnp.exp2(gap) * step
                        w = d * gm[at, t]
                        p = pt[h, at, t]
                        dg[j] = dg[j] + d * p
                        e = w * p
                        hi, lo = split2(w)
                        whi[h, at, t] = hi
                        wlo[h, at, t] = lo
                        if i == j:
                            parts = [jnp.where(ahead, e, 0.0), jnp.where(behind, e, 0.0)]
                        else:
                            parts = [e, None] if j > i else [None, e]
                        for strand in range(2):
                            piece = parts[strand]
                            if piece is None:
                                continue
                            slot = (h * 2 + j) * 2 + strand
                            add = piece[0:8]
                            for u in range(1, STRIP // 8):
                                add = add + piece[u * 8 : (u + 1) * 8]
                            sums[slot] = sums[slot] + add
                            old = lane_sums[strand]
                            lane_sums[strand] = piece if old is None else old + piece
                    for strand in range(2):
                        total = jnp.sum(lane_sums[strand], axis=1, keepdims=True)
                        collected = jnp.where(lane128 == strand * 4 + h, total, collected)
                csum[at, :] = collected
                rows_at = segment_at(starts_ref, first + start + iota((STRIP, 1), 0))
                for j in range(2):
                    t = slice(j * 128, (j + 1) * 128)
                    cols_at = segment_at(starts_ref, first + j * 128 + iota((1, 128), 1))
                    hi, lo = split2(jnp.where(rows_at == cols_at, dg[j], 0.0))
                    dghi[at, t] = hi
                    dglo[at, t] = lo
                return tuple(sums)

            row_sums.append(lax.fori_loop(0, 128 // STRIP, strip, (zero_row,) * 16))
        rows_in = []
        for strand in range(2):
            for h in range(4):
                lanes = []
                for j in range(2):
                    slot = (h * 2 + j) * 2 + strand
                    lanes.append(jnp.sum(row_sums[0][slot] + row_sums[1][slot], axis=0, keepdims=True))
                rows_in.append(jnp.concatenate(lanes, axis=1))
        row_keep[c] = jnp.concatenate(rows_in, axis=0)
        col_keep[c] = csum[...].T[0:8]
        for k in range(2):
            total = None
            for h in (2 * k, 2 * k + 1):
                masked = gs[k] * half_mask[h % 2]
                term = dot(whi[h], masked) + dot(wlo[h], masked)
                total = term if total is None else total + term
            dx_ref[span, k * 128 : (k + 1) * 128] = total
        put_part(c, slice(0, 128), dot(dghi[...], cc) + dot(dglo[...], cc))
        dgt_hi, dgt_lo = dghi[...].T, dglo[...].T
        put_part(c, slice(128, 256), dot(dgt_hi, bc) + dot(dgt_lo, bc))


    other = 1 - core
    trade = remote(pair_out.at[other], pair_in, pair_sems.at[0], pair_sems.at[1], "seq", core_peer)
    trade.start()
    inside(0)
    trade.wait()

    def gain_of(ref, a, k):
        return ref[512 + (a * 2 + k) * 8 : 512 + (a * 2 + k + 1) * 8][0:1]

    mine = pair_out.at[core]
    slice_rows = 256 // zs
    for a in range(2):
        for k in range(2):
            rows = slice(a * 256 + k * 128, a * 256 + (k + 1) * 128)
            chip = gain_of(pair_in, a, k) * mine[rows] + pair_in[rows]
            slices = slice(k * (zs // 2), (k + 1) * (zs // 2))
            slice_out[slices, a * slice_rows : (a + 1) * slice_rows] = chip.reshape(zs // 2, slice_rows, 128)
    for k in range(2):
        gains = [gain_of(pair_in, a, k) * gain_of(mine, a, k) for a in range(2)]
        both = jnp.where(iota((8, 128), 0) < 4, gains[0], gains[1])
        slices = slice(k * (zs // 2), (k + 1) * (zs // 2))
        slice_out[slices, 2 * slice_rows : 2 * slice_rows + 8] = jnp.broadcast_to(both[None], (zs // 2, 8, 128))
    slice_in[z_me] = slice_out[z_me]
    sliced = z_copies(lambda z: slice_out.at[z], slice_in.at[z_me], z_sems.at[0], z_sems.at[1])
    inside(1)
    sliced()

    def order(i):
        return i + core * (zs - 1 - 2 * i)

    runs = [jnp.zeros((slice_rows, 128), F32) for _ in range(2)]
    for i in range(zs):
        z = order(i)
        for a in range(2):
            rows = slice(a * slice_rows, (a + 1) * slice_rows)
            scan_out[z, rows] = runs[a]
            gain = slice_in[z, 2 * slice_rows + a * 4 : 2 * slice_rows + a * 4 + 1]
            runs[a] = gain * runs[a] + slice_in[z, rows]
    for a in range(2):
        total_out[a * slice_rows : (a + 1) * slice_rows] = runs[a]
    swap = remote(total_out, total_in, pair_sems.at[2], pair_sems.at[3], "seq", x_peer)
    swap.start()
    inside(2)
    swap.wait()
    second = jnp.where(x_me == 1 - core, 1.0, 0.0)
    runs = [total_in[a * slice_rows : (a + 1) * slice_rows] * second for a in range(2)]
    for i in range(zs):
        z = order(i)
        for a in range(2):
            rows = slice(a * slice_rows, (a + 1) * slice_rows)
            scan_out[z, rows] = scan_out[z, rows] + runs[a]
            gain = slice_in[z, 2 * slice_rows + a * 4 : 2 * slice_rows + a * 4 + 1]
            runs[a] = gain * runs[a]
    back_in[z_me] = scan_out[z_me]
    returned = z_copies(lambda z: scan_out.at[z], back_in.at[z_me], z_sems.at[2], z_sems.at[3])
    inside(3)
    returned()
    for a in range(2):
        for k in range(2):
            rows = slice(a * 256 + k * 128, a * 256 + (k + 1) * 128)
            slices = slice(k * (zs // 2), (k + 1) * (zs // 2))
            enter = back_in[slices, a * slice_rows : (a + 1) * slice_rows].reshape(128, 128)
            entering[core, rows] = enter
            next_out[rows] = gain_of(mine, a, k) * enter + mine[rows]
    passed = remote(next_out, entering.at[core], pair_sems.at[4], pair_sems.at[5], "seq", core_peer)
    passed.start()

    pick = jnp.where(iota((8, 512), 0) == iota((8, 512), 1) // 64, 1.0, 0.0)
    pick_bf = pick.astype(BF16)
    pick2_bf = jnp.where(iota((8, 256), 0) % 4 == iota((8, 256), 1) // 64, 1.0, 0.0).astype(BF16)
    ones_bf = jnp.ones((8, 128), BF16)

    def same_place(c, carry):
        span = pl.ds(pl.multiple_of(c * Q, Q), Q)
        bc_prod = split2(b_ref[span, :].astype(F32) * c_ref[span, :].astype(F32))
        score8 = dot_nt(ones_bf, bc_prod[0]) + dot_nt(ones_bf, bc_prod[1])
        xg = split2(x_ref[span, :].astype(F32) * g_ref[span, :].astype(F32))
        pair8 = dot_nt(pick2_bf, xg[0]) + dot_nt(pick2_bf, xg[1])
        other_ref[:, span] = score8 * pair8
        return carry

    lax.fori_loop(0, chunks, same_place, 0)
    passed.wait()


    def incoming(q):
        at = (q % 2) * 256
        return jnp.concatenate([entering[q // 2, at + k * 128 : at + (k + 1) * 128] for k in range(2)], axis=1)

    for q, (terms, lanes, way) in enumerate(quantities):
        target = states if terms is ends_ref else adjoints
        run = incoming(q)
        for c in way:
            target[c, :, lanes] = run
            run = run * gain_ref[c, 0:1, lanes] + terms[c, :, lanes]
        if target is states:
            target[chunks, :, lanes] = run

    sent = []
    for c in range(chunks):
        span = slice(c * Q, (c + 1) * Q)
        state_hi, state_lo = split2(states[c])
        adj_hi, adj_lo = split2(adjoints[c])
        xhi, xlo, ghi, glo = xhi_ref[span, :], xlo_ref[span, :], ghi_ref[span, :], glo_ref[span, :]
        db = dot_nt(xhi, adj_hi) + dot_nt(xlo, adj_hi) + dot_nt(xhi, adj_lo)
        dc = dot_nt(ghi, state_hi) + dot_nt(glo, state_hi) + dot_nt(ghi, state_lo)
        part[c, :, :, 0:128] = part[c, :, :, 0:128] + db.reshape(nh, part_rows, 128)
        part[c, :, :, 128:256] = part[c, :, :, 128:256] + dc.reshape(nh, part_rows, 128)
        sent.append(
            head_copies(
                lambda peer, c=c: part.at[c, peer], got.at[c, head_me], head_sems.at[0, c], head_sems.at[1, c]
            )
        )

    def across(c, carry):
        span = pl.ds(pl.multiple_of(c * Q, Q), Q)
        state_hi, state_lo = split2(states[c])
        adj_hi, adj_lo = split2(adjoints[c])
        bc, cc = b_ref[span, :], c_ref[span, :]
        v = dot(bc, adj_hi) + dot(bc, adj_lo)
        y = dot(cc, state_hi) + dot(cc, state_lo)
        scaled = el_ref[span, :] * v
        dx_ref[span, :] = dx_ref[span, :] + scaled[:, FRONT] + scaled[:, MIRROR]
        x_prod = split2((xhi_ref[span, :].astype(F32) + xlo_ref[span, :].astype(F32)) * v)
        g_prod = split2((ghi_ref[span, :].astype(F32) + glo_ref[span, :].astype(F32)) * y)
        col8 = col_keep[c] + dot_nt(pick_bf, x_prod[0]) + dot_nt(pick_bf, x_prod[1])
        row8 = row_keep[c] + dot_nt(pick_bf, g_prod[0]) + dot_nt(pick_bf, g_prod[1])
        s8 = jnp.concatenate([rows_ref[c, 0, 12:16, :], rows_ref[c, 1, 12:16, :]], axis=0)
        step8 = col8 / s8 + other_ref[:, span]
        flow_f = jnp.sum(states[c + 1, :, FRONT] * adjoints[c, :, FRONT], axis=0, keepdims=True)
        under = lax.rem(c + chunks, chunks + 1)
        flow_m = jnp.sum(states[under, :, MIRROR] * adjoints[c, :, MIRROR], axis=0, keepdims=True)
        flow8 = jnp.sum(pick * jnp.concatenate([flow_f, flow_m], axis=1), axis=1, keepdims=True)
        diff = split3(row8 - col8)
        front8 = iota((8, Q), 0) < 4
        decay8 = jnp.where(front8, dot_sum(diff, low_one), dot_sum(diff, up_one)) + flow8
        own_ref[0:4, span] = step8[0:4]
        own_ref[4:8, span] = decay8[0:4]
        other_ref[0:4, span] = step8[4:8]
        other_ref[4:8, span] = decay8[4:8]
        return carry

    def add_up(c):
        sent[c]()
        total = part[c, head_me]
        for k in range(1, nh):
            total = total + got[c, lax.rem(head_me + k, nh)]
        sums_ref[c, head_me] = total
        return head_copies(
            lambda peer: sums_ref.at[c, head_me], sums_ref.at[c, head_me], head_sems.at[2, c], head_sems.at[3, c]
        )

    lax.fori_loop(0, chunks, across, 0)
    others[head_me] = other_ref[...]
    shared = head_copies(lambda peer: other_ref, others.at[head_me], other_sems.at[0], other_sems.at[1])
    ended = [add_up(c) for c in range(chunks)]
    shared()
    for h in range(4):
        place = 0 * head_me
        for k in range(nh * 4):
            place = jnp.where(heads_ref[k] == head_me * 4 + h, k, place)
        dstep_ref[h : h + 1, :] = own_ref[h : h + 1, :] + others[place // 4, pl.ds(place % 4, 1), :]
        ddecay_ref[h : h + 1, :] = own_ref[4 + h : 5 + h, :] + others[place // 4, pl.ds(place % 4 + 4, 1), :]
    for wait in ended:
        wait()


def hand_on(dx_ref, sums_ref, step_ref, decay_ref, dx_out, db_out, dc_out, step_out, decay_out):
    dx_out[...] = dx_ref[...]
    db_out[...] = sums_ref[:, 0:128]
    dc_out[...] = sums_ref[:, 128:256]
    step_out[...] = step_ref[...]
    decay_out[...] = decay_ref[...]


def on_device(signal, write_keys, read_queries, step_sizes, log_decay, mirror_heads, contig_starts, out_grad):
    nh, ns = lax.axis_size("head"), lax.axis_size("seq")
    length = signal.shape[0]
    chunks = length // Q
    zs = ns // 4
    slice_rows = 256 // zs
    part_rows = Q // nh
    vmem = pl.BlockSpec(memory_space=pltpu.VMEM)
    smem = pl.BlockSpec(memory_space=pltpu.SMEM)
    across_lanes = pl.BlockSpec((4, Q), lambda i: (0, i))

    def across_rows(width):
        return pl.BlockSpec((Q, width), lambda i: (i, 0))

    def shape(*dims, dtype=F32):
        return jax.ShapeDtypeStruct(dims, dtype)

    def room(*dims, dtype=F32):
        return pltpu.VMEM(dims, dtype)

    dx, sums, dstep, ddecay = pl.pallas_call(
        functools.partial(kernel, nh, ns),
        out_shape=[shape(length, 256), shape(chunks, nh, part_rows, 256), shape(4, length), shape(4, length)],
        in_specs=[smem] * 2 + [vmem] * 6,
        out_specs=[vmem] * 4,
        scratch_shapes=[
            room(nh, 8, length),
            room(chunks, 2, 16, Q),
            room(2, length, 16),
            room(length, 512, dtype=BF16),
            room(length, 512, dtype=BF16),
            room(length, 512, dtype=BF16),
            room(length, 512, dtype=BF16),
            room(length, 512),
            room(chunks, 128, 512),
            room(chunks, 128, 512),
            room(chunks, 8, 512),
            room(2, 544, 128),
            room(544, 128),
            room(zs, 2 * slice_rows + 8, 128),
            room(zs, 2 * slice_rows + 8, 128),
            room(zs, 2 * slice_rows, 128),
            room(2 * slice_rows, 128),
            room(2 * slice_rows, 128),
            room(zs, 2 * slice_rows, 128),
            room(512, 128),
            room(2, 512, 128),
            room(chunks + 1, 128, 512),
            room(chunks, 128, 512),
            room(Q, Q),
            room(4, Q, Q),
            room(4, Q, Q, dtype=BF16),
            room(4, Q, Q, dtype=BF16),
            room(Q, Q, dtype=BF16),
            room(Q, Q, dtype=BF16),
            room(Q, 128),
            room(chunks, 8, Q),
            room(chunks, 8, Q),
            room(chunks, nh, part_rows, 256),
            room(chunks, nh, part_rows, 256),
            room(8, length),
            room(8, length),
            room(nh, 8, length),
            pltpu.SemaphoreType.DMA((2, nh)),
            pltpu.SemaphoreType.DMA((6,)),
            pltpu.SemaphoreType.DMA((4, zs)),
            pltpu.SemaphoreType.DMA((4, chunks, nh)),
            pltpu.SemaphoreType.DMA((2, nh)),
        ],
        compiler_params=pltpu.CompilerParams(
            vmem_limit_bytes=VMEM_LIMIT, collective_id=0, has_side_effects=True
        ),
        name="mixer_backward",
    )(mirror_heads, contig_starts, signal, out_grad, write_keys, read_queries, step_sizes, log_decay)

    return pl.pallas_call(
        hand_on,
        out_shape=[shape(length, 256), shape(length, 128), shape(length, 128), shape(4, length), shape(4, length)],
        grid=(chunks,),
        in_specs=[across_rows(256)] * 2 + [across_lanes] * 2,
        out_specs=[across_rows(256), across_rows(128), across_rows(128)] + [across_lanes] * 2,
        name="hand_on",
    )(dx, sums.reshape(length, 256), dstep, ddecay)


def solution(mesh):
    return jax.shard_map(
        on_device,
        mesh=mesh,
        in_specs=(
            P("seq", "head"),
            P("seq", None),
            P("seq", None),
            P("head", "seq"),
            P("head", "seq"),
            P(),
            P(),
            P("seq", "head"),
        ),
        out_specs=(
            P("seq", "head"),
            P("seq", None),
            P("seq", None),
            P("head", "seq"),
            P("head", "seq"),
        ),
        check_vma=False,
    )
```

```python
import functools

import jax
import jax.numpy as jnp
from jax import lax
from jax.experimental import pallas as pl
from jax.experimental.pallas import tpu as pltpu
from jax.sharding import PartitionSpec as P

Q = 256
STRIP = 32
LOG2E = 1.4426950408889634
F32, BF16 = jnp.float32, jnp.bfloat16
MESH = pl.DeviceIdType.MESH
VMEM_LIMIT = 56 * 1024 * 1024


def iota(shape, dim):
    return lax.broadcasted_iota(jnp.int32, shape, dim)


def split2(v):
    hi = v.astype(BF16)
    return hi, (v - hi.astype(F32)).astype(BF16)


def split3(v):
    hi = v.astype(BF16)
    rest = v - hi.astype(F32)
    mid = rest.astype(BF16)
    return hi, mid, (rest - mid.astype(F32)).astype(BF16)


def dot(a, b):
    return lax.dot_general(a, b, (((1,), (0,)), ((), ())), preferred_element_type=F32)


def dot_nt(a, b):
    return lax.dot_general(a, b, (((1,), (1,)), ((), ())), preferred_element_type=F32)


def dot_sum(parts, b, how=dot):
    total = how(parts[0], b)
    for part in parts[1:]:
        total = total + how(part, b)
    return total


def segment_at(starts_ref, t):
    total = (starts_ref[0] <= t).astype(jnp.int32)
    for k in range(1, 4):
        total = total + (starts_ref[k] <= t).astype(jnp.int32)
    return total


FRONT, MIRROR = slice(0, 256), slice(256, 512)
STRANDS = (FRONT, MIRROR)


def kernel(
    nh,
    ns,
    heads_ref,
    starts_ref,
    x_ref,
    g_ref,
    b_ref,
    c_ref,
    step_ref,
    decay_ref,
    dx_ref,
    sums_ref,
    dstep_ref,
    ddecay_ref,
    all_ref,
    rows_ref,
    cols_ref,
    xhi_ref,
    xlo_ref,
    ghi_ref,
    glo_ref,
    el_ref,
    ends_ref,
    seeds_ref,
    gain_ref,
    pair_out,
    pair_in,
    slice_out,
    slice_in,
    scan_out,
    total_out,
    total_in,
    back_in,
    next_out,
    entering,
    states,
    adjoints,
    gm,
    pt,
    whi,
    wlo,
    dghi,
    dglo,
    csum,
    row_keep,
    col_keep,
    part,
    got,
    own_ref,
    other_ref,
    others,
    far_out,
    far_in,
    gather_sems,
    pair_sems,
    z_sems,
    head_sems,
    other_sems,
):
    length = x_ref.shape[0]
    chunks = length // Q
    head_me = lax.axis_index("head")
    seq_me = lax.axis_index("seq")
    offset = seq_me * length
    core = lax.rem(seq_me, 2)
    zs = ns // 4
    z_me = lax.rem(seq_me // 2, zs)
    x_me = seq_me // (2 * zs)
    core_peer = seq_me + 1 - 2 * core
    x_peer = lax.rem(seq_me + ns // 2, ns)

    def z_peer(k):
        z = lax.rem(z_me + k, zs)
        return z, x_me * 2 * zs + z * 2 + core

    all_ref[head_me, 0:4, :] = step_ref[...]
    all_ref[head_me, 4:8, :] = decay_ref[...]
    barrier = pltpu.get_barrier_semaphore()

    def greet_head(k, carry):
        peer = lax.rem(head_me + k, nh)
        pl.semaphore_signal(barrier, inc=1, device_id={"head": peer}, device_id_type=MESH)
        return carry

    def greet_z(k, carry):
        pl.semaphore_signal(barrier, inc=1, device_id={"seq": z_peer(k)[1]}, device_id_type=MESH)
        return carry

    lax.fori_loop(1, nh, greet_head, 0)
    lax.fori_loop(1, zs, greet_z, 0)
    pl.semaphore_signal(barrier, inc=1, device_id={"seq": core_peer}, device_id_type=MESH)
    pl.semaphore_signal(barrier, inc=1, device_id={"seq": x_peer}, device_id_type=MESH)
    pl.semaphore_wait(barrier, nh + zs)

    def remote(source, target, send, recv, axis, peer):
        return pltpu.make_async_remote_copy(
            src_ref=source,
            dst_ref=target,
            send_sem=send,
            recv_sem=recv,
            device_id={axis: peer},
            device_id_type=MESH,
        )

    def every(count, copy):
        def begin(k, carry):
            copy(k).start()
            return carry

        def end(k, carry):
            copy(k).wait()
            return carry

        lax.fori_loop(1, count, begin, 0)
        return lambda: lax.fori_loop(1, count, end, 0)

    def head_copies(source, target, send, recv):
        def copy(k):
            peer = lax.rem(head_me + k, nh)
            return remote(source(peer), target, send.at[k], recv.at[k], "head", peer)

        return every(nh, copy)

    def z_copies(source, target, send, recv):
        def copy(k):
            z, peer = z_peer(k)
            return remote(source(z), target, send.at[k], recv.at[k], "seq", peer)

        return every(zs, copy)

    gathered = head_copies(
        lambda peer: all_ref.at[head_me], all_ref.at[head_me], gather_sems.at[0], gather_sems.at[1]
    )

    lower = iota((Q, Q), 0) >= iota((Q, Q), 1)
    upper = iota((Q, Q), 0) <= iota((Q, Q), 1)
    low_one = jnp.where(lower, 1.0, 0.0).astype(BF16)
    up_one = jnp.where(upper, 1.0, 0.0).astype(BF16)
    lane = iota((16, 512), 1)
    source = jnp.where(lane < 256, 8, 4) + (lane % 256) // 64
    spread = jnp.where(iota((16, 512), 0) == source, 1.0, 0.0).astype(BF16)
    pick8 = jnp.where(iota((8, 256), 0) == iota((8, 256), 1) // 64, 1.0, 0.0)


    def prepare(strand):
        def chunk(c, carry):
            base = pl.multiple_of(c * Q, Q)
            span = pl.ds(base, Q)
            if strand == 0:
                s4 = all_ref[head_me, 0:4, span]
                d4 = all_ref[head_me, 4:8, span]
            else:
                heads = [heads_ref[head_me * 4 + h] for h in range(4)]
                s4 = jnp.concatenate([all_ref[i // 4, pl.ds(i % 4, 1), span] for i in heads], axis=0)
                d4 = jnp.concatenate([all_ref[i // 4, pl.ds(i % 4 + 4, 1), span] for i in heads], axis=0)
            s8 = jnp.concatenate([s4, s4], axis=0)
            d8 = jnp.concatenate([d4, d4], axis=0)
            cum8 = dot_sum(split3(d8), low_one if strand else up_one) * LOG2E
            total8 = cum8[:, 0:1] if strand else cum8[:, Q - 1 : Q]
            first = offset + base
            seg = segment_at(starts_ref, first + iota((8, Q), 1))
            seg_first, seg_last = segment_at(starts_ref, first), segment_at(starts_ref, first + Q - 1)
            if strand:
                seg_in, seg_far = segment_at(starts_ref, first + Q), seg_first
            else:
                seg_in = jnp.where(first == 0, -1, segment_at(starts_ref, first - 1))
                seg_far = seg_last
            e8 = jnp.where(seg == seg_in, jnp.exp2(cum8), 0.0)
            l8 = jnp.where(seg == seg_far, jnp.exp2(total8 - cum8) * s8, 0.0)
            gain8 = jnp.exp2(total8) * (seg_in == seg_far).astype(F32)
            gain = jnp.sum(pick8 * gain8, axis=0, keepdims=True)
            gain_ref[c, :, STRANDS[strand]] = jnp.broadcast_to(gain, (8, 256))
            rows = jnp.concatenate([cum8[0:4], e8[0:4], l8[0:4], s8[0:4]], axis=0)
            rows_ref[c, strand] = rows
            cols = rows.T
            cols_ref[strand, span, :] = cols
            wide = dot_sum(split3(cols), spread)
            lanes = STRANDS[strand]
            el_ref[span, lanes] = wide[:, 0:256]
            xhi, xlo = split2(x_ref[span, :].astype(F32) * wide[:, 0:256])
            ghi, glo = split2(g_ref[span, :].astype(F32) * wide[:, 256:512])
            xhi_ref[span, lanes] = xhi
            xlo_ref[span, lanes] = xlo
            ghi_ref[span, lanes] = ghi
            glo_ref[span, lanes] = glo
            bt, ct = b_ref[span, :].T, c_ref[span, :].T
            ends_ref[c, :, lanes] = dot(bt, xhi) + dot(bt, xlo)
            seeds_ref[c, :, lanes] = dot(ct, ghi) + dot(ct, glo)
            return carry

        lax.fori_loop(0, chunks, chunk, 0)


    ascending, descending = range(chunks), range(chunks - 1, -1, -1)
    way = (ascending, descending)

    def terms_of(strand, d):
        return (ends_ref, seeds_ref)[(strand + d) % 2]

    def fold(strand):
        lanes = STRANDS[strand]
        for d in range(2):
            run = None
            for c in way[d]:
                term = terms_of(strand, d)[c, :, lanes]
                run = term if run is None else run * gain_ref[c, 0:1, lanes] + term
            for k in range(2):
                pair_out[strand, d, k * 128 : (k + 1) * 128] = run[:, k * 128 : (k + 1) * 128]
        whole = gain_ref[0, :, lanes]
        for c in range(1, chunks):
            whole = whole * gain_ref[c, :, lanes]
        for d in range(2):
            for k in range(2):
                pair_out[strand, d, 256 + k * 8 : 264 + k * 8] = whole[:, k * 128 : (k + 1) * 128]


    half_mask = [jnp.where(iota((1, 128), 1) // 64 == k, 1.0, 0.0).astype(BF16) for k in range(2)]
    zero_row = jnp.zeros((8, 128), F32)
    part_rows = Q // nh

    def put_part(c, lanes, value):
        part[c, :, :, lanes] = value.reshape(nh, part_rows, 128)

    kept_sums = {}

    def inside(c, i):
        base = c * Q
        span = slice(base, base + Q)
        first = offset + base
        bc, cc = b_ref[span, :], c_ref[span, :]
        xs = [x_ref[span, k * 128 : (k + 1) * 128] for k in range(2)]
        gs = [g_ref[span, k * 128 : (k + 1) * 128] for k in range(2)]
        if i == 0:
            seg_s = segment_at(starts_ref, first + iota((Q, 1), 0))
            seg_t = segment_at(starts_ref, first + iota((1, Q), 1))
            gm[...] = jnp.where(seg_s == seg_t, dot_nt(bc, cc), 0.0)
            for h in range(4):
                pt[h] = dot_nt(xs[h // 2] * half_mask[h % 2], gs[h // 2])

        def strip(r, sums):
            start = pl.multiple_of(i * 128 + r * STRIP, STRIP)
            at = pl.ds(start, STRIP)
            at_cols = pl.ds(pl.multiple_of(base + start, STRIP), STRIP)
            col_f, col_m = cols_ref[0, at_cols, :], cols_ref[1, at_cols, :]
            lane128 = iota((STRIP, 128), 1)
            s_index = r * STRIP + iota((STRIP, 128), 0)
            ahead = lane128 > s_index
            behind = lane128 < s_index
            sums = list(sums)
            collected = jnp.zeros((STRIP, 128), F32)
            dg = [jnp.zeros((STRIP, 128), F32) for _ in range(2)]
            for h in range(4):
                cum_f, cum_m = col_f[:, h : h + 1], col_m[:, h : h + 1]
                step_f, step_m = col_f[:, 12 + h : 13 + h], col_m[:, 12 + h : 13 + h]
                lane_sums = [None, None]
                for j in range(2):
                    t = slice(j * 128, (j + 1) * 128)
                    row_f = rows_ref[c, 0, h : h + 1, t]
                    row_m = rows_ref[c, 1, h : h + 1, t]
                    if i == j:
                        gap = jnp.where(behind, row_m - cum_m, row_f - cum_f)
                        step = jnp.where(behind, step_m, jnp.where(ahead, step_f, step_f + step_m))
                    elif j > i:
                        gap, step = row_f - cum_f, step_f
                    else:
                        gap, step = row_m - cum_m, step_m
                    d = jnp.exp2(gap) * step
                    w = d * gm[at, t]
                    p = pt[h, at, t]
                    dg[j] = dg[j] + d * p
                    e = w * p
                    hi, lo = split2(w)
                    whi[h, at, t] = hi
                    wlo[h, at, t] = lo
                    if i == j:
                        parts = [jnp.where(ahead, e, 0.0), jnp.where(behind, e, 0.0)]
                    else:
                        parts = [e, None] if j > i else [None, e]
                    for strand in range(2):
                        piece = parts[strand]
                        if piece is None:
                            continue
                        slot = (h * 2 + j) * 2 + strand
                        add = piece[0:8]
                        for u in range(1, STRIP // 8):
                            add = add + piece[u * 8 : (u + 1) * 8]
                        sums[slot] = sums[slot] + add
                        old = lane_sums[strand]
                        lane_sums[strand] = piece if old is None else old + piece
                for strand in range(2):
                    total = jnp.sum(lane_sums[strand], axis=1, keepdims=True)
                    collected = jnp.where(lane128 == strand * 4 + h, total, collected)
            csum[at, :] = collected
            rows_at = segment_at(starts_ref, first + start + iota((STRIP, 1), 0))
            for j in range(2):
                t = slice(j * 128, (j + 1) * 128)
                cols_at = segment_at(starts_ref, first + j * 128 + iota((1, 128), 1))
                hi, lo = split2(jnp.where(rows_at == cols_at, dg[j], 0.0))
                dghi[at, t] = hi
                dglo[at, t] = lo
            return tuple(sums)

        kept_sums[i] = lax.fori_loop(0, 128 // STRIP, strip, (zero_row,) * 16)
        if i == 0:
            return
        row_sums = [kept_sums[0], kept_sums[1]]
        rows_in = []
        for strand in range(2):
            for h in range(4):
                lanes = []
                for j in range(2):
                    slot = (h * 2 + j) * 2 + strand
                    lanes.append(jnp.sum(row_sums[0][slot] + row_sums[1][slot], axis=0, keepdims=True))
                rows_in.append(jnp.concatenate(lanes, axis=1))
        row_keep[c] = jnp.concatenate(rows_in, axis=0)
        col_keep[c] = csum[...].T[0:8]
        for k in range(2):
            total = None
            for h in (2 * k, 2 * k + 1):
                masked = gs[k] * half_mask[h % 2]
                term = dot(whi[h], masked) + dot(wlo[h], masked)
                total = term if total is None else total + term
            dx_ref[span, k * 128 : (k + 1) * 128] = total
        put_part(c, slice(0, 128), dot(dghi[...], cc) + dot(dglo[...], cc))
        dgt_hi, dgt_lo = dghi[...].T, dglo[...].T
        put_part(c, slice(128, 256), dot(dgt_hi, bc) + dot(dgt_lo, bc))


    other = 1 - core
    slice_rows = 256 // zs
    half_slices = zs // 2
    waits = {}

    def gain_of(ref, k):
        return ref[256 + k * 8 : 257 + k * 8]

    def order(i):
        return i + core * (zs - 1 - 2 * i)

    def trade(strand):
        fold(strand)
        copy = remote(
            pair_out.at[strand, other],
            pair_in.at[strand],
            pair_sems.at[strand, 0],
            pair_sems.at[strand, 1],
            "seq",
            core_peer,
        )
        copy.start()
        waits["trade", strand] = copy.wait

    def spread_chip(strand):
        waits["trade", strand]()
        mine, theirs = pair_out.at[strand, core], pair_in.at[strand]
        for k in range(2):
            rows = slice(k * 128, (k + 1) * 128)
            slices = slice(k * half_slices, (k + 1) * half_slices)
            chip = gain_of(theirs, k) * mine[rows] + theirs[rows]
            slice_out[strand, slices, 0:slice_rows] = chip.reshape(half_slices, slice_rows, 128)
            gain = gain_of(theirs, k) * gain_of(mine, k)
            slice_out[strand, slices, slice_rows : slice_rows + 8] = jnp.broadcast_to(
                gain[None], (half_slices, 8, 128)
            )
        slice_in[strand, z_me] = slice_out[strand, z_me]
        waits["spread", strand] = z_copies(
            lambda z: slice_out.at[strand, z], slice_in.at[strand, z_me], z_sems.at[strand, 0], z_sems.at[strand, 1]
        )

    def scan_half(strand):
        waits["spread", strand]()
        run = jnp.zeros((slice_rows, 128), F32)
        for i in range(zs):
            z = order(i)
            scan_out[strand, z] = run
            run = slice_in[strand, z, slice_rows : slice_rows + 1] * run + slice_in[strand, z, 0:slice_rows]
        total_out[strand] = run
        copy = remote(
            total_out.at[strand],
            total_in.at[strand],
            pair_sems.at[strand, 2],
            pair_sems.at[strand, 3],
            "seq",
            x_peer,
        )
        copy.start()
        waits["swap", strand] = copy.wait

    def send_back(strand):
        waits["swap", strand]()
        run = total_in[strand] * jnp.where(x_me == 1 - core, 1.0, 0.0)
        for i in range(zs):
            z = order(i)
            scan_out[strand, z] = scan_out[strand, z] + run
            run = slice_in[strand, z, slice_rows : slice_rows + 1] * run
        back_in[strand, z_me] = scan_out[strand, z_me]
        waits["back", strand] = z_copies(
            lambda z: scan_out.at[strand, z], back_in.at[strand, z_me], z_sems.at[strand, 2], z_sems.at[strand, 3]
        )

    def pass_on(strand):
        waits["back", strand]()
        mine = pair_out.at[strand, core]
        for k in range(2):
            rows = slice(k * 128, (k + 1) * 128)
            enter = back_in[strand, k * half_slices : (k + 1) * half_slices].reshape(128, 128)
            entering[strand, core, rows] = enter
            next_out[strand, rows] = gain_of(mine, k) * enter + mine[rows]
        copy = remote(
            next_out.at[strand],
            entering.at[strand, core],
            pair_sems.at[strand, 4],
            pair_sems.at[strand, 5],
            "seq",
            core_peer,
        )
        copy.start()
        waits["pass", strand] = copy.wait

    def enter_chunks(strand):
        waits["pass", strand]()
        lanes = STRANDS[strand]
        for d in range(2):
            terms = terms_of(strand, d)
            target = states if terms is ends_ref else adjoints
            run = jnp.concatenate([entering[strand, d, k * 128 : (k + 1) * 128] for k in range(2)], axis=1)
            for c in way[d]:
                target[c, :, lanes] = run
                run = run * gain_ref[c, 0:1, lanes] + terms[c, :, lanes]
            if target is states:
                target[chunks, :, lanes] = run

    def cross(c, strand):
        span = slice(c * Q, (c + 1) * Q)
        lanes = STRANDS[strand]
        state_hi, state_lo = split2(states[c, :, lanes])
        adj_hi, adj_lo = split2(adjoints[c, :, lanes])
        xhi, xlo, ghi, glo = xhi_ref[span, lanes], xlo_ref[span, lanes], ghi_ref[span, lanes], glo_ref[span, lanes]
        db = dot_nt(xhi, adj_hi) + dot_nt(xlo, adj_hi) + dot_nt(xhi, adj_lo)
        dc = dot_nt(ghi, state_hi) + dot_nt(glo, state_hi) + dot_nt(ghi, state_lo)
        part[c, :, :, 0:128] = part[c, :, :, 0:128] + db.reshape(nh, part_rows, 128)
        part[c, :, :, 128:256] = part[c, :, :, 128:256] + dc.reshape(nh, part_rows, 128)

    prepare(0)
    trade(0)
    gathered()
    spread_chip(0)
    prepare(1)
    trade(1)
    scan_half(0)
    inside(0, 0)
    spread_chip(1)
    inside(0, 1)
    send_back(0)
    inside(1, 0)
    inside(1, 1)
    scan_half(1)
    inside(2, 0)
    pass_on(0)
    inside(2, 1)
    send_back(1)
    inside(3, 0)
    inside(3, 1)
    enter_chunks(0)
    pass_on(1)

    pick = jnp.where(iota((8, 512), 0) == iota((8, 512), 1) // 64, 1.0, 0.0)
    pick_bf = pick.astype(BF16)
    pick2_bf = jnp.where(iota((8, 256), 0) % 4 == iota((8, 256), 1) // 64, 1.0, 0.0).astype(BF16)
    ones_bf = jnp.ones((8, 128), BF16)

    def same_place(c, carry):
        span = pl.ds(pl.multiple_of(c * Q, Q), Q)
        bc_prod = split2(b_ref[span, :].astype(F32) * c_ref[span, :].astype(F32))
        score8 = dot_nt(ones_bf, bc_prod[0]) + dot_nt(ones_bf, bc_prod[1])
        xg = split2(x_ref[span, :].astype(F32) * g_ref[span, :].astype(F32))
        pair8 = dot_nt(pick2_bf, xg[0]) + dot_nt(pick2_bf, xg[1])
        other_ref[:, span] = score8 * pair8
        return carry

    lax.fori_loop(0, chunks, same_place, 0)
    for c in range(chunks):
        cross(c, 0)
    enter_chunks(1)

    sent = []
    for c in range(chunks):
        cross(c, 1)
        sent.append(
            head_copies(
                lambda peer, c=c: part.at[c, peer], got.at[c, head_me], head_sems.at[0, c], head_sems.at[1, c]
            )
        )

    def across(c, carry):
        span = pl.ds(pl.multiple_of(c * Q, Q), Q)
        state_hi, state_lo = split2(states[c])
        adj_hi, adj_lo = split2(adjoints[c])
        bc, cc = b_ref[span, :], c_ref[span, :]
        v = dot(bc, adj_hi) + dot(bc, adj_lo)
        y = dot(cc, state_hi) + dot(cc, state_lo)
        scaled = el_ref[span, :] * v
        dx_ref[span, :] = dx_ref[span, :] + scaled[:, FRONT] + scaled[:, MIRROR]
        x_prod = split2((xhi_ref[span, :].astype(F32) + xlo_ref[span, :].astype(F32)) * v)
        g_prod = split2((ghi_ref[span, :].astype(F32) + glo_ref[span, :].astype(F32)) * y)
        col8 = col_keep[c] + dot_nt(pick_bf, x_prod[0]) + dot_nt(pick_bf, x_prod[1])
        row8 = row_keep[c] + dot_nt(pick_bf, g_prod[0]) + dot_nt(pick_bf, g_prod[1])
        s8 = jnp.concatenate([rows_ref[c, 0, 12:16, :], rows_ref[c, 1, 12:16, :]], axis=0)
        step8 = col8 / s8 + other_ref[:, span]
        flow_f = jnp.sum(states[c + 1, :, FRONT] * adjoints[c, :, FRONT], axis=0, keepdims=True)
        under = lax.rem(c + chunks, chunks + 1)
        flow_m = jnp.sum(states[under, :, MIRROR] * adjoints[c, :, MIRROR], axis=0, keepdims=True)
        flow8 = jnp.sum(pick * jnp.concatenate([flow_f, flow_m], axis=1), axis=1, keepdims=True)
        diff = split3(row8 - col8)
        front8 = iota((8, Q), 0) < 4
        decay8 = jnp.where(front8, dot_sum(diff, low_one), dot_sum(diff, up_one)) + flow8
        own_ref[0:4, span] = step8[0:4]
        own_ref[4:8, span] = decay8[0:4]
        other_ref[0:4, span] = step8[4:8]
        other_ref[4:8, span] = decay8[4:8]
        return carry

    def add_up(c):
        sent[c]()
        total = part[c, head_me]
        for k in range(1, nh):
            total = total + got[c, lax.rem(head_me + k, nh)]
        sums_ref[c, head_me] = total
        return head_copies(
            lambda peer: sums_ref.at[c, head_me], sums_ref.at[c, head_me], head_sems.at[2, c], head_sems.at[3, c]
        )

    lax.fori_loop(0, chunks, across, 0)
    ny = nh // 2
    y_me, side = lax.rem(head_me, ny), head_me // ny
    x_head = lax.rem(head_me + ny, nh)
    others[y_me] = other_ref[...]

    def y_copy(k):
        peer = side * ny + lax.rem(y_me + k, ny)
        return remote(other_ref, others.at[y_me], other_sems.at[0, k], other_sems.at[1, k], "head", peer)

    shared = every(ny, y_copy)

    def find(head):
        place = 0 * head
        for k in range(nh * 4):
            place = jnp.where(heads_ref[k] == head, k, place)
        return place

    def row_of(place, row):
        return others[lax.rem(place // 4, ny), pl.ds(lax.rem(place, 4) + row, 1), :]

    ended = [add_up(c) for c in range(chunks // 2)]
    shared()
    for h in range(4):
        place = find(x_head * 4 + h)
        far_out[h : h + 1, :] = row_of(place, 0)
        far_out[4 + h : 5 + h, :] = row_of(place, 4)
    far = remote(far_out, far_in, other_sems.at[0, 0], other_sems.at[1, 0], "head", x_head)
    far.start()
    ended += [add_up(c) for c in range(chunks // 2, chunks)]
    far.wait()
    for h in range(4):
        place = find(head_me * 4 + h)
        near = place // (4 * ny) == side
        for row, target in ((0, dstep_ref), (4, ddecay_ref)):
            back = jnp.where(near, row_of(place, row), far_in[row + h : row + h + 1, :])
            target[h : h + 1, :] = own_ref[row + h : row + h + 1, :] + back
    for wait in ended:
        wait()


def hand_on(dx_ref, sums_ref, step_ref, decay_ref, dx_out, db_out, dc_out, step_out, decay_out):
    dx_out[...] = dx_ref[...]
    db_out[...] = sums_ref[:, 0:128]
    dc_out[...] = sums_ref[:, 128:256]
    step_out[...] = step_ref[...]
    decay_out[...] = decay_ref[...]


def on_device(signal, write_keys, read_queries, step_sizes, log_decay, mirror_heads, contig_starts, out_grad):
    nh, ns = lax.axis_size("head"), lax.axis_size("seq")
    length = signal.shape[0]
    chunks = length // Q
    zs = ns // 4
    slice_rows = 256 // zs
    part_rows = Q // nh
    vmem = pl.BlockSpec(memory_space=pltpu.VMEM)
    smem = pl.BlockSpec(memory_space=pltpu.SMEM)
    across_lanes = pl.BlockSpec((4, Q), lambda i: (0, i))

    def across_rows(width):
        return pl.BlockSpec((Q, width), lambda i: (i, 0))

    def shape(*dims, dtype=F32):
        return jax.ShapeDtypeStruct(dims, dtype)

    def room(*dims, dtype=F32):
        return pltpu.VMEM(dims, dtype)

    dx, sums, dstep, ddecay = pl.pallas_call(
        functools.partial(kernel, nh, ns),
        out_shape=[shape(length, 256), shape(chunks, nh, part_rows, 256), shape(4, length), shape(4, length)],
        in_specs=[smem] * 2 + [vmem] * 6,
        out_specs=[vmem] * 4,
        scratch_shapes=[
            room(nh, 8, length),
            room(chunks, 2, 16, Q),
            room(2, length, 16),
            room(length, 512, dtype=BF16),
            room(length, 512, dtype=BF16),
            room(length, 512, dtype=BF16),
            room(length, 512, dtype=BF16),
            room(length, 512),
            room(chunks, 128, 512),
            room(chunks, 128, 512),
            room(chunks, 8, 512),
            room(2, 2, 272, 128),
            room(2, 272, 128),
            room(2, zs, slice_rows + 8, 128),
            room(2, zs, slice_rows + 8, 128),
            room(2, zs, slice_rows, 128),
            room(2, slice_rows, 128),
            room(2, slice_rows, 128),
            room(2, zs, slice_rows, 128),
            room(2, 256, 128),
            room(2, 2, 256, 128),
            room(chunks + 1, 128, 512),
            room(chunks, 128, 512),
            room(Q, Q),
            room(4, Q, Q),
            room(4, Q, Q, dtype=BF16),
            room(4, Q, Q, dtype=BF16),
            room(Q, Q, dtype=BF16),
            room(Q, Q, dtype=BF16),
            room(Q, 128),
            room(chunks, 8, Q),
            room(chunks, 8, Q),
            room(chunks, nh, part_rows, 256),
            room(chunks, nh, part_rows, 256),
            room(8, length),
            room(8, length),
            room(nh // 2, 8, length),
            room(8, length),
            room(8, length),
            pltpu.SemaphoreType.DMA((2, nh)),
            pltpu.SemaphoreType.DMA((2, 6)),
            pltpu.SemaphoreType.DMA((2, 4, zs)),
            pltpu.SemaphoreType.DMA((4, chunks, nh)),
            pltpu.SemaphoreType.DMA((2, nh)),
        ],
        compiler_params=pltpu.CompilerParams(
            vmem_limit_bytes=VMEM_LIMIT, collective_id=0, has_side_effects=True
        ),
        name="mixer_backward",
    )(mirror_heads, contig_starts, signal, out_grad, write_keys, read_queries, step_sizes, log_decay)

    return pl.pallas_call(
        hand_on,
        out_shape=[shape(length, 256), shape(length, 128), shape(length, 128), shape(4, length), shape(4, length)],
        grid=(chunks,),
        in_specs=[across_rows(256)] * 2 + [across_lanes] * 2,
        out_specs=[across_rows(256), across_rows(128), across_rows(128)] + [across_lanes] * 2,
        name="hand_on",
    )(dx, sums.reshape(length, 256), dstep, ddecay)


def solution(mesh):
    return jax.shard_map(
        on_device,
        mesh=mesh,
        in_specs=(
            P("seq", "head"),
            P("seq", None),
            P("seq", None),
            P("head", "seq"),
            P("head", "seq"),
            P(),
            P(),
            P("seq", "head"),
        ),
        out_specs=(
            P("seq", "head"),
            P("seq", None),
            P("seq", None),
            P("head", "seq"),
            P("head", "seq"),
        ),
        check_vma=False,
    )
```

```python
import functools

import jax
import jax.numpy as jnp
from jax import lax
from jax.experimental import pallas as pl
from jax.experimental.pallas import tpu as pltpu
from jax.sharding import PartitionSpec as P

Q = 256
STRIP = 32
LOG2E = 1.4426950408889634
F32, BF16 = jnp.float32, jnp.bfloat16
MESH = pl.DeviceIdType.MESH
VMEM_LIMIT = 56 * 1024 * 1024


def iota(shape, dim):
    return lax.broadcasted_iota(jnp.int32, shape, dim)


def split2(v):
    hi = v.astype(BF16)
    return hi, (v - hi.astype(F32)).astype(BF16)


def split3(v):
    hi = v.astype(BF16)
    rest = v - hi.astype(F32)
    mid = rest.astype(BF16)
    return hi, mid, (rest - mid.astype(F32)).astype(BF16)


def dot(a, b):
    return lax.dot_general(a, b, (((1,), (0,)), ((), ())), preferred_element_type=F32)


def dot_nt(a, b):
    return lax.dot_general(a, b, (((1,), (1,)), ((), ())), preferred_element_type=F32)


def dot_sum(parts, b, how=dot):
    total = how(parts[0], b)
    for part in parts[1:]:
        total = total + how(part, b)
    return total


def segment_at(starts_ref, t):
    total = (starts_ref[0] <= t).astype(jnp.int32)
    for k in range(1, 4):
        total = total + (starts_ref[k] <= t).astype(jnp.int32)
    return total


FRONT, MIRROR = slice(0, 256), slice(256, 512)
STRANDS = (FRONT, MIRROR)


def kernel(
    nh,
    ns,
    heads_ref,
    starts_ref,
    x_hbm,
    g_hbm,
    b_hbm,
    c_hbm,
    step_ref,
    decay_ref,
    dx_hbm,
    sums_hbm,
    dstep_ref,
    ddecay_ref,
    x_ref,
    g_ref,
    b_ref,
    c_ref,
    bt_ref,
    ct_ref,
    dx_ref,
    sums_ref,
    local_sems,
    all_ref,
    rows_ref,
    cols_ref,
    xhi_ref,
    xlo_ref,
    ghi_ref,
    glo_ref,
    el_ref,
    ends_ref,
    seeds_ref,
    gain_ref,
    pair_out,
    pair_in,
    slice_out,
    slice_in,
    scan_out,
    total_out,
    total_in,
    back_in,
    next_out,
    entering,
    states,
    adjoints,
    gm,
    pt,
    whi,
    wlo,
    dghi,
    dglo,
    csum,
    row_keep,
    col_keep,
    part,
    got,
    own_ref,
    other_ref,
    others,
    far_out,
    far_in,
    gather_sems,
    pair_sems,
    z_sems,
    head_sems,
    other_sems,
):
    length = x_ref.shape[0]
    chunks = length // Q
    head_me = lax.axis_index("head")
    seq_me = lax.axis_index("seq")
    offset = seq_me * length
    core = lax.rem(seq_me, 2)
    zs = ns // 4
    z_me = lax.rem(seq_me // 2, zs)
    x_me = seq_me // (2 * zs)
    core_peer = seq_me + 1 - 2 * core
    x_peer = lax.rem(seq_me + ns // 2, ns)

    def z_peer(k):
        z = lax.rem(z_me + k, zs)
        return z, x_me * 2 * zs + z * 2 + core

    loads = [
        pltpu.make_async_copy(a, b, local_sems.at[i])
        for i, (a, b) in enumerate(((x_hbm, x_ref), (g_hbm, g_ref), (b_hbm, b_ref), (c_hbm, c_ref)))
    ]
    for load in loads:
        load.start()

    all_ref[head_me, 0:4, :] = step_ref[...]
    all_ref[head_me, 4:8, :] = decay_ref[...]
    barrier = pltpu.get_barrier_semaphore()

    def greet_head(k, carry):
        peer = lax.rem(head_me + k, nh)
        pl.semaphore_signal(barrier, inc=1, device_id={"head": peer}, device_id_type=MESH)
        return carry

    def greet_z(k, carry):
        pl.semaphore_signal(barrier, inc=1, device_id={"seq": z_peer(k)[1]}, device_id_type=MESH)
        return carry

    lax.fori_loop(1, nh, greet_head, 0)
    lax.fori_loop(1, zs, greet_z, 0)
    pl.semaphore_signal(barrier, inc=1, device_id={"seq": core_peer}, device_id_type=MESH)
    pl.semaphore_signal(barrier, inc=1, device_id={"seq": x_peer}, device_id_type=MESH)
    pl.semaphore_wait(barrier, nh + zs)

    def remote(source, target, send, recv, axis, peer):
        return pltpu.make_async_remote_copy(
            src_ref=source,
            dst_ref=target,
            send_sem=send,
            recv_sem=recv,
            device_id={axis: peer},
            device_id_type=MESH,
        )

    def every(count, copy):
        def begin(k, carry):
            copy(k).start()
            return carry

        def end(k, carry):
            copy(k).wait()
            return carry

        lax.fori_loop(1, count, begin, 0)
        return lambda: lax.fori_loop(1, count, end, 0)

    def head_copies(source, target, send, recv):
        def copy(k):
            peer = lax.rem(head_me + k, nh)
            return remote(source(peer), target, send.at[k], recv.at[k], "head", peer)

        return every(nh, copy)

    def z_copies(source, target, send, recv):
        def copy(k):
            z, peer = z_peer(k)
            return remote(source(z), target, send.at[k], recv.at[k], "seq", peer)

        return every(zs, copy)

    gathered = head_copies(
        lambda peer: all_ref.at[head_me], all_ref.at[head_me], gather_sems.at[0], gather_sems.at[1]
    )

    lower = iota((Q, Q), 0) >= iota((Q, Q), 1)
    upper = iota((Q, Q), 0) <= iota((Q, Q), 1)
    low_one = jnp.where(lower, 1.0, 0.0).astype(BF16)
    up_one = jnp.where(upper, 1.0, 0.0).astype(BF16)
    lane = iota((16, 512), 1)
    source = jnp.where(lane < 256, 8, 4) + (lane % 256) // 64
    spread = jnp.where(iota((16, 512), 0) == source, 1.0, 0.0).astype(BF16)
    pick8 = jnp.where(iota((8, 256), 0) == iota((8, 256), 1) // 64, 1.0, 0.0)


    def prepare(strand):
        def chunk(c):
            base = c * Q
            span = slice(base, base + Q)
            if strand == 0:
                s4 = all_ref[head_me, 0:4, span]
                d4 = all_ref[head_me, 4:8, span]
            else:
                heads = [heads_ref[head_me * 4 + h] for h in range(4)]
                s4 = jnp.concatenate([all_ref[i // 4, pl.ds(i % 4, 1), span] for i in heads], axis=0)
                d4 = jnp.concatenate([all_ref[i // 4, pl.ds(i % 4 + 4, 1), span] for i in heads], axis=0)
            s8 = jnp.concatenate([s4, s4], axis=0)
            d8 = jnp.concatenate([d4, d4], axis=0)
            cum8 = dot_sum(split3(d8), low_one if strand else up_one) * LOG2E
            total8 = cum8[:, 0:1] if strand else cum8[:, Q - 1 : Q]
            first = offset + base
            seg = segment_at(starts_ref, first + iota((8, Q), 1))
            seg_first, seg_last = segment_at(starts_ref, first), segment_at(starts_ref, first + Q - 1)
            if strand:
                seg_in, seg_far = segment_at(starts_ref, first + Q), seg_first
            else:
                seg_in = jnp.where(first == 0, -1, segment_at(starts_ref, first - 1))
                seg_far = seg_last
            e8 = jnp.where(seg == seg_in, jnp.exp2(cum8), 0.0)
            l8 = jnp.where(seg == seg_far, jnp.exp2(total8 - cum8) * s8, 0.0)
            gain8 = jnp.exp2(total8) * (seg_in == seg_far).astype(F32)
            gain = jnp.sum(pick8 * gain8, axis=0, keepdims=True)
            gain_ref[c, :, STRANDS[strand]] = jnp.broadcast_to(gain, (8, 256))
            rows = jnp.concatenate([cum8[0:4], e8[0:4], l8[0:4], s8[0:4]], axis=0)
            rows_ref[c, strand] = rows
            cols = rows.T
            cols_ref[strand, span, :] = cols
            wide = dot_sum(split3(cols), spread)
            lanes = STRANDS[strand]
            el_ref[span, lanes] = wide[:, 0:256]
            xhi, xlo = split2(x_ref[span, :].astype(F32) * wide[:, 0:256])
            ghi, glo = split2(g_ref[span, :].astype(F32) * wide[:, 256:512])
            xhi_ref[span, lanes] = xhi
            xlo_ref[span, lanes] = xlo
            ghi_ref[span, lanes] = ghi
            glo_ref[span, lanes] = glo
            if strand == 0:
                bt_ref[c] = b_ref[span, :].T
                ct_ref[c] = c_ref[span, :].T
            bt, ct = bt_ref[c], ct_ref[c]
            ends_ref[c, :, lanes] = dot(bt, xhi) + dot(bt, xlo)
            seeds_ref[c, :, lanes] = dot(ct, ghi) + dot(ct, glo)

        for c in range(chunks):
            chunk(c)


    ascending, descending = range(chunks), range(chunks - 1, -1, -1)
    way = (ascending, descending)

    def terms_of(strand, d):
        return (ends_ref, seeds_ref)[(strand + d) % 2]

    def fold(strand):
        lanes = STRANDS[strand]
        for d in range(2):
            run = None
            for c in way[d]:
                term = terms_of(strand, d)[c, :, lanes]
                run = term if run is None else run * gain_ref[c, 0:1, lanes] + term
            for k in range(2):
                pair_out[strand, d, k * 128 : (k + 1) * 128] = run[:, k * 128 : (k + 1) * 128]
        whole = gain_ref[0, :, lanes]
        for c in range(1, chunks):
            whole = whole * gain_ref[c, :, lanes]
        for d in range(2):
            for k in range(2):
                pair_out[strand, d, 256 + k * 8 : 264 + k * 8] = whole[:, k * 128 : (k + 1) * 128]


    half_mask = [jnp.where(iota((1, 128), 1) // 64 == k, 1.0, 0.0).astype(BF16) for k in range(2)]
    zero_row = jnp.zeros((8, 128), F32)
    part_rows = Q // nh

    def put_part(c, lanes, value):
        part[c, :, :, lanes] = value.reshape(nh, part_rows, 128)

    kept_sums = {}

    def inside(c, i):
        base = c * Q
        span = slice(base, base + Q)
        first = offset + base
        bc, cc = b_ref[span, :], c_ref[span, :]
        xs = [x_ref[span, k * 128 : (k + 1) * 128] for k in range(2)]
        gs = [g_ref[span, k * 128 : (k + 1) * 128] for k in range(2)]
        if i == 0:
            seg_s = segment_at(starts_ref, first + iota((Q, 1), 0))
            seg_t = segment_at(starts_ref, first + iota((1, Q), 1))
            gm[...] = jnp.where(seg_s == seg_t, dot_nt(bc, cc), 0.0)
            for h in range(4):
                pt[h] = dot_nt(xs[h // 2] * half_mask[h % 2], gs[h // 2])

        def strip(r, sums):
            start = pl.multiple_of(i * 128 + r * STRIP, STRIP)
            at = pl.ds(start, STRIP)
            at_cols = pl.ds(pl.multiple_of(base + start, STRIP), STRIP)
            col_f, col_m = cols_ref[0, at_cols, :], cols_ref[1, at_cols, :]
            lane128 = iota((STRIP, 128), 1)
            s_index = r * STRIP + iota((STRIP, 128), 0)
            ahead = lane128 > s_index
            behind = lane128 < s_index
            sums = list(sums)
            collected = jnp.zeros((STRIP, 128), F32)
            dg = [jnp.zeros((STRIP, 128), F32) for _ in range(2)]
            for h in range(4):
                cum_f, cum_m = col_f[:, h : h + 1], col_m[:, h : h + 1]
                step_f, step_m = col_f[:, 12 + h : 13 + h], col_m[:, 12 + h : 13 + h]
                lane_sums = [None, None]
                for j in range(2):
                    t = slice(j * 128, (j + 1) * 128)
                    row_f = rows_ref[c, 0, h : h + 1, t]
                    row_m = rows_ref[c, 1, h : h + 1, t]
                    if i == j:
                        gap = jnp.where(behind, row_m - cum_m, row_f - cum_f)
                        step = jnp.where(behind, step_m, jnp.where(ahead, step_f, step_f + step_m))
                    elif j > i:
                        gap, step = row_f - cum_f, step_f
                    else:
                        gap, step = row_m - cum_m, step_m
                    d = jnp.exp2(gap) * step
                    w = d * gm[at, t]
                    p = pt[h, at, t]
                    dg[j] = dg[j] + d * p
                    e = w * p
                    hi, lo = split2(w)
                    whi[h, at, t] = hi
                    wlo[h, at, t] = lo
                    if i == j:
                        parts = [jnp.where(ahead, e, 0.0), jnp.where(behind, e, 0.0)]
                    else:
                        parts = [e, None] if j > i else [None, e]
                    for strand in range(2):
                        piece = parts[strand]
                        if piece is None:
                            continue
                        slot = (h * 2 + j) * 2 + strand
                        add = piece[0:8]
                        for u in range(1, STRIP // 8):
                            add = add + piece[u * 8 : (u + 1) * 8]
                        sums[slot] = sums[slot] + add
                        old = lane_sums[strand]
                        lane_sums[strand] = piece if old is None else old + piece
                for strand in range(2):
                    total = jnp.sum(lane_sums[strand], axis=1, keepdims=True)
                    collected = jnp.where(lane128 == strand * 4 + h, total, collected)
            csum[at, :] = collected
            rows_at = segment_at(starts_ref, first + start + iota((STRIP, 1), 0))
            for j in range(2):
                t = slice(j * 128, (j + 1) * 128)
                cols_at = segment_at(starts_ref, first + j * 128 + iota((1, 128), 1))
                hi, lo = split2(jnp.where(rows_at == cols_at, dg[j], 0.0))
                dghi[at, t] = hi
                dglo[at, t] = lo
            return tuple(sums)

        kept_sums[i] = lax.fori_loop(0, 128 // STRIP, strip, (zero_row,) * 16)
        if i == 0:
            return
        row_sums = [kept_sums[0], kept_sums[1]]
        rows_in = []
        for strand in range(2):
            for h in range(4):
                lanes = []
                for j in range(2):
                    slot = (h * 2 + j) * 2 + strand
                    lanes.append(jnp.sum(row_sums[0][slot] + row_sums[1][slot], axis=0, keepdims=True))
                rows_in.append(jnp.concatenate(lanes, axis=1))
        row_keep[c] = jnp.concatenate(rows_in, axis=0)
        col_keep[c] = csum[...].T[0:8]
        for k in range(2):
            total = None
            for h in (2 * k, 2 * k + 1):
                masked = gs[k] * half_mask[h % 2]
                term = dot(whi[h], masked) + dot(wlo[h], masked)
                total = term if total is None else total + term
            dx_ref[span, k * 128 : (k + 1) * 128] = total
        put_part(c, slice(0, 128), dot(dghi[...], cc) + dot(dglo[...], cc))
        dgt_hi, dgt_lo = dghi[...].T, dglo[...].T
        put_part(c, slice(128, 256), dot(dgt_hi, bc) + dot(dgt_lo, bc))


    other = 1 - core
    slice_rows = 256 // zs
    half_slices = zs // 2
    waits = {}

    def gain_of(ref, k):
        return ref[256 + k * 8 : 257 + k * 8]

    def order(i):
        return i + core * (zs - 1 - 2 * i)

    def trade(strand):
        fold(strand)
        copy = remote(
            pair_out.at[strand, other],
            pair_in.at[strand],
            pair_sems.at[strand, 0],
            pair_sems.at[strand, 1],
            "seq",
            core_peer,
        )
        copy.start()
        waits["trade", strand] = copy.wait

    def spread_chip(strand):
        waits["trade", strand]()
        mine, theirs = pair_out.at[strand, core], pair_in.at[strand]
        for k in range(2):
            rows = slice(k * 128, (k + 1) * 128)
            slices = slice(k * half_slices, (k + 1) * half_slices)
            chip = gain_of(theirs, k) * mine[rows] + theirs[rows]
            slice_out[strand, slices, 0:slice_rows] = chip.reshape(half_slices, slice_rows, 128)
            gain = gain_of(theirs, k) * gain_of(mine, k)
            slice_out[strand, slices, slice_rows : slice_rows + 8] = jnp.broadcast_to(
                gain[None], (half_slices, 8, 128)
            )
        slice_in[strand, z_me] = slice_out[strand, z_me]
        waits["spread", strand] = z_copies(
            lambda z: slice_out.at[strand, z], slice_in.at[strand, z_me], z_sems.at[strand, 0], z_sems.at[strand, 1]
        )

    def scan_half(strand):
        waits["spread", strand]()
        run = jnp.zeros((slice_rows, 128), F32)
        for i in range(zs):
            z = order(i)
            scan_out[strand, z] = run
            run = slice_in[strand, z, slice_rows : slice_rows + 1] * run + slice_in[strand, z, 0:slice_rows]
        total_out[strand] = run
        copy = remote(
            total_out.at[strand],
            total_in.at[strand],
            pair_sems.at[strand, 2],
            pair_sems.at[strand, 3],
            "seq",
            x_peer,
        )
        copy.start()
        waits["swap", strand] = copy.wait

    def send_back(strand):
        waits["swap", strand]()
        run = total_in[strand] * jnp.where(x_me == 1 - core, 1.0, 0.0)
        for i in range(zs):
            z = order(i)
            scan_out[strand, z] = scan_out[strand, z] + run
            run = slice_in[strand, z, slice_rows : slice_rows + 1] * run
        back_in[strand, z_me] = scan_out[strand, z_me]
        waits["back", strand] = z_copies(
            lambda z: scan_out.at[strand, z], back_in.at[strand, z_me], z_sems.at[strand, 2], z_sems.at[strand, 3]
        )

    def pass_on(strand):
        waits["back", strand]()
        mine = pair_out.at[strand, core]
        for k in range(2):
            rows = slice(k * 128, (k + 1) * 128)
            enter = back_in[strand, k * half_slices : (k + 1) * half_slices].reshape(128, 128)
            entering[strand, core, rows] = enter
            next_out[strand, rows] = gain_of(mine, k) * enter + mine[rows]
        copy = remote(
            next_out.at[strand],
            entering.at[strand, core],
            pair_sems.at[strand, 4],
            pair_sems.at[strand, 5],
            "seq",
            core_peer,
        )
        copy.start()
        waits["pass", strand] = copy.wait

    def enter_chunks(strand):
        waits["pass", strand]()
        lanes = STRANDS[strand]
        for d in range(2):
            terms = terms_of(strand, d)
            target = states if terms is ends_ref else adjoints
            run = jnp.concatenate([entering[strand, d, k * 128 : (k + 1) * 128] for k in range(2)], axis=1)
            for c in way[d]:
                target[c, :, lanes] = run
                run = run * gain_ref[c, 0:1, lanes] + terms[c, :, lanes]
            if target is states:
                target[chunks, :, lanes] = run

    def cross(c, strand):
        span = slice(c * Q, (c + 1) * Q)
        lanes = STRANDS[strand]
        state_hi, state_lo = split2(states[c, :, lanes])
        adj_hi, adj_lo = split2(adjoints[c, :, lanes])
        xhi, xlo, ghi, glo = xhi_ref[span, lanes], xlo_ref[span, lanes], ghi_ref[span, lanes], glo_ref[span, lanes]
        db = dot_nt(xhi, adj_hi) + dot_nt(xlo, adj_hi) + dot_nt(xhi, adj_lo)
        dc = dot_nt(ghi, state_hi) + dot_nt(glo, state_hi) + dot_nt(ghi, state_lo)
        part[c, :, :, 0:128] = part[c, :, :, 0:128] + db.reshape(nh, part_rows, 128)
        part[c, :, :, 128:256] = part[c, :, :, 128:256] + dc.reshape(nh, part_rows, 128)

    for load in loads:
        load.wait()
    prepare(0)
    trade(0)
    gathered()
    spread_chip(0)
    prepare(1)
    trade(1)
    scan_half(0)
    inside(0, 0)
    spread_chip(1)
    inside(0, 1)
    send_back(0)
    inside(1, 0)
    inside(1, 1)
    scan_half(1)
    inside(2, 0)
    pass_on(0)
    inside(2, 1)
    send_back(1)
    inside(3, 0)
    inside(3, 1)
    enter_chunks(0)
    pass_on(1)

    pick = jnp.where(iota((8, 512), 0) == iota((8, 512), 1) // 64, 1.0, 0.0)
    pick_bf = pick.astype(BF16)
    pick2_bf = jnp.where(iota((8, 256), 0) % 4 == iota((8, 256), 1) // 64, 1.0, 0.0).astype(BF16)
    ones_bf = jnp.ones((8, 128), BF16)

    def same_place(c, carry):
        span = pl.ds(pl.multiple_of(c * Q, Q), Q)
        bc_prod = split2(b_ref[span, :].astype(F32) * c_ref[span, :].astype(F32))
        score8 = dot_nt(ones_bf, bc_prod[0]) + dot_nt(ones_bf, bc_prod[1])
        xg = split2(x_ref[span, :].astype(F32) * g_ref[span, :].astype(F32))
        pair8 = dot_nt(pick2_bf, xg[0]) + dot_nt(pick2_bf, xg[1])
        other_ref[:, span] = score8 * pair8
        return carry

    lax.fori_loop(0, chunks, same_place, 0)
    for c in range(chunks):
        cross(c, 0)
    enter_chunks(1)

    sent = []
    for c in range(chunks):
        cross(c, 1)
        sent.append(
            head_copies(
                lambda peer, c=c: part.at[c, peer], got.at[c, head_me], head_sems.at[0, c], head_sems.at[1, c]
            )
        )

    def across(c, carry):
        span = pl.ds(pl.multiple_of(c * Q, Q), Q)
        state_hi, state_lo = split2(states[c])
        adj_hi, adj_lo = split2(adjoints[c])
        bc, cc = b_ref[span, :], c_ref[span, :]
        v = dot(bc, adj_hi) + dot(bc, adj_lo)
        y = dot(cc, state_hi) + dot(cc, state_lo)
        scaled = el_ref[span, :] * v
        dx_ref[span, :] = dx_ref[span, :] + scaled[:, FRONT] + scaled[:, MIRROR]
        x_prod = split2((xhi_ref[span, :].astype(F32) + xlo_ref[span, :].astype(F32)) * v)
        g_prod = split2((ghi_ref[span, :].astype(F32) + glo_ref[span, :].astype(F32)) * y)
        col8 = col_keep[c] + dot_nt(pick_bf, x_prod[0]) + dot_nt(pick_bf, x_prod[1])
        row8 = row_keep[c] + dot_nt(pick_bf, g_prod[0]) + dot_nt(pick_bf, g_prod[1])
        s8 = jnp.concatenate([rows_ref[c, 0, 12:16, :], rows_ref[c, 1, 12:16, :]], axis=0)
        step8 = col8 / s8 + other_ref[:, span]
        flow_f = jnp.sum(states[c + 1, :, FRONT] * adjoints[c, :, FRONT], axis=0, keepdims=True)
        under = lax.rem(c + chunks, chunks + 1)
        flow_m = jnp.sum(states[under, :, MIRROR] * adjoints[c, :, MIRROR], axis=0, keepdims=True)
        flow8 = jnp.sum(pick * jnp.concatenate([flow_f, flow_m], axis=1), axis=1, keepdims=True)
        diff = split3(row8 - col8)
        front8 = iota((8, Q), 0) < 4
        decay8 = jnp.where(front8, dot_sum(diff, low_one), dot_sum(diff, up_one)) + flow8
        own_ref[0:4, span] = step8[0:4]
        own_ref[4:8, span] = decay8[0:4]
        other_ref[0:4, span] = step8[4:8]
        other_ref[4:8, span] = decay8[4:8]
        return carry

    def add_up(c):
        sent[c]()
        total = part[c, head_me]
        for k in range(1, nh):
            total = total + got[c, lax.rem(head_me + k, nh)]
        sums_ref[c] = total
        own = pltpu.make_async_copy(sums_ref.at[c], sums_hbm.at[c, head_me], local_sems.at[5 + c])
        own.start()
        stores.append(own)
        return head_copies(
            lambda peer: sums_ref.at[c], sums_hbm.at[c, head_me], head_sems.at[2, c], head_sems.at[3, c]
        )

    lax.fori_loop(0, chunks, across, 0)
    stores = [pltpu.make_async_copy(dx_ref, dx_hbm, local_sems.at[4])]
    stores[0].start()
    ny = nh // 2
    y_me, side = lax.rem(head_me, ny), head_me // ny
    x_head = lax.rem(head_me + ny, nh)
    others[y_me] = other_ref[...]

    def y_copy(k):
        peer = side * ny + lax.rem(y_me + k, ny)
        return remote(other_ref, others.at[y_me], other_sems.at[0, k], other_sems.at[1, k], "head", peer)

    shared = every(ny, y_copy)

    def find(head):
        place = 0 * head
        for k in range(nh * 4):
            place = jnp.where(heads_ref[k] == head, k, place)
        return place

    def row_of(place, row):
        return others[lax.rem(place // 4, ny), pl.ds(lax.rem(place, 4) + row, 1), :]

    ended = [add_up(c) for c in range(chunks // 2)]
    shared()
    for h in range(4):
        place = find(x_head * 4 + h)
        far_out[h : h + 1, :] = row_of(place, 0)
        far_out[4 + h : 5 + h, :] = row_of(place, 4)
    far = remote(far_out, far_in, other_sems.at[0, 0], other_sems.at[1, 0], "head", x_head)
    far.start()
    ended += [add_up(c) for c in range(chunks // 2, chunks)]
    far.wait()
    for h in range(4):
        place = find(head_me * 4 + h)
        near = place // (4 * ny) == side
        for row, target in ((0, dstep_ref), (4, ddecay_ref)):
            back = jnp.where(near, row_of(place, row), far_in[row + h : row + h + 1, :])
            target[h : h + 1, :] = own_ref[row + h : row + h + 1, :] + back
    for wait in ended:
        wait()
    for store in stores:
        store.wait()


def hand_on(dx_ref, sums_ref, step_ref, decay_ref, dx_out, db_out, dc_out, step_out, decay_out, dx, sums, step, decay, sems):
    pieces = []
    for c in range(dx_ref.shape[0] // Q):
        rows = slice(c * Q, (c + 1) * Q)
        pieces.append((sums_ref.at[rows], sums.at[rows], ((sums.at[rows, 0:128], db_out.at[rows]), (sums.at[rows, 128:256], dc_out.at[rows]))))
        pieces.append((dx_ref.at[rows], dx.at[rows], ((dx.at[rows], dx_out.at[rows]),)))
    pieces.append((step_ref, step, ((step, step_out),)))
    pieces.append((decay_ref, decay, ((decay, decay_out),)))
    loads = [pltpu.make_async_copy(a, b, sems.at[0, i]) for i, (a, b, _) in enumerate(pieces)]
    for load in loads:
        load.start()
    stores = []
    for i, (_, _, targets) in enumerate(pieces):
        loads[i].wait()
        for k, (a, b) in enumerate(targets):
            store = pltpu.make_async_copy(a, b, sems.at[1 + k, i])
            store.start()
            stores.append(store)
    for store in stores:
        store.wait()


def on_device(signal, write_keys, read_queries, step_sizes, log_decay, mirror_heads, contig_starts, out_grad):
    nh, ns = lax.axis_size("head"), lax.axis_size("seq")
    length = signal.shape[0]
    chunks = length // Q
    zs = ns // 4
    slice_rows = 256 // zs
    part_rows = Q // nh
    vmem = pl.BlockSpec(memory_space=pltpu.VMEM)
    smem = pl.BlockSpec(memory_space=pltpu.SMEM)
    hbm = pl.BlockSpec(memory_space=pl.ANY)

    def shape(*dims, dtype=F32):
        return jax.ShapeDtypeStruct(dims, dtype)

    def room(*dims, dtype=F32):
        return pltpu.VMEM(dims, dtype)

    dx, sums, dstep, ddecay = pl.pallas_call(
        functools.partial(kernel, nh, ns),
        out_shape=[shape(length, 256), shape(chunks, nh, part_rows, 256), shape(4, length), shape(4, length)],
        in_specs=[smem] * 2 + [hbm] * 4 + [vmem] * 2,
        out_specs=[hbm] * 2 + [vmem] * 2,
        scratch_shapes=[
            room(length, 256, dtype=BF16),
            room(length, 256, dtype=BF16),
            room(length, 128, dtype=BF16),
            room(length, 128, dtype=BF16),
            room(chunks, 128, Q, dtype=BF16),
            room(chunks, 128, Q, dtype=BF16),
            room(length, 256),
            room(chunks, part_rows, 256),
            pltpu.SemaphoreType.DMA((5 + chunks,)),
            room(nh, 8, length),
            room(chunks, 2, 16, Q),
            room(2, length, 16),
            room(length, 512, dtype=BF16),
            room(length, 512, dtype=BF16),
            room(length, 512, dtype=BF16),
            room(length, 512, dtype=BF16),
            room(length, 512),
            room(chunks, 128, 512),
            room(chunks, 128, 512),
            room(chunks, 8, 512),
            room(2, 2, 272, 128),
            room(2, 272, 128),
            room(2, zs, slice_rows + 8, 128),
            room(2, zs, slice_rows + 8, 128),
            room(2, zs, slice_rows, 128),
            room(2, slice_rows, 128),
            room(2, slice_rows, 128),
            room(2, zs, slice_rows, 128),
            room(2, 256, 128),
            room(2, 2, 256, 128),
            room(chunks + 1, 128, 512),
            room(chunks, 128, 512),
            room(Q, Q),
            room(4, Q, Q),
            room(4, Q, Q, dtype=BF16),
            room(4, Q, Q, dtype=BF16),
            room(Q, Q, dtype=BF16),
            room(Q, Q, dtype=BF16),
            room(Q, 128),
            room(chunks, 8, Q),
            room(chunks, 8, Q),
            room(chunks, nh, part_rows, 256),
            room(chunks, nh, part_rows, 256),
            room(8, length),
            room(8, length),
            room(nh // 2, 8, length),
            room(8, length),
            room(8, length),
            pltpu.SemaphoreType.DMA((2, nh)),
            pltpu.SemaphoreType.DMA((2, 6)),
            pltpu.SemaphoreType.DMA((2, 4, zs)),
            pltpu.SemaphoreType.DMA((4, chunks, nh)),
            pltpu.SemaphoreType.DMA((2, nh)),
        ],
        compiler_params=pltpu.CompilerParams(
            vmem_limit_bytes=VMEM_LIMIT, collective_id=0, has_side_effects=True
        ),
        name="mixer_backward",
    )(mirror_heads, contig_starts, signal, out_grad, write_keys, read_queries, step_sizes, log_decay)

    return pl.pallas_call(
        hand_on,
        out_shape=[shape(length, 256), shape(length, 128), shape(length, 128), shape(4, length), shape(4, length)],
        in_specs=[hbm] * 4,
        out_specs=[hbm] * 5,
        scratch_shapes=[
            room(length, 256),
            room(length, 256),
            room(4, length),
            room(4, length),
            pltpu.SemaphoreType.DMA((3, 2 * chunks + 2)),
        ],
        compiler_params=pltpu.CompilerParams(vmem_limit_bytes=VMEM_LIMIT),
        name="hand_on",
    )(dx, sums.reshape(length, 256), dstep, ddecay)


def solution(mesh):
    return jax.shard_map(
        on_device,
        mesh=mesh,
        in_specs=(
            P("seq", "head"),
            P("seq", None),
            P("seq", None),
            P("head", "seq"),
            P("head", "seq"),
            P(),
            P(),
            P("seq", "head"),
        ),
        out_specs=(
            P("seq", "head"),
            P("seq", None),
            P("seq", None),
            P("head", "seq"),
            P("head", "seq"),
        ),
        check_vma=False,
    )
```

```python
import functools

import jax
import jax.numpy as jnp
from jax import lax
from jax.experimental import pallas as pl
from jax.experimental.pallas import tpu as pltpu
from jax.sharding import PartitionSpec as P

Q = 256
STRIP = 32
LOG2E = 1.4426950408889634
F32, BF16 = jnp.float32, jnp.bfloat16
MESH = pl.DeviceIdType.MESH
VMEM_LIMIT = 56 * 1024 * 1024


def iota(shape, dim):
    return lax.broadcasted_iota(jnp.int32, shape, dim)


def split2(v):
    hi = v.astype(BF16)
    return hi, (v - hi.astype(F32)).astype(BF16)


def split3(v):
    hi = v.astype(BF16)
    rest = v - hi.astype(F32)
    mid = rest.astype(BF16)
    return hi, mid, (rest - mid.astype(F32)).astype(BF16)


def dot(a, b):
    return lax.dot_general(a, b, (((1,), (0,)), ((), ())), preferred_element_type=F32)


def dot_nt(a, b):
    return lax.dot_general(a, b, (((1,), (1,)), ((), ())), preferred_element_type=F32)


def dot_sum(parts, b, how=dot):
    total = how(parts[0], b)
    for part in parts[1:]:
        total = total + how(part, b)
    return total


def segment_at(starts_ref, t):
    total = (starts_ref[0] <= t).astype(jnp.int32)
    for k in range(1, 4):
        total = total + (starts_ref[k] <= t).astype(jnp.int32)
    return total


FRONT, MIRROR = slice(0, 256), slice(256, 512)
STRANDS = (FRONT, MIRROR)


def kernel(
    nh,
    ns,
    heads_ref,
    starts_ref,
    x_hbm,
    g_hbm,
    b_hbm,
    c_hbm,
    step_ref,
    decay_ref,
    dx_hbm,
    sums_hbm,
    dstep_ref,
    ddecay_ref,
    x_ref,
    g_ref,
    b_ref,
    c_ref,
    bt_ref,
    ct_ref,
    dx_ref,
    sums_ref,
    local_sems,
    all_ref,
    rows_ref,
    cols_ref,
    hi_ref,
    lo_ref,
    el_ref,
    terms_ref,
    gain_ref,
    pair_out,
    pair_in,
    slice_out,
    slice_in,
    scan_out,
    total_out,
    total_in,
    back_in,
    next_out,
    entering,
    meet,
    gm,
    pt,
    whi,
    wlo,
    dghi,
    dglo,
    csum,
    row_keep,
    col_keep,
    part,
    got,
    own_ref,
    other_ref,
    others,
    far_out,
    far_in,
    gather_sems,
    pair_sems,
    z_sems,
    head_sems,
    other_sems,
):
    length = x_ref.shape[0]
    chunks = length // Q
    head_me = lax.axis_index("head")
    seq_me = lax.axis_index("seq")
    offset = seq_me * length
    core = lax.rem(seq_me, 2)
    zs = ns // 4
    z_me = lax.rem(seq_me // 2, zs)
    x_me = seq_me // (2 * zs)
    core_peer = seq_me + 1 - 2 * core
    x_peer = lax.rem(seq_me + ns // 2, ns)

    def z_peer(k):
        z = lax.rem(z_me + k, zs)
        return z, x_me * 2 * zs + z * 2 + core

    loads = [
        pltpu.make_async_copy(a, b, local_sems.at[i])
        for i, (a, b) in enumerate(((x_hbm, x_ref), (g_hbm, g_ref), (b_hbm, b_ref), (c_hbm, c_ref)))
    ]
    for load in loads:
        load.start()

    all_ref[head_me, 0:4, :] = step_ref[...]
    all_ref[head_me, 4:8, :] = decay_ref[...]
    barrier = pltpu.get_barrier_semaphore()

    def greet_head(k, carry):
        peer = lax.rem(head_me + k, nh)
        pl.semaphore_signal(barrier, inc=1, device_id={"head": peer}, device_id_type=MESH)
        return carry

    def greet_z(k, carry):
        pl.semaphore_signal(barrier, inc=1, device_id={"seq": z_peer(k)[1]}, device_id_type=MESH)
        return carry

    lax.fori_loop(1, nh, greet_head, 0)
    lax.fori_loop(1, zs, greet_z, 0)
    pl.semaphore_signal(barrier, inc=1, device_id={"seq": core_peer}, device_id_type=MESH)
    pl.semaphore_signal(barrier, inc=1, device_id={"seq": x_peer}, device_id_type=MESH)
    pl.semaphore_wait(barrier, nh + zs)

    def remote(source, target, send, recv, axis, peer):
        return pltpu.make_async_remote_copy(
            src_ref=source,
            dst_ref=target,
            send_sem=send,
            recv_sem=recv,
            device_id={axis: peer},
            device_id_type=MESH,
        )

    def every(count, copy):
        def begin(k, carry):
            copy(k).start()
            return carry

        def end(k, carry):
            copy(k).wait()
            return carry

        lax.fori_loop(1, count, begin, 0)
        return lambda: lax.fori_loop(1, count, end, 0)

    def head_copies(source, target, send, recv):
        def copy(k):
            peer = lax.rem(head_me + k, nh)
            return remote(source(peer), target, send.at[k], recv.at[k], "head", peer)

        return every(nh, copy)

    def z_copies(source, target, send, recv):
        def copy(k):
            z, peer = z_peer(k)
            return remote(source(z), target, send.at[k], recv.at[k], "seq", peer)

        return every(zs, copy)

    gathered = head_copies(
        lambda peer: all_ref.at[head_me], all_ref.at[head_me], gather_sems.at[0], gather_sems.at[1]
    )

    lower = iota((Q, Q), 0) >= iota((Q, Q), 1)
    upper = iota((Q, Q), 0) <= iota((Q, Q), 1)
    low_one = jnp.where(lower, 1.0, 0.0).astype(BF16)
    up_one = jnp.where(upper, 1.0, 0.0).astype(BF16)
    lane = iota((16, 512), 1)
    source = jnp.where(lane < 256, 8, 4) + (lane % 256) // 64
    spread = jnp.where(iota((16, 512), 0) == source, 1.0, 0.0).astype(BF16)
    pick8 = jnp.where(iota((8, 256), 0) == iota((8, 256), 1) // 64, 1.0, 0.0)


    def prepare(strand):
        def chunk(c):
            base = c * Q
            span = slice(base, base + Q)
            if strand == 0:
                s4 = all_ref[head_me, 0:4, span]
                d4 = all_ref[head_me, 4:8, span]
            else:
                heads = [heads_ref[head_me * 4 + h] for h in range(4)]
                s4 = jnp.concatenate([all_ref[i // 4, pl.ds(i % 4, 1), span] for i in heads], axis=0)
                d4 = jnp.concatenate([all_ref[i // 4, pl.ds(i % 4 + 4, 1), span] for i in heads], axis=0)
            s8 = jnp.concatenate([s4, s4], axis=0)
            d8 = jnp.concatenate([d4, d4], axis=0)
            cum8 = dot_sum(split3(d8), low_one if strand else up_one) * LOG2E
            total8 = cum8[:, 0:1] if strand else cum8[:, Q - 1 : Q]
            first = offset + base
            seg = segment_at(starts_ref, first + iota((8, Q), 1))
            seg_first, seg_last = segment_at(starts_ref, first), segment_at(starts_ref, first + Q - 1)
            if strand:
                seg_in, seg_far = segment_at(starts_ref, first + Q), seg_first
            else:
                seg_in = jnp.where(first == 0, -1, segment_at(starts_ref, first - 1))
                seg_far = seg_last
            e8 = jnp.where(seg == seg_in, jnp.exp2(cum8), 0.0)
            l8 = jnp.where(seg == seg_far, jnp.exp2(total8 - cum8) * s8, 0.0)
            gain8 = jnp.exp2(total8) * (seg_in == seg_far).astype(F32)
            gain = jnp.sum(pick8 * gain8, axis=0, keepdims=True)
            gain_ref[c, :, STRANDS[strand]] = jnp.broadcast_to(gain, (8, 256))
            rows = jnp.concatenate([cum8[0:4], e8[0:4], l8[0:4], s8[0:4]], axis=0)
            rows_ref[c, strand] = rows
            cols = rows.T
            cols_ref[strand, span, :] = cols
            wide = dot_sum(split3(cols), spread)
            lanes = STRANDS[strand]
            el_ref[span, lanes] = wide[:, 0:256]
            xhi, xlo = split2(x_ref[span, :].astype(F32) * wide[:, 0:256])
            ghi, glo = split2(g_ref[span, :].astype(F32) * wide[:, 256:512])
            hi_ref[0, span, lanes] = xhi
            lo_ref[0, span, lanes] = xlo
            hi_ref[1, span, lanes] = ghi
            lo_ref[1, span, lanes] = glo
            if strand == 0:
                bt_ref[c] = b_ref[span, :].T
                ct_ref[c] = c_ref[span, :].T
            bt, ct = bt_ref[c], ct_ref[c]
            terms_ref[1, c, :, lanes] = dot(bt, xhi) + dot(bt, xlo)
            terms_ref[0, c, :, lanes] = dot(ct, ghi) + dot(ct, glo)

        for c in range(chunks):
            chunk(c)


    ascending, descending = range(chunks), range(chunks - 1, -1, -1)
    way = (ascending, descending)

    def kind(strand, d):
        return d if strand else 1 - d

    def fold(strand):
        lanes = STRANDS[strand]
        for d in range(2):
            run = None
            for c in way[d]:
                term = terms_ref[kind(strand, d), c, :, lanes]
                run = term if run is None else run * gain_ref[c, 0:1, lanes] + term
            for k in range(2):
                pair_out[strand, d, k * 128 : (k + 1) * 128] = run[:, k * 128 : (k + 1) * 128]
        whole = gain_ref[0, :, lanes]
        for c in range(1, chunks):
            whole = whole * gain_ref[c, :, lanes]
        for d in range(2):
            for k in range(2):
                pair_out[strand, d, 256 + k * 8 : 264 + k * 8] = whole[:, k * 128 : (k + 1) * 128]


    half_mask = [jnp.where(iota((1, 128), 1) // 64 == k, 1.0, 0.0).astype(BF16) for k in range(2)]
    zero_row = jnp.zeros((8, 128), F32)
    part_rows = length // nh
    kept_sums = {}

    def inside(c, i):
        base = c * Q
        span = slice(base, base + Q)
        first = offset + base
        bc, cc = b_ref[span, :], c_ref[span, :]
        xs = [x_ref[span, k * 128 : (k + 1) * 128] for k in range(2)]
        gs = [g_ref[span, k * 128 : (k + 1) * 128] for k in range(2)]
        if i == 0:
            seg_s = segment_at(starts_ref, first + iota((Q, 1), 0))
            seg_t = segment_at(starts_ref, first + iota((1, Q), 1))
            gm[...] = jnp.where(seg_s == seg_t, dot_nt(bc, cc), 0.0)
            for h in range(4):
                pt[h] = dot_nt(xs[h // 2] * half_mask[h % 2], gs[h // 2])

        def strip(r, sums):
            start = pl.multiple_of(i * 128 + r * STRIP, STRIP)
            at = pl.ds(start, STRIP)
            at_cols = pl.ds(pl.multiple_of(base + start, STRIP), STRIP)
            col_f, col_m = cols_ref[0, at_cols, :], cols_ref[1, at_cols, :]
            lane128 = iota((STRIP, 128), 1)
            s_index = r * STRIP + iota((STRIP, 128), 0)
            ahead = lane128 > s_index
            behind = lane128 < s_index
            sums = list(sums)
            collected = jnp.zeros((STRIP, 128), F32)
            dg = [jnp.zeros((STRIP, 128), F32) for _ in range(2)]
            for h in range(4):
                cum_f, cum_m = col_f[:, h : h + 1], col_m[:, h : h + 1]
                step_f, step_m = col_f[:, 12 + h : 13 + h], col_m[:, 12 + h : 13 + h]
                lane_sums = [None, None]
                for j in range(2):
                    t = slice(j * 128, (j + 1) * 128)
                    row_f = rows_ref[c, 0, h : h + 1, t]
                    row_m = rows_ref[c, 1, h : h + 1, t]
                    if i == j:
                        gap = jnp.where(behind, row_m - cum_m, row_f - cum_f)
                        step = jnp.where(behind, step_m, jnp.where(ahead, step_f, step_f + step_m))
                    elif j > i:
                        gap, step = row_f - cum_f, step_f
                    else:
                        gap, step = row_m - cum_m, step_m
                    d = jnp.exp2(gap) * step
                    w = d * gm[at, t]
                    p = pt[h, at, t]
                    dg[j] = dg[j] + d * p
                    e = w * p
                    hi, lo = split2(w)
                    whi[h, at, t] = hi
                    wlo[h, at, t] = lo
                    if i == j:
                        parts = [jnp.where(ahead, e, 0.0), jnp.where(behind, e, 0.0)]
                    else:
                        parts = [e, None] if j > i else [None, e]
                    for strand in range(2):
                        piece = parts[strand]
                        if piece is None:
                            continue
                        slot = (h * 2 + j) * 2 + strand
                        add = piece[0:8]
                        for u in range(1, STRIP // 8):
                            add = add + piece[u * 8 : (u + 1) * 8]
                        sums[slot] = sums[slot] + add
                        old = lane_sums[strand]
                        lane_sums[strand] = piece if old is None else old + piece
                for strand in range(2):
                    total = jnp.sum(lane_sums[strand], axis=1, keepdims=True)
                    collected = jnp.where(lane128 == strand * 4 + h, total, collected)
            csum[at, :] = collected
            rows_at = segment_at(starts_ref, first + start + iota((STRIP, 1), 0))
            for j in range(2):
                t = slice(j * 128, (j + 1) * 128)
                cols_at = segment_at(starts_ref, first + j * 128 + iota((1, 128), 1))
                hi, lo = split2(jnp.where(rows_at == cols_at, dg[j], 0.0))
                dghi[at, t] = hi
                dglo[at, t] = lo
            return tuple(sums)

        kept_sums[i] = lax.fori_loop(0, 128 // STRIP, strip, (zero_row,) * 16)
        if i == 0:
            return
        row_sums = [kept_sums[0], kept_sums[1]]
        rows_in = []
        for strand in range(2):
            for h in range(4):
                lanes = []
                for j in range(2):
                    slot = (h * 2 + j) * 2 + strand
                    lanes.append(jnp.sum(row_sums[0][slot] + row_sums[1][slot], axis=0, keepdims=True))
                rows_in.append(jnp.concatenate(lanes, axis=1))
        row_keep[c] = jnp.concatenate(rows_in, axis=0)
        col_keep[c] = csum[...].T[0:8]
        for k in range(2):
            total = None
            for h in (2 * k, 2 * k + 1):
                masked = gs[k] * half_mask[h % 2]
                term = dot(whi[h], masked) + dot(wlo[h], masked)
                total = term if total is None else total + term
            dx_ref[span, k * 128 : (k + 1) * 128] = total
        part[0, span, :] = dot(dghi[...], cc) + dot(dglo[...], cc)
        dgt_hi, dgt_lo = dghi[...].T, dglo[...].T
        part[1, span, :] = dot(dgt_hi, bc) + dot(dgt_lo, bc)


    other = 1 - core
    slice_rows = 256 // zs
    half_slices = zs // 2
    waits = {}

    def gain_of(ref, k):
        return ref[256 + k * 8 : 257 + k * 8]

    def order(i):
        return i + core * (zs - 1 - 2 * i)

    def trade(strand):
        fold(strand)
        copy = remote(
            pair_out.at[strand, other],
            pair_in.at[strand],
            pair_sems.at[strand, 0],
            pair_sems.at[strand, 1],
            "seq",
            core_peer,
        )
        copy.start()
        waits["trade", strand] = copy.wait

    def spread_chip(strand):
        waits["trade", strand]()
        mine, theirs = pair_out.at[strand, core], pair_in.at[strand]
        for k in range(2):
            rows = slice(k * 128, (k + 1) * 128)
            slices = slice(k * half_slices, (k + 1) * half_slices)
            chip = gain_of(theirs, k) * mine[rows] + theirs[rows]
            slice_out[strand, slices, 0:slice_rows] = chip.reshape(half_slices, slice_rows, 128)
            gain = gain_of(theirs, k) * gain_of(mine, k)
            slice_out[strand, slices, slice_rows : slice_rows + 8] = jnp.broadcast_to(
                gain[None], (half_slices, 8, 128)
            )
        slice_in[strand, z_me] = slice_out[strand, z_me]
        waits["spread", strand] = z_copies(
            lambda z: slice_out.at[strand, z], slice_in.at[strand, z_me], z_sems.at[strand, 0], z_sems.at[strand, 1]
        )

    def scan_half(strand):
        waits["spread", strand]()
        run = jnp.zeros((slice_rows, 128), F32)
        for i in range(zs):
            z = order(i)
            scan_out[strand, z] = run
            run = slice_in[strand, z, slice_rows : slice_rows + 1] * run + slice_in[strand, z, 0:slice_rows]
        total_out[strand] = run
        copy = remote(
            total_out.at[strand],
            total_in.at[strand],
            pair_sems.at[strand, 2],
            pair_sems.at[strand, 3],
            "seq",
            x_peer,
        )
        copy.start()
        waits["swap", strand] = copy.wait

    def send_back(strand):
        waits["swap", strand]()
        run = total_in[strand] * jnp.where(x_me == 1 - core, 1.0, 0.0)
        for i in range(zs):
            z = order(i)
            scan_out[strand, z] = scan_out[strand, z] + run
            run = slice_in[strand, z, slice_rows : slice_rows + 1] * run
        back_in[strand, z_me] = scan_out[strand, z_me]
        waits["back", strand] = z_copies(
            lambda z: scan_out.at[strand, z], back_in.at[strand, z_me], z_sems.at[strand, 2], z_sems.at[strand, 3]
        )

    def pass_on(strand):
        waits["back", strand]()
        mine = pair_out.at[strand, core]
        for k in range(2):
            rows = slice(k * 128, (k + 1) * 128)
            enter = back_in[strand, k * half_slices : (k + 1) * half_slices].reshape(128, 128)
            entering[strand, core, rows] = enter
            next_out[strand, rows] = gain_of(mine, k) * enter + mine[rows]
        copy = remote(
            next_out.at[strand],
            entering.at[strand, core],
            pair_sems.at[strand, 4],
            pair_sems.at[strand, 5],
            "seq",
            core_peer,
        )
        copy.start()
        waits["pass", strand] = copy.wait

    def enter_chunks(strand, d):
        lanes = STRANDS[strand]
        w = kind(strand, d)
        run = jnp.concatenate([entering[strand, d, k * 128 : (k + 1) * 128] for k in range(2)], axis=1)
        for i in range(chunks):
            c = i + d * (chunks - 1 - 2 * i)
            meet[w, c, :, lanes] = run
            run = run * gain_ref[c, 0:1, lanes] + terms_ref[w, c, :, lanes]
        meet[w, chunks, :, lanes] = run

    def cross(strand, w):
        lanes = STRANDS[strand]
        for c in range(chunks):
            span = slice(c * Q, (c + 1) * Q)
            m_hi, m_lo = split2(meet[w, c, :, lanes])
            hi, lo = hi_ref[w, span, lanes], lo_ref[w, span, lanes]
            part[w, span, :] = part[w, span, :] + (dot_nt(hi, m_hi) + dot_nt(lo, m_hi) + dot_nt(hi, m_lo))

    def share(w, n):
        return head_copies(
            lambda peer: part.at[w, pl.ds(peer * part_rows, part_rows)],
            got.at[w, head_me],
            head_sems.at[0, n],
            head_sems.at[1, n],
        )

    for load in loads:
        load.wait()
    prepare(0)
    trade(0)
    gathered()
    spread_chip(0)
    prepare(1)
    trade(1)
    scan_half(0)
    inside(0, 0)
    spread_chip(1)
    inside(0, 1)
    inside(1, 0)
    inside(1, 1)
    scan_half(1)
    send_back(0)
    inside(2, 0)
    inside(2, 1)
    send_back(1)
    inside(3, 0)
    pass_on(0)
    inside(3, 1)
    waits["pass", 0]()
    for d in range(2):
        enter_chunks(0, d)
        cross(0, kind(0, d))
    pass_on(1)
    enter_chunks(1, core)
    cross(1, core)
    sent = [share(core, 0)]

    pick = jnp.where(iota((8, 512), 0) == iota((8, 512), 1) // 64, 1.0, 0.0)
    pick_bf = pick.astype(BF16)
    pick2_bf = jnp.where(iota((8, 256), 0) % 4 == iota((8, 256), 1) // 64, 1.0, 0.0).astype(BF16)
    ones_bf = jnp.ones((8, 128), BF16)

    def same_place(c, carry):
        span = pl.ds(pl.multiple_of(c * Q, Q), Q)
        bc_prod = split2(b_ref[span, :].astype(F32) * c_ref[span, :].astype(F32))
        score8 = dot_nt(ones_bf, bc_prod[0]) + dot_nt(ones_bf, bc_prod[1])
        xg = split2(x_ref[span, :].astype(F32) * g_ref[span, :].astype(F32))
        pair8 = dot_nt(pick2_bf, xg[0]) + dot_nt(pick2_bf, xg[1])
        other_ref[:, span] = score8 * pair8
        return carry

    lax.fori_loop(0, chunks, same_place, 0)
    waits["pass", 1]()
    enter_chunks(1, other)
    cross(1, other)
    sent.append(share(other, 1))

    def across(c, carry):
        span = pl.ds(pl.multiple_of(c * Q, Q), Q)
        state_hi, state_lo = split2(meet[1, c])
        adj_hi, adj_lo = split2(meet[0, c])
        bc, cc = b_ref[span, :], c_ref[span, :]
        v = dot(bc, adj_hi) + dot(bc, adj_lo)
        y = dot(cc, state_hi) + dot(cc, state_lo)
        scaled = el_ref[span, :] * v
        dx_ref[span, :] = dx_ref[span, :] + scaled[:, FRONT] + scaled[:, MIRROR]
        x_prod = split2((hi_ref[0, span, :].astype(F32) + lo_ref[0, span, :].astype(F32)) * v)
        g_prod = split2((hi_ref[1, span, :].astype(F32) + lo_ref[1, span, :].astype(F32)) * y)
        col8 = col_keep[c] + dot_nt(pick_bf, x_prod[0]) + dot_nt(pick_bf, x_prod[1])
        row8 = row_keep[c] + dot_nt(pick_bf, g_prod[0]) + dot_nt(pick_bf, g_prod[1])
        s8 = jnp.concatenate([rows_ref[c, 0, 12:16, :], rows_ref[c, 1, 12:16, :]], axis=0)
        step8 = col8 / s8 + other_ref[:, span]
        flow_f = jnp.sum(meet[1, c + 1, :, FRONT] * meet[0, c, :, FRONT], axis=0, keepdims=True)
        under = lax.rem(c + chunks, chunks + 1)
        flow_m = jnp.sum(meet[1, under, :, MIRROR] * meet[0, c, :, MIRROR], axis=0, keepdims=True)
        flow8 = jnp.sum(pick * jnp.concatenate([flow_f, flow_m], axis=1), axis=1, keepdims=True)
        diff = split3(row8 - col8)
        front8 = iota((8, Q), 0) < 4
        decay8 = jnp.where(front8, dot_sum(diff, low_one), dot_sum(diff, up_one)) + flow8
        own_ref[0:4, span] = step8[0:4]
        own_ref[4:8, span] = decay8[0:4]
        other_ref[0:4, span] = step8[4:8]
        other_ref[4:8, span] = decay8[4:8]
        return carry

    own_rows = pl.ds(head_me * part_rows, part_rows)

    def add_up(w, n):
        sent[n]()
        total = part[w, own_rows, :]
        for k in range(1, nh):
            total = total + got[w, lax.rem(head_me + k, nh)]
        sums_ref[w] = total
        own = pltpu.make_async_copy(sums_ref.at[w], sums_hbm.at[w, own_rows], local_sems.at[5 + n])
        own.start()
        stores.append(own)
        return head_copies(
            lambda peer: sums_ref.at[w], sums_hbm.at[w, own_rows], head_sems.at[2, n], head_sems.at[3, n]
        )

    lax.fori_loop(0, chunks, across, 0)
    stores = [pltpu.make_async_copy(dx_ref, dx_hbm, local_sems.at[4])]
    stores[0].start()
    ny = nh // 2
    y_me, side = lax.rem(head_me, ny), head_me // ny
    x_head = lax.rem(head_me + ny, nh)
    others[y_me] = other_ref[...]

    def y_copy(k):
        peer = side * ny + lax.rem(y_me + k, ny)
        return remote(other_ref, others.at[y_me], other_sems.at[0, k], other_sems.at[1, k], "head", peer)

    shared = every(ny, y_copy)

    def find(head):
        place = 0 * head
        for k in range(nh * 4):
            place = jnp.where(heads_ref[k] == head, k, place)
        return place

    def row_of(place, row):
        return others[lax.rem(place // 4, ny), pl.ds(lax.rem(place, 4) + row, 1), :]

    ended = [add_up(core, 0)]
    shared()
    for h in range(4):
        place = find(x_head * 4 + h)
        far_out[h : h + 1, :] = row_of(place, 0)
        far_out[4 + h : 5 + h, :] = row_of(place, 4)
    far = remote(far_out, far_in, other_sems.at[0, 0], other_sems.at[1, 0], "head", x_head)
    far.start()
    ended.append(add_up(other, 1))
    far.wait()
    for h in range(4):
        place = find(head_me * 4 + h)
        near = place // (4 * ny) == side
        for row, target in ((0, dstep_ref), (4, ddecay_ref)):
            back = jnp.where(near, row_of(place, row), far_in[row + h : row + h + 1, :])
            target[h : h + 1, :] = own_ref[row + h : row + h + 1, :] + back
    for wait in ended:
        wait()
    for store in stores:
        store.wait()


def hand_on(dx_ref, sums_ref, step_ref, decay_ref, dx_out, db_out, dc_out, step_out, decay_out, dx, sums, step, decay, sems):
    pieces = []
    for c in range(dx_ref.shape[0] // Q):
        rows = slice(c * Q, (c + 1) * Q)
        for w, out in enumerate((db_out, dc_out)):
            pieces.append((sums_ref.at[w, rows], sums.at[w, rows], out.at[rows]))
        pieces.append((dx_ref.at[rows], dx.at[rows], dx_out.at[rows]))
    pieces.append((step_ref, step, step_out))
    pieces.append((decay_ref, decay, decay_out))
    loads = [pltpu.make_async_copy(a, b, sems.at[0, i]) for i, (a, b, _) in enumerate(pieces)]
    for load in loads:
        load.start()
    stores = []
    for i, (_, a, b) in enumerate(pieces):
        loads[i].wait()
        stores.append(pltpu.make_async_copy(a, b, sems.at[1, i]))
        stores[-1].start()
    for store in stores:
        store.wait()


def on_device(signal, write_keys, read_queries, step_sizes, log_decay, mirror_heads, contig_starts, out_grad):
    nh, ns = lax.axis_size("head"), lax.axis_size("seq")
    length = signal.shape[0]
    chunks = length // Q
    zs = ns // 4
    slice_rows = 256 // zs
    part_rows = length // nh
    vmem = pl.BlockSpec(memory_space=pltpu.VMEM)
    smem = pl.BlockSpec(memory_space=pltpu.SMEM)
    hbm = pl.BlockSpec(memory_space=pl.ANY)

    def shape(*dims, dtype=F32):
        return jax.ShapeDtypeStruct(dims, dtype)

    def room(*dims, dtype=F32):
        return pltpu.VMEM(dims, dtype)

    dx, sums, dstep, ddecay = pl.pallas_call(
        functools.partial(kernel, nh, ns),
        out_shape=[shape(length, 256), shape(2, length, 128), shape(4, length), shape(4, length)],
        in_specs=[smem] * 2 + [hbm] * 4 + [vmem] * 2,
        out_specs=[hbm] * 2 + [vmem] * 2,
        scratch_shapes=[
            room(length, 256, dtype=BF16),
            room(length, 256, dtype=BF16),
            room(length, 128, dtype=BF16),
            room(length, 128, dtype=BF16),
            room(chunks, 128, Q, dtype=BF16),
            room(chunks, 128, Q, dtype=BF16),
            room(length, 256),
            room(2, part_rows, 128),
            pltpu.SemaphoreType.DMA((7,)),
            room(nh, 8, length),
            room(chunks, 2, 16, Q),
            room(2, length, 16),
            room(2, length, 512, dtype=BF16),
            room(2, length, 512, dtype=BF16),
            room(length, 512),
            room(2, chunks, 128, 512),
            room(chunks, 8, 512),
            room(2, 2, 272, 128),
            room(2, 272, 128),
            room(2, zs, slice_rows + 8, 128),
            room(2, zs, slice_rows + 8, 128),
            room(2, zs, slice_rows, 128),
            room(2, slice_rows, 128),
            room(2, slice_rows, 128),
            room(2, zs, slice_rows, 128),
            room(2, 256, 128),
            room(2, 2, 256, 128),
            room(2, chunks + 1, 128, 512),
            room(Q, Q),
            room(4, Q, Q),
            room(4, Q, Q, dtype=BF16),
            room(4, Q, Q, dtype=BF16),
            room(Q, Q, dtype=BF16),
            room(Q, Q, dtype=BF16),
            room(Q, 128),
            room(chunks, 8, Q),
            room(chunks, 8, Q),
            room(2, length, 128),
            room(2, nh, part_rows, 128),
            room(8, length),
            room(8, length),
            room(nh // 2, 8, length),
            room(8, length),
            room(8, length),
            pltpu.SemaphoreType.DMA((2, nh)),
            pltpu.SemaphoreType.DMA((2, 6)),
            pltpu.SemaphoreType.DMA((2, 4, zs)),
            pltpu.SemaphoreType.DMA((4, 2, nh)),
            pltpu.SemaphoreType.DMA((2, nh)),
        ],
        compiler_params=pltpu.CompilerParams(
            vmem_limit_bytes=VMEM_LIMIT, collective_id=0, has_side_effects=True
        ),
        name="mixer_backward",
    )(mirror_heads, contig_starts, signal, out_grad, write_keys, read_queries, step_sizes, log_decay)

    return pl.pallas_call(
        hand_on,
        out_shape=[shape(length, 256), shape(length, 128), shape(length, 128), shape(4, length), shape(4, length)],
        in_specs=[hbm] * 4,
        out_specs=[hbm] * 5,
        scratch_shapes=[
            room(length, 256),
            room(2, length, 128),
            room(4, length),
            room(4, length),
            pltpu.SemaphoreType.DMA((2, 3 * chunks + 2)),
        ],
        compiler_params=pltpu.CompilerParams(vmem_limit_bytes=VMEM_LIMIT),
        name="hand_on",
    )(dx, sums, dstep, ddecay)


def solution(mesh):
    return jax.shard_map(
        on_device,
        mesh=mesh,
        in_specs=(
            P("seq", "head"),
            P("seq", None),
            P("seq", None),
            P("head", "seq"),
            P("head", "seq"),
            P(),
            P(),
            P("seq", "head"),
        ),
        out_specs=(
            P("seq", "head"),
            P("seq", None),
            P("seq", None),
            P("head", "seq"),
            P("head", "seq"),
        ),
        check_vma=False,
    )
```

```python
import functools

import jax
import jax.numpy as jnp
from jax import lax
from jax.experimental import pallas as pl
from jax.experimental.pallas import tpu as pltpu
from jax.sharding import PartitionSpec as P

Q = 256
STRIP = 32
LOG2E = 1.4426950408889634
F32, BF16 = jnp.float32, jnp.bfloat16
MESH = pl.DeviceIdType.MESH
VMEM_LIMIT = 56 * 1024 * 1024


def iota(shape, dim):
    return lax.broadcasted_iota(jnp.int32, shape, dim)


def split2(v):
    hi = v.astype(BF16)
    return hi, (v - hi.astype(F32)).astype(BF16)


def split3(v):
    hi = v.astype(BF16)
    rest = v - hi.astype(F32)
    mid = rest.astype(BF16)
    return hi, mid, (rest - mid.astype(F32)).astype(BF16)


def dot(a, b):
    return lax.dot_general(a, b, (((1,), (0,)), ((), ())), preferred_element_type=F32)


def dot_nt(a, b):
    return lax.dot_general(a, b, (((1,), (1,)), ((), ())), preferred_element_type=F32)


def dot_sum(parts, b, how=dot):
    total = how(parts[0], b)
    for part in parts[1:]:
        total = total + how(part, b)
    return total


def segment_at(starts_ref, t):
    total = (starts_ref[0] <= t).astype(jnp.int32)
    for k in range(1, 4):
        total = total + (starts_ref[k] <= t).astype(jnp.int32)
    return total


FRONT, MIRROR = slice(0, 256), slice(256, 512)
STRANDS = (FRONT, MIRROR)


def kernel(
    nh,
    ns,
    heads_ref,
    starts_ref,
    x_hbm,
    g_hbm,
    b_hbm,
    c_hbm,
    step_ref,
    decay_ref,
    dx_hbm,
    sums_hbm,
    dstep_ref,
    ddecay_ref,
    x_ref,
    g_ref,
    b_ref,
    c_ref,
    bt_ref,
    ct_ref,
    dx_ref,
    sums_ref,
    local_sems,
    all_ref,
    rows_ref,
    cols_ref,
    hi_ref,
    lo_ref,
    el_ref,
    terms_ref,
    gain_ref,
    pair_out,
    pair_in,
    slice_out,
    slice_in,
    scan_out,
    total_out,
    total_in,
    back_in,
    next_out,
    entering,
    meet,
    gm,
    pt,
    whi,
    wlo,
    dghi,
    dglo,
    csum,
    row_keep,
    col_keep,
    part,
    got,
    own_ref,
    other_ref,
    others,
    far_out,
    far_in,
    gather_sems,
    pair_sems,
    z_sems,
    head_sems,
    other_sems,
):
    length = x_ref.shape[0]
    chunks = length // Q
    head_me = lax.axis_index("head")
    seq_me = lax.axis_index("seq")
    offset = seq_me * length
    core = lax.rem(seq_me, 2)
    zs = ns // 4
    z_me = lax.rem(seq_me // 2, zs)
    x_me = seq_me // (2 * zs)
    core_peer = seq_me + 1 - 2 * core
    x_peer = lax.rem(seq_me + ns // 2, ns)

    def z_peer(k):
        z = lax.rem(z_me + k, zs)
        return z, x_me * 2 * zs + z * 2 + core

    loads = [
        pltpu.make_async_copy(a, b, local_sems.at[i])
        for i, (a, b) in enumerate(((x_hbm, x_ref), (g_hbm, g_ref), (b_hbm, b_ref), (c_hbm, c_ref)))
    ]
    for load in loads:
        load.start()

    all_ref[head_me, 0:4, :] = step_ref[...]
    all_ref[head_me, 4:8, :] = decay_ref[...]
    barrier = pltpu.get_barrier_semaphore()

    def greet_head(k, carry):
        peer = lax.rem(head_me + k, nh)
        pl.semaphore_signal(barrier, inc=1, device_id={"head": peer}, device_id_type=MESH)
        return carry

    def greet_z(k, carry):
        pl.semaphore_signal(barrier, inc=1, device_id={"seq": z_peer(k)[1]}, device_id_type=MESH)
        return carry

    lax.fori_loop(1, nh, greet_head, 0)
    lax.fori_loop(1, zs, greet_z, 0)
    pl.semaphore_signal(barrier, inc=1, device_id={"seq": core_peer}, device_id_type=MESH)
    pl.semaphore_signal(barrier, inc=1, device_id={"seq": x_peer}, device_id_type=MESH)
    pl.semaphore_wait(barrier, nh + zs)

    def remote(source, target, send, recv, axis, peer):
        return pltpu.make_async_remote_copy(
            src_ref=source,
            dst_ref=target,
            send_sem=send,
            recv_sem=recv,
            device_id={axis: peer},
            device_id_type=MESH,
        )

    def every(count, copy):
        def begin(k, carry):
            copy(k).start()
            return carry

        def end(k, carry):
            copy(k).wait()
            return carry

        lax.fori_loop(1, count, begin, 0)
        return lambda: lax.fori_loop(1, count, end, 0)

    def head_copies(source, target, send, recv):
        def copy(k):
            peer = lax.rem(head_me + k, nh)
            return remote(source(peer), target, send.at[k], recv.at[k], "head", peer)

        return every(nh, copy)

    def z_copies(source, target, send, recv):
        def copy(k):
            step = (k // 2) * (2 * lax.rem(k, 2) - 1)
            z, peer = z_peer(zs // 2 + step)
            return remote(source(z), target, send.at[k], recv.at[k], "seq", peer)

        return every(zs, copy)

    gathered = head_copies(
        lambda peer: all_ref.at[head_me], all_ref.at[head_me], gather_sems.at[0], gather_sems.at[1]
    )

    lower = iota((Q, Q), 0) >= iota((Q, Q), 1)
    upper = iota((Q, Q), 0) <= iota((Q, Q), 1)
    low_one = jnp.where(lower, 1.0, 0.0).astype(BF16)
    up_one = jnp.where(upper, 1.0, 0.0).astype(BF16)
    lane = iota((16, 512), 1)
    source = jnp.where(lane < 256, 8, 4) + (lane % 256) // 64
    spread = jnp.where(iota((16, 512), 0) == source, 1.0, 0.0).astype(BF16)
    pick8 = jnp.where(iota((8, 256), 0) == iota((8, 256), 1) // 64, 1.0, 0.0)


    def prepare(strand):
        def chunk(c):
            base = c * Q
            span = slice(base, base + Q)
            if strand == 0:
                s4 = all_ref[head_me, 0:4, span]
                d4 = all_ref[head_me, 4:8, span]
            else:
                heads = [heads_ref[head_me * 4 + h] for h in range(4)]
                s4 = jnp.concatenate([all_ref[i // 4, pl.ds(i % 4, 1), span] for i in heads], axis=0)
                d4 = jnp.concatenate([all_ref[i // 4, pl.ds(i % 4 + 4, 1), span] for i in heads], axis=0)
            s8 = jnp.concatenate([s4, s4], axis=0)
            d8 = jnp.concatenate([d4, d4], axis=0)
            cum8 = dot_sum(split3(d8), low_one if strand else up_one) * LOG2E
            total8 = cum8[:, 0:1] if strand else cum8[:, Q - 1 : Q]
            first = offset + base
            seg = segment_at(starts_ref, first + iota((8, Q), 1))
            seg_first, seg_last = segment_at(starts_ref, first), segment_at(starts_ref, first + Q - 1)
            if strand:
                seg_in, seg_far = segment_at(starts_ref, first + Q), seg_first
            else:
                seg_in = jnp.where(first == 0, -1, segment_at(starts_ref, first - 1))
                seg_far = seg_last
            e8 = jnp.where(seg == seg_in, jnp.exp2(cum8), 0.0)
            l8 = jnp.where(seg == seg_far, jnp.exp2(total8 - cum8) * s8, 0.0)
            gain8 = jnp.exp2(total8) * (seg_in == seg_far).astype(F32)
            gain = jnp.sum(pick8 * gain8, axis=0, keepdims=True)
            gain_ref[c, :, STRANDS[strand]] = jnp.broadcast_to(gain, (8, 256))
            rows = jnp.concatenate([cum8[0:4], e8[0:4], l8[0:4], s8[0:4]], axis=0)
            rows_ref[c, strand] = rows
            cols = rows.T
            cols_ref[strand, span, :] = cols
            wide = dot_sum(split3(cols), spread)
            lanes = STRANDS[strand]
            el_ref[span, lanes] = wide[:, 0:256]
            xhi, xlo = split2(x_ref[span, :].astype(F32) * wide[:, 0:256])
            ghi, glo = split2(g_ref[span, :].astype(F32) * wide[:, 256:512])
            hi_ref[0, span, lanes] = xhi
            lo_ref[0, span, lanes] = xlo
            hi_ref[1, span, lanes] = ghi
            lo_ref[1, span, lanes] = glo
            if strand == 0:
                bt_ref[c] = b_ref[span, :].T
                ct_ref[c] = c_ref[span, :].T
            bt, ct = bt_ref[c], ct_ref[c]
            terms_ref[1, c, :, lanes] = dot(bt, xhi) + dot(bt, xlo)
            terms_ref[0, c, :, lanes] = dot(ct, ghi) + dot(ct, glo)

        for c in range(chunks):
            chunk(c)


    ascending, descending = range(chunks), range(chunks - 1, -1, -1)
    way = (ascending, descending)

    def kind(strand, d):
        return d if strand else 1 - d

    def fold(strand):
        lanes = STRANDS[strand]
        for d in range(2):
            run = None
            for c in way[d]:
                term = terms_ref[kind(strand, d), c, :, lanes]
                run = term if run is None else run * gain_ref[c, 0:1, lanes] + term
            for k in range(2):
                pair_out[strand, d, k * 128 : (k + 1) * 128] = run[:, k * 128 : (k + 1) * 128]
        whole = gain_ref[0, :, lanes]
        for c in range(1, chunks):
            whole = whole * gain_ref[c, :, lanes]
        for d in range(2):
            for k in range(2):
                pair_out[strand, d, 256 + k * 8 : 264 + k * 8] = whole[:, k * 128 : (k + 1) * 128]


    half_mask = [jnp.where(iota((1, 128), 1) // 64 == k, 1.0, 0.0).astype(BF16) for k in range(2)]
    zero_row = jnp.zeros((8, 128), F32)
    part_rows = length // nh
    kept_sums = {}

    def inside(c, i):
        base = c * Q
        span = slice(base, base + Q)
        first = offset + base
        bc, cc = b_ref[span, :], c_ref[span, :]
        xs = [x_ref[span, k * 128 : (k + 1) * 128] for k in range(2)]
        gs = [g_ref[span, k * 128 : (k + 1) * 128] for k in range(2)]
        if i == 0:
            seg_s = segment_at(starts_ref, first + iota((Q, 1), 0))
            seg_t = segment_at(starts_ref, first + iota((1, Q), 1))
            gm[...] = jnp.where(seg_s == seg_t, dot_nt(bc, cc), 0.0)
            for h in range(4):
                pt[h] = dot_nt(xs[h // 2] * half_mask[h % 2], gs[h // 2])

        def strip(r, sums):
            start = pl.multiple_of(i * 128 + r * STRIP, STRIP)
            at = pl.ds(start, STRIP)
            at_cols = pl.ds(pl.multiple_of(base + start, STRIP), STRIP)
            col_f, col_m = cols_ref[0, at_cols, :], cols_ref[1, at_cols, :]
            lane128 = iota((STRIP, 128), 1)
            s_index = r * STRIP + iota((STRIP, 128), 0)
            ahead = lane128 > s_index
            behind = lane128 < s_index
            sums = list(sums)
            collected = jnp.zeros((STRIP, 128), F32)
            dg = [jnp.zeros((STRIP, 128), F32) for _ in range(2)]
            for h in range(4):
                cum_f, cum_m = col_f[:, h : h + 1], col_m[:, h : h + 1]
                step_f, step_m = col_f[:, 12 + h : 13 + h], col_m[:, 12 + h : 13 + h]
                lane_sums = [None, None]
                for j in range(2):
                    t = slice(j * 128, (j + 1) * 128)
                    row_f = rows_ref[c, 0, h : h + 1, t]
                    row_m = rows_ref[c, 1, h : h + 1, t]
                    if i == j:
                        gap = jnp.where(behind, row_m - cum_m, row_f - cum_f)
                        step = jnp.where(behind, step_m, jnp.where(ahead, step_f, step_f + step_m))
                    elif j > i:
                        gap, step = row_f - cum_f, step_f
                    else:
                        gap, step = row_m - cum_m, step_m
                    d = jnp.exp2(gap) * step
                    w = d * gm[at, t]
                    p = pt[h, at, t]
                    dg[j] = dg[j] + d * p
                    e = w * p
                    hi, lo = split2(w)
                    whi[h, at, t] = hi
                    wlo[h, at, t] = lo
                    if i == j:
                        parts = [jnp.where(ahead, e, 0.0), jnp.where(behind, e, 0.0)]
                    else:
                        parts = [e, None] if j > i else [None, e]
                    for strand in range(2):
                        piece = parts[strand]
                        if piece is None:
                            continue
                        slot = (h * 2 + j) * 2 + strand
                        add = piece[0:8]
                        for u in range(1, STRIP // 8):
                            add = add + piece[u * 8 : (u + 1) * 8]
                        sums[slot] = sums[slot] + add
                        old = lane_sums[strand]
                        lane_sums[strand] = piece if old is None else old + piece
                for strand in range(2):
                    total = jnp.sum(lane_sums[strand], axis=1, keepdims=True)
                    collected = jnp.where(lane128 == strand * 4 + h, total, collected)
            csum[at, :] = collected
            rows_at = segment_at(starts_ref, first + start + iota((STRIP, 1), 0))
            for j in range(2):
                t = slice(j * 128, (j + 1) * 128)
                cols_at = segment_at(starts_ref, first + j * 128 + iota((1, 128), 1))
                hi, lo = split2(jnp.where(rows_at == cols_at, dg[j], 0.0))
                dghi[at, t] = hi
                dglo[at, t] = lo
            return tuple(sums)

        kept_sums[i] = lax.fori_loop(0, 128 // STRIP, strip, (zero_row,) * 16)
        if i == 0:
            return
        row_sums = [kept_sums[0], kept_sums[1]]
        rows_in = []
        for strand in range(2):
            for h in range(4):
                lanes = []
                for j in range(2):
                    slot = (h * 2 + j) * 2 + strand
                    lanes.append(jnp.sum(row_sums[0][slot] + row_sums[1][slot], axis=0, keepdims=True))
                rows_in.append(jnp.concatenate(lanes, axis=1))
        row_keep[c] = jnp.concatenate(rows_in, axis=0)
        col_keep[c] = csum[...].T[0:8]
        for k in range(2):
            total = None
            for h in (2 * k, 2 * k + 1):
                masked = gs[k] * half_mask[h % 2]
                term = dot(whi[h], masked) + dot(wlo[h], masked)
                total = term if total is None else total + term
            dx_ref[span, k * 128 : (k + 1) * 128] = total
        part[0, span, :] = dot(dghi[...], cc) + dot(dglo[...], cc)
        dgt_hi, dgt_lo = dghi[...].T, dglo[...].T
        part[1, span, :] = dot(dgt_hi, bc) + dot(dgt_lo, bc)


    other = 1 - core
    slice_rows = 256 // zs
    half_slices = zs // 2
    waits = {}

    def gain_of(ref, k):
        return ref[256 + k * 8 : 257 + k * 8]

    def order(i):
        return i + core * (zs - 1 - 2 * i)

    def trade(strand):
        fold(strand)
        copy = remote(
            pair_out.at[strand, other],
            pair_in.at[strand],
            pair_sems.at[strand, 0],
            pair_sems.at[strand, 1],
            "seq",
            core_peer,
        )
        copy.start()
        waits["trade", strand] = copy.wait

    def spread_chip(strand):
        waits["trade", strand]()
        mine, theirs = pair_out.at[strand, core], pair_in.at[strand]
        for k in range(2):
            rows = slice(k * 128, (k + 1) * 128)
            slices = slice(k * half_slices, (k + 1) * half_slices)
            chip = gain_of(theirs, k) * mine[rows] + theirs[rows]
            slice_out[strand, slices, 0:slice_rows] = chip.reshape(half_slices, slice_rows, 128)
            gain = gain_of(theirs, k) * gain_of(mine, k)
            slice_out[strand, slices, slice_rows : slice_rows + 8] = jnp.broadcast_to(
                gain[None], (half_slices, 8, 128)
            )
        slice_in[strand, z_me] = slice_out[strand, z_me]
        waits["spread", strand] = z_copies(
            lambda z: slice_out.at[strand, z], slice_in.at[strand, z_me], z_sems.at[strand, 0], z_sems.at[strand, 1]
        )

    def scan_half(strand):
        waits["spread", strand]()
        run = jnp.zeros((slice_rows, 128), F32)
        for i in range(zs):
            z = order(i)
            scan_out[strand, z] = run
            run = slice_in[strand, z, slice_rows : slice_rows + 1] * run + slice_in[strand, z, 0:slice_rows]
        total_out[strand] = run
        copy = remote(
            total_out.at[strand],
            total_in.at[strand],
            pair_sems.at[strand, 2],
            pair_sems.at[strand, 3],
            "seq",
            x_peer,
        )
        copy.start()
        waits["swap", strand] = copy.wait

    def send_back(strand):
        waits["swap", strand]()
        run = total_in[strand] * jnp.where(x_me == 1 - core, 1.0, 0.0)
        for i in range(zs):
            z = order(i)
            scan_out[strand, z] = scan_out[strand, z] + run
            run = slice_in[strand, z, slice_rows : slice_rows + 1] * run
        back_in[strand, z_me] = scan_out[strand, z_me]
        waits["back", strand] = z_copies(
            lambda z: scan_out.at[strand, z], back_in.at[strand, z_me], z_sems.at[strand, 2], z_sems.at[strand, 3]
        )

    def pass_on(strand):
        waits["back", strand]()
        mine = pair_out.at[strand, core]
        for k in range(2):
            rows = slice(k * 128, (k + 1) * 128)
            enter = back_in[strand, k * half_slices : (k + 1) * half_slices].reshape(128, 128)
            entering[strand, core, rows] = enter
            next_out[strand, rows] = gain_of(mine, k) * enter + mine[rows]
        copy = remote(
            next_out.at[strand],
            entering.at[strand, core],
            pair_sems.at[strand, 4],
            pair_sems.at[strand, 5],
            "seq",
            core_peer,
        )
        copy.start()
        waits["pass", strand] = copy.wait

    def enter_chunks(strand, d):
        lanes = STRANDS[strand]
        w = kind(strand, d)
        run = jnp.concatenate([entering[strand, d, k * 128 : (k + 1) * 128] for k in range(2)], axis=1)
        for i in range(chunks):
            c = i + d * (chunks - 1 - 2 * i)
            meet[w, c, :, lanes] = run
            run = run * gain_ref[c, 0:1, lanes] + terms_ref[w, c, :, lanes]
        meet[w, chunks, :, lanes] = run

    def cross(strand, w):
        lanes = STRANDS[strand]
        for c in range(chunks):
            span = slice(c * Q, (c + 1) * Q)
            m_hi, m_lo = split2(meet[w, c, :, lanes])
            hi, lo = hi_ref[w, span, lanes], lo_ref[w, span, lanes]
            part[w, span, :] = part[w, span, :] + (dot_nt(hi, m_hi) + dot_nt(lo, m_hi) + dot_nt(hi, m_lo))

    def share(w, n):
        return head_copies(
            lambda peer: part.at[w, pl.ds(peer * part_rows, part_rows)],
            got.at[w, head_me],
            head_sems.at[0, n],
            head_sems.at[1, n],
        )

    for load in loads:
        load.wait()
    prepare(0)
    trade(0)
    gathered()
    spread_chip(0)
    prepare(1)
    trade(1)
    scan_half(0)
    inside(0, 0)
    spread_chip(1)
    inside(0, 1)
    inside(1, 0)
    inside(1, 1)
    scan_half(1)
    send_back(0)
    inside(2, 0)
    inside(2, 1)
    send_back(1)
    inside(3, 0)
    pass_on(0)
    inside(3, 1)
    waits["pass", 0]()
    for d in range(2):
        enter_chunks(0, d)
        cross(0, kind(0, d))
    pass_on(1)
    enter_chunks(1, core)
    cross(1, core)
    sent = [share(core, 0)]

    pick = jnp.where(iota((8, 512), 0) == iota((8, 512), 1) // 64, 1.0, 0.0)
    pick_bf = pick.astype(BF16)
    pick2_bf = jnp.where(iota((8, 256), 0) % 4 == iota((8, 256), 1) // 64, 1.0, 0.0).astype(BF16)
    ones_bf = jnp.ones((8, 128), BF16)

    def same_place(c, carry):
        span = pl.ds(pl.multiple_of(c * Q, Q), Q)
        bc_prod = split2(b_ref[span, :].astype(F32) * c_ref[span, :].astype(F32))
        score8 = dot_nt(ones_bf, bc_prod[0]) + dot_nt(ones_bf, bc_prod[1])
        xg = split2(x_ref[span, :].astype(F32) * g_ref[span, :].astype(F32))
        pair8 = dot_nt(pick2_bf, xg[0]) + dot_nt(pick2_bf, xg[1])
        other_ref[:, span] = score8 * pair8
        return carry

    lax.fori_loop(0, chunks, same_place, 0)
    waits["pass", 1]()
    enter_chunks(1, other)
    cross(1, other)
    sent.append(share(other, 1))

    def across(c, carry):
        span = pl.ds(pl.multiple_of(c * Q, Q), Q)
        state_hi, state_lo = split2(meet[1, c])
        adj_hi, adj_lo = split2(meet[0, c])
        bc, cc = b_ref[span, :], c_ref[span, :]
        v = dot(bc, adj_hi) + dot(bc, adj_lo)
        y = dot(cc, state_hi) + dot(cc, state_lo)
        scaled = el_ref[span, :] * v
        dx_ref[span, :] = dx_ref[span, :] + scaled[:, FRONT] + scaled[:, MIRROR]
        x_prod = split2((hi_ref[0, span, :].astype(F32) + lo_ref[0, span, :].astype(F32)) * v)
        g_prod = split2((hi_ref[1, span, :].astype(F32) + lo_ref[1, span, :].astype(F32)) * y)
        col8 = col_keep[c] + dot_nt(pick_bf, x_prod[0]) + dot_nt(pick_bf, x_prod[1])
        row8 = row_keep[c] + dot_nt(pick_bf, g_prod[0]) + dot_nt(pick_bf, g_prod[1])
        s8 = jnp.concatenate([rows_ref[c, 0, 12:16, :], rows_ref[c, 1, 12:16, :]], axis=0)
        step8 = col8 / s8 + other_ref[:, span]
        flow_f = jnp.sum(meet[1, c + 1, :, FRONT] * meet[0, c, :, FRONT], axis=0, keepdims=True)
        under = lax.rem(c + chunks, chunks + 1)
        flow_m = jnp.sum(meet[1, under, :, MIRROR] * meet[0, c, :, MIRROR], axis=0, keepdims=True)
        flow8 = jnp.sum(pick * jnp.concatenate([flow_f, flow_m], axis=1), axis=1, keepdims=True)
        diff = split3(row8 - col8)
        front8 = iota((8, Q), 0) < 4
        decay8 = jnp.where(front8, dot_sum(diff, low_one), dot_sum(diff, up_one)) + flow8
        own_ref[0:4, span] = step8[0:4]
        own_ref[4:8, span] = decay8[0:4]
        other_ref[0:4, span] = step8[4:8]
        other_ref[4:8, span] = decay8[4:8]
        return carry

    own_rows = pl.ds(head_me * part_rows, part_rows)

    def add_up(w, n):
        sent[n]()
        total = part[w, own_rows, :]
        for k in range(1, nh):
            total = total + got[w, lax.rem(head_me + k, nh)]
        sums_ref[w] = total
        own = pltpu.make_async_copy(sums_ref.at[w], sums_hbm.at[w, own_rows], local_sems.at[5 + n])
        own.start()
        stores.append(own)
        return head_copies(
            lambda peer: sums_ref.at[w], sums_hbm.at[w, own_rows], head_sems.at[2, n], head_sems.at[3, n]
        )

    lax.fori_loop(0, chunks, across, 0)
    stores = [pltpu.make_async_copy(dx_ref, dx_hbm, local_sems.at[4])]
    stores[0].start()
    ny = nh // 2
    y_me, side = lax.rem(head_me, ny), head_me // ny
    x_head = lax.rem(head_me + ny, nh)
    others[y_me] = other_ref[...]

    def y_copy(k):
        peer = side * ny + lax.rem(y_me + k, ny)
        return remote(other_ref, others.at[y_me], other_sems.at[0, k], other_sems.at[1, k], "head", peer)

    shared = every(ny, y_copy)

    def find(head):
        place = 0 * head
        for k in range(nh * 4):
            place = jnp.where(heads_ref[k] == head, k, place)
        return place

    def row_of(place, row):
        return others[lax.rem(place // 4, ny), pl.ds(lax.rem(place, 4) + row, 1), :]

    ended = [add_up(core, 0)]
    shared()
    for h in range(4):
        place = find(x_head * 4 + h)
        far_out[h : h + 1, :] = row_of(place, 0)
        far_out[4 + h : 5 + h, :] = row_of(place, 4)
    far = remote(far_out, far_in, other_sems.at[0, 0], other_sems.at[1, 0], "head", x_head)
    far.start()
    ended.append(add_up(other, 1))
    far.wait()
    for h in range(4):
        place = find(head_me * 4 + h)
        near = place // (4 * ny) == side
        for row, target in ((0, dstep_ref), (4, ddecay_ref)):
            back = jnp.where(near, row_of(place, row), far_in[row + h : row + h + 1, :])
            target[h : h + 1, :] = own_ref[row + h : row + h + 1, :] + back
    for wait in ended:
        wait()
    for store in stores:
        store.wait()


def hand_on(dx_ref, sums_ref, step_ref, decay_ref, dx_out, db_out, dc_out, step_out, decay_out, dx, sums, step, decay, sems):
    pieces = []
    for c in range(dx_ref.shape[0] // Q):
        rows = slice(c * Q, (c + 1) * Q)
        for w, out in enumerate((db_out, dc_out)):
            pieces.append((sums_ref.at[w, rows], sums.at[w, rows], out.at[rows]))
        pieces.append((dx_ref.at[rows], dx.at[rows], dx_out.at[rows]))
    pieces.append((step_ref, step, step_out))
    pieces.append((decay_ref, decay, decay_out))
    loads = [pltpu.make_async_copy(a, b, sems.at[0, i]) for i, (a, b, _) in enumerate(pieces)]
    for load in loads:
        load.start()
    stores = []
    for i, (_, a, b) in enumerate(pieces):
        loads[i].wait()
        stores.append(pltpu.make_async_copy(a, b, sems.at[1, i]))
        stores[-1].start()
    for store in stores:
        store.wait()


def on_device(signal, write_keys, read_queries, step_sizes, log_decay, mirror_heads, contig_starts, out_grad):
    nh, ns = lax.axis_size("head"), lax.axis_size("seq")
    length = signal.shape[0]
    chunks = length // Q
    zs = ns // 4
    slice_rows = 256 // zs
    part_rows = length // nh
    vmem = pl.BlockSpec(memory_space=pltpu.VMEM)
    smem = pl.BlockSpec(memory_space=pltpu.SMEM)
    hbm = pl.BlockSpec(memory_space=pl.ANY)

    def shape(*dims, dtype=F32):
        return jax.ShapeDtypeStruct(dims, dtype)

    def room(*dims, dtype=F32):
        return pltpu.VMEM(dims, dtype)

    dx, sums, dstep, ddecay = pl.pallas_call(
        functools.partial(kernel, nh, ns),
        out_shape=[shape(length, 256), shape(2, length, 128), shape(4, length), shape(4, length)],
        in_specs=[smem] * 2 + [hbm] * 4 + [vmem] * 2,
        out_specs=[hbm] * 2 + [vmem] * 2,
        scratch_shapes=[
            room(length, 256, dtype=BF16),
            room(length, 256, dtype=BF16),
            room(length, 128, dtype=BF16),
            room(length, 128, dtype=BF16),
            room(chunks, 128, Q, dtype=BF16),
            room(chunks, 128, Q, dtype=BF16),
            room(length, 256),
            room(2, part_rows, 128),
            pltpu.SemaphoreType.DMA((7,)),
            room(nh, 8, length),
            room(chunks, 2, 16, Q),
            room(2, length, 16),
            room(2, length, 512, dtype=BF16),
            room(2, length, 512, dtype=BF16),
            room(length, 512),
            room(2, chunks, 128, 512),
            room(chunks, 8, 512),
            room(2, 2, 272, 128),
            room(2, 272, 128),
            room(2, zs, slice_rows + 8, 128),
            room(2, zs, slice_rows + 8, 128),
            room(2, zs, slice_rows, 128),
            room(2, slice_rows, 128),
            room(2, slice_rows, 128),
            room(2, zs, slice_rows, 128),
            room(2, 256, 128),
            room(2, 2, 256, 128),
            room(2, chunks + 1, 128, 512),
            room(Q, Q),
            room(4, Q, Q),
            room(4, Q, Q, dtype=BF16),
            room(4, Q, Q, dtype=BF16),
            room(Q, Q, dtype=BF16),
            room(Q, Q, dtype=BF16),
            room(Q, 128),
            room(chunks, 8, Q),
            room(chunks, 8, Q),
            room(2, length, 128),
            room(2, nh, part_rows, 128),
            room(8, length),
            room(8, length),
            room(nh // 2, 8, length),
            room(8, length),
            room(8, length),
            pltpu.SemaphoreType.DMA((2, nh)),
            pltpu.SemaphoreType.DMA((2, 6)),
            pltpu.SemaphoreType.DMA((2, 4, zs)),
            pltpu.SemaphoreType.DMA((4, 2, nh)),
            pltpu.SemaphoreType.DMA((2, nh)),
        ],
        compiler_params=pltpu.CompilerParams(
            vmem_limit_bytes=VMEM_LIMIT, collective_id=0, has_side_effects=True
        ),
        name="mixer_backward",
    )(mirror_heads, contig_starts, signal, out_grad, write_keys, read_queries, step_sizes, log_decay)

    return pl.pallas_call(
        hand_on,
        out_shape=[shape(length, 256), shape(length, 128), shape(length, 128), shape(4, length), shape(4, length)],
        in_specs=[hbm] * 4,
        out_specs=[hbm] * 5,
        scratch_shapes=[
            room(length, 256),
            room(2, length, 128),
            room(4, length),
            room(4, length),
            pltpu.SemaphoreType.DMA((2, 3 * chunks + 2)),
        ],
        compiler_params=pltpu.CompilerParams(vmem_limit_bytes=VMEM_LIMIT),
        name="hand_on",
    )(dx, sums, dstep, ddecay)


def solution(mesh):
    return jax.shard_map(
        on_device,
        mesh=mesh,
        in_specs=(
            P("seq", "head"),
            P("seq", None),
            P("seq", None),
            P("head", "seq"),
            P("head", "seq"),
            P(),
            P(),
            P("seq", "head"),
        ),
        out_specs=(
            P("seq", "head"),
            P("seq", None),
            P("seq", None),
            P("head", "seq"),
            P("head", "seq"),
        ),
        check_vma=False,
    )
```

```python
import functools

import jax
import jax.numpy as jnp
from jax import lax
from jax.experimental import pallas as pl
from jax.experimental.pallas import tpu as pltpu
from jax.sharding import PartitionSpec as P

Q = 256
STRIP = 32
LOG2E = 1.4426950408889634
F32, BF16 = jnp.float32, jnp.bfloat16
MESH = pl.DeviceIdType.MESH
VMEM_LIMIT = 56 * 1024 * 1024


def iota(shape, dim):
    return lax.broadcasted_iota(jnp.int32, shape, dim)


def split2(v):
    hi = v.astype(BF16)
    return hi, (v - hi.astype(F32)).astype(BF16)


def split3(v):
    hi = v.astype(BF16)
    rest = v - hi.astype(F32)
    mid = rest.astype(BF16)
    return hi, mid, (rest - mid.astype(F32)).astype(BF16)


def dot(a, b):
    return lax.dot_general(a, b, (((1,), (0,)), ((), ())), preferred_element_type=F32)


def dot_nt(a, b):
    return lax.dot_general(a, b, (((1,), (1,)), ((), ())), preferred_element_type=F32)


def dot_sum(parts, b, how=dot):
    total = how(parts[0], b)
    for part in parts[1:]:
        total = total + how(part, b)
    return total


def segment_at(starts_ref, t):
    total = (starts_ref[0] <= t).astype(jnp.int32)
    for k in range(1, 4):
        total = total + (starts_ref[k] <= t).astype(jnp.int32)
    return total


FRONT, MIRROR = slice(0, 256), slice(256, 512)
STRANDS = (FRONT, MIRROR)


def kernel(
    nh,
    ns,
    heads_ref,
    starts_ref,
    x_hbm,
    g_hbm,
    b_hbm,
    c_hbm,
    step_ref,
    decay_ref,
    dx_hbm,
    sums_hbm,
    dstep_ref,
    ddecay_ref,
    x_ref,
    g_ref,
    b_ref,
    c_ref,
    bt_ref,
    ct_ref,
    dx_ref,
    sums_ref,
    local_sems,
    all_ref,
    rows_ref,
    cols_ref,
    hi_ref,
    lo_ref,
    el_ref,
    terms_ref,
    gain_ref,
    pair_out,
    pair_in,
    slice_out,
    slice_in,
    scan_out,
    total_out,
    total_in,
    back_in,
    next_out,
    entering,
    meet,
    gm,
    pt,
    whi,
    wlo,
    dghi,
    dglo,
    csum,
    row_keep,
    col_keep,
    part,
    got,
    own_ref,
    other_ref,
    others,
    far_out,
    far_in,
    gather_sems,
    pair_sems,
    z_sems,
    head_sems,
    other_sems,
):
    length = x_ref.shape[0]
    chunks = length // Q
    head_me = lax.axis_index("head")
    seq_me = lax.axis_index("seq")
    offset = seq_me * length
    core = lax.rem(seq_me, 2)
    zs = ns // 4
    z_me = lax.rem(seq_me // 2, zs)
    x_me = seq_me // (2 * zs)
    core_peer = seq_me + 1 - 2 * core
    x_peer = lax.rem(seq_me + ns // 2, ns)

    def z_peer(k):
        z = lax.rem(z_me + k, zs)
        return z, x_me * 2 * zs + z * 2 + core

    loads = [
        pltpu.make_async_copy(a, b, local_sems.at[i])
        for i, (a, b) in enumerate(((x_hbm, x_ref), (g_hbm, g_ref), (b_hbm, b_ref), (c_hbm, c_ref)))
    ]
    for load in loads:
        load.start()

    all_ref[head_me, 0:4, :] = step_ref[...]
    all_ref[head_me, 4:8, :] = decay_ref[...]
    barrier = pltpu.get_barrier_semaphore()

    def greet_head(k, carry):
        peer = lax.rem(head_me + k, nh)
        pl.semaphore_signal(barrier, inc=1, device_id={"head": peer}, device_id_type=MESH)
        return carry

    def greet_z(k, carry):
        pl.semaphore_signal(barrier, inc=1, device_id={"seq": z_peer(k)[1]}, device_id_type=MESH)
        return carry

    lax.fori_loop(1, nh, greet_head, 0)
    lax.fori_loop(1, zs, greet_z, 0)
    pl.semaphore_signal(barrier, inc=1, device_id={"seq": core_peer}, device_id_type=MESH)
    pl.semaphore_signal(barrier, inc=1, device_id={"seq": x_peer}, device_id_type=MESH)
    pl.semaphore_wait(barrier, nh + zs)

    def remote(source, target, send, recv, axis, peer):
        return pltpu.make_async_remote_copy(
            src_ref=source,
            dst_ref=target,
            send_sem=send,
            recv_sem=recv,
            device_id={axis: peer},
            device_id_type=MESH,
        )

    def every(count, copy):
        def begin(k, carry):
            copy(k).start()
            return carry

        def end(k, carry):
            copy(k).wait()
            return carry

        lax.fori_loop(1, count, begin, 0)
        return lambda: lax.fori_loop(1, count, end, 0)

    def head_copies(source, target, send, recv):
        def copy(k):
            peer = lax.rem(head_me + k, nh)
            return remote(source(peer), target, send.at[k], recv.at[k], "head", peer)

        return every(nh, copy)

    def z_copies(source, target, send, recv):
        def copy(k):
            step = (k // 2) * (2 * lax.rem(k, 2) - 1)
            z, peer = z_peer(zs // 2 + step)
            return remote(source(z), target, send.at[k], recv.at[k], "seq", peer)

        return every(zs, copy)

    gathered = head_copies(
        lambda peer: all_ref.at[head_me], all_ref.at[head_me], gather_sems.at[0], gather_sems.at[1]
    )

    lower = iota((Q, Q), 0) >= iota((Q, Q), 1)
    upper = iota((Q, Q), 0) <= iota((Q, Q), 1)
    low_one = jnp.where(lower, 1.0, 0.0).astype(BF16)
    up_one = jnp.where(upper, 1.0, 0.0).astype(BF16)
    lane = iota((16, 512), 1)
    source = jnp.where(lane < 256, 8, 4) + (lane % 256) // 64
    spread = jnp.where(iota((16, 512), 0) == source, 1.0, 0.0).astype(BF16)
    pick8 = jnp.where(iota((8, 256), 0) == iota((8, 256), 1) // 64, 1.0, 0.0)


    def prepare(strand):
        def chunk(c):
            base = c * Q
            span = slice(base, base + Q)
            if strand == 0:
                s4 = all_ref[head_me, 0:4, span]
                d4 = all_ref[head_me, 4:8, span]
            else:
                heads = [heads_ref[head_me * 4 + h] for h in range(4)]
                s4 = jnp.concatenate([all_ref[i // 4, pl.ds(i % 4, 1), span] for i in heads], axis=0)
                d4 = jnp.concatenate([all_ref[i // 4, pl.ds(i % 4 + 4, 1), span] for i in heads], axis=0)
            s8 = jnp.concatenate([s4, s4], axis=0)
            d8 = jnp.concatenate([d4, d4], axis=0)
            cum8 = dot_sum(split3(d8), low_one if strand else up_one) * LOG2E
            total8 = cum8[:, 0:1] if strand else cum8[:, Q - 1 : Q]
            first = offset + base
            seg = segment_at(starts_ref, first + iota((8, Q), 1))
            seg_first, seg_last = segment_at(starts_ref, first), segment_at(starts_ref, first + Q - 1)
            if strand:
                seg_in, seg_far = segment_at(starts_ref, first + Q), seg_first
            else:
                seg_in = jnp.where(first == 0, -1, segment_at(starts_ref, first - 1))
                seg_far = seg_last
            e8 = jnp.where(seg == seg_in, jnp.exp2(cum8), 0.0)
            l8 = jnp.where(seg == seg_far, jnp.exp2(total8 - cum8) * s8, 0.0)
            gain8 = jnp.exp2(total8) * (seg_in == seg_far).astype(F32)
            gain = jnp.sum(pick8 * gain8, axis=0, keepdims=True)
            gain_ref[c, :, STRANDS[strand]] = jnp.broadcast_to(gain, (8, 256))
            rows = jnp.concatenate([cum8[0:4], e8[0:4], l8[0:4], s8[0:4]], axis=0)
            rows_ref[c, strand] = rows
            cols = rows.T
            cols_ref[strand, span, :] = cols
            wide = dot_sum(split3(cols), spread)
            lanes = STRANDS[strand]
            el_ref[span, lanes] = wide[:, 0:256]
            xhi, xlo = split2(x_ref[span, :].astype(F32) * wide[:, 0:256])
            ghi, glo = split2(g_ref[span, :].astype(F32) * wide[:, 256:512])
            hi_ref[0, span, lanes] = xhi
            lo_ref[0, span, lanes] = xlo
            hi_ref[1, span, lanes] = ghi
            lo_ref[1, span, lanes] = glo
            if strand == 0:
                bt_ref[c] = b_ref[span, :].T
                ct_ref[c] = c_ref[span, :].T
            bt, ct = bt_ref[c], ct_ref[c]
            terms_ref[1, c, :, lanes] = dot(bt, xhi) + dot(bt, xlo)
            terms_ref[0, c, :, lanes] = dot(ct, ghi) + dot(ct, glo)

        for c in range(chunks):
            chunk(c)


    ascending, descending = range(chunks), range(chunks - 1, -1, -1)
    way = (ascending, descending)

    def kind(strand, d):
        return d if strand else 1 - d

    def fold(strand):
        lanes = STRANDS[strand]
        for d in range(2):
            run = None
            for c in way[d]:
                term = terms_ref[kind(strand, d), c, :, lanes]
                run = term if run is None else run * gain_ref[c, 0:1, lanes] + term
            for k in range(2):
                pair_out[strand, d, k * 128 : (k + 1) * 128] = run[:, k * 128 : (k + 1) * 128]
        whole = gain_ref[0, :, lanes]
        for c in range(1, chunks):
            whole = whole * gain_ref[c, :, lanes]
        for d in range(2):
            for k in range(2):
                pair_out[strand, d, 256 + k * 8 : 264 + k * 8] = whole[:, k * 128 : (k + 1) * 128]


    half_mask = [jnp.where(iota((1, 128), 1) // 64 == k, 1.0, 0.0).astype(BF16) for k in range(2)]
    zero_row = jnp.zeros((8, 128), F32)
    part_rows = length // nh
    kept_sums = {}

    def inside(c, i):
        base = c * Q
        span = slice(base, base + Q)
        first = offset + base
        bc, cc = b_ref[span, :], c_ref[span, :]
        xs = [x_ref[span, k * 128 : (k + 1) * 128] for k in range(2)]
        gs = [g_ref[span, k * 128 : (k + 1) * 128] for k in range(2)]
        if i == 0:
            seg_s = segment_at(starts_ref, first + iota((Q, 1), 0))
            seg_t = segment_at(starts_ref, first + iota((1, Q), 1))
            gm[...] = jnp.where(seg_s == seg_t, dot_nt(bc, cc), 0.0)
            for h in range(4):
                pt[h] = dot_nt(xs[h // 2] * half_mask[h % 2], gs[h // 2])

        def strip(r, sums):
            start = pl.multiple_of(i * 128 + r * STRIP, STRIP)
            at = pl.ds(start, STRIP)
            at_cols = pl.ds(pl.multiple_of(base + start, STRIP), STRIP)
            col_f, col_m = cols_ref[0, at_cols, :], cols_ref[1, at_cols, :]
            lane128 = iota((STRIP, 128), 1)
            s_index = r * STRIP + iota((STRIP, 128), 0)
            ahead = lane128 > s_index
            behind = lane128 < s_index
            sums = list(sums)
            collected = jnp.zeros((STRIP, 128), F32)
            dg = [jnp.zeros((STRIP, 128), F32) for _ in range(2)]
            for h in range(4):
                cum_f, cum_m = col_f[:, h : h + 1], col_m[:, h : h + 1]
                step_f, step_m = col_f[:, 12 + h : 13 + h], col_m[:, 12 + h : 13 + h]
                lane_sums = [None, None]
                for j in range(2):
                    t = slice(j * 128, (j + 1) * 128)
                    row_f = rows_ref[c, 0, h : h + 1, t]
                    row_m = rows_ref[c, 1, h : h + 1, t]
                    if i == j:
                        gap = jnp.where(behind, row_m - cum_m, row_f - cum_f)
                        step = jnp.where(behind, step_m, jnp.where(ahead, step_f, step_f + step_m))
                    elif j > i:
                        gap, step = row_f - cum_f, step_f
                    else:
                        gap, step = row_m - cum_m, step_m
                    d = jnp.exp2(gap) * step
                    w = d * gm[at, t]
                    p = pt[h, at, t]
                    dg[j] = dg[j] + d * p
                    e = w * p
                    hi, lo = split2(w)
                    whi[h, at, t] = hi
                    wlo[h, at, t] = lo
                    if i == j:
                        parts = [jnp.where(ahead, e, 0.0), jnp.where(behind, e, 0.0)]
                    else:
                        parts = [e, None] if j > i else [None, e]
                    for strand in range(2):
                        piece = parts[strand]
                        if piece is None:
                            continue
                        slot = (h * 2 + j) * 2 + strand
                        add = piece[0:8]
                        for u in range(1, STRIP // 8):
                            add = add + piece[u * 8 : (u + 1) * 8]
                        sums[slot] = sums[slot] + add
                        old = lane_sums[strand]
                        lane_sums[strand] = piece if old is None else old + piece
                for strand in range(2):
                    total = jnp.sum(lane_sums[strand], axis=1, keepdims=True)
                    collected = jnp.where(lane128 == strand * 4 + h, total, collected)
            csum[at, :] = collected
            rows_at = segment_at(starts_ref, first + start + iota((STRIP, 1), 0))
            for j in range(2):
                t = slice(j * 128, (j + 1) * 128)
                cols_at = segment_at(starts_ref, first + j * 128 + iota((1, 128), 1))
                hi, lo = split2(jnp.where(rows_at == cols_at, dg[j], 0.0))
                dghi[at, t] = hi
                dglo[at, t] = lo
            return tuple(sums)

        kept_sums[i] = lax.fori_loop(0, 128 // STRIP, strip, (zero_row,) * 16)
        if i == 0:
            return
        row_sums = [kept_sums[0], kept_sums[1]]
        rows_in = []
        for strand in range(2):
            for h in range(4):
                lanes = []
                for j in range(2):
                    slot = (h * 2 + j) * 2 + strand
                    lanes.append(jnp.sum(row_sums[0][slot] + row_sums[1][slot], axis=0, keepdims=True))
                rows_in.append(jnp.concatenate(lanes, axis=1))
        row_keep[c] = jnp.concatenate(rows_in, axis=0)
        col_keep[c] = csum[...].T[0:8]
        for k in range(2):
            total = None
            for h in (2 * k, 2 * k + 1):
                masked = gs[k] * half_mask[h % 2]
                term = dot(whi[h], masked) + dot(wlo[h], masked)
                total = term if total is None else total + term
            dx_ref[span, k * 128 : (k + 1) * 128] = total
        part[0, span, :] = dot(dghi[...], cc) + dot(dglo[...], cc)
        dgt_hi, dgt_lo = dghi[...].T, dglo[...].T
        part[1, span, :] = dot(dgt_hi, bc) + dot(dgt_lo, bc)


    other = 1 - core
    slice_rows = 256 // zs
    half_slices = zs // 2
    waits = {}

    def gain_of(ref, k):
        return ref[256 + k * 8 : 257 + k * 8]

    def order(i):
        return i + core * (zs - 1 - 2 * i)

    def trade(strand):
        fold(strand)
        copy = remote(
            pair_out.at[strand, other],
            pair_in.at[strand],
            pair_sems.at[strand, 0],
            pair_sems.at[strand, 1],
            "seq",
            core_peer,
        )
        copy.start()
        waits["trade", strand] = copy.wait

    def spread_chip(strand):
        waits["trade", strand]()
        mine, theirs = pair_out.at[strand, core], pair_in.at[strand]
        for k in range(2):
            rows = slice(k * 128, (k + 1) * 128)
            slices = slice(k * half_slices, (k + 1) * half_slices)
            chip = gain_of(theirs, k) * mine[rows] + theirs[rows]
            slice_out[strand, slices, 0:slice_rows] = chip.reshape(half_slices, slice_rows, 128)
            gain = gain_of(theirs, k) * gain_of(mine, k)
            slice_out[strand, slices, slice_rows : slice_rows + 8] = jnp.broadcast_to(
                gain[None], (half_slices, 8, 128)
            )
        slice_in[strand, z_me] = slice_out[strand, z_me]
        waits["spread", strand] = z_copies(
            lambda z: slice_out.at[strand, z], slice_in.at[strand, z_me], z_sems.at[strand, 0], z_sems.at[strand, 1]
        )

    def scan_half(strand):
        waits["spread", strand]()
        run = jnp.zeros((slice_rows, 128), F32)
        for i in range(zs):
            z = order(i)
            scan_out[strand, z] = run
            run = slice_in[strand, z, slice_rows : slice_rows + 1] * run + slice_in[strand, z, 0:slice_rows]
        total_out[strand] = run
        copy = remote(
            total_out.at[strand],
            total_in.at[strand],
            pair_sems.at[strand, 2],
            pair_sems.at[strand, 3],
            "seq",
            x_peer,
        )
        copy.start()
        waits["swap", strand] = copy.wait

    def send_back(strand):
        waits["swap", strand]()
        run = total_in[strand] * jnp.where(x_me == 1 - core, 1.0, 0.0)
        for i in range(zs):
            z = order(i)
            scan_out[strand, z] = scan_out[strand, z] + run
            run = slice_in[strand, z, slice_rows : slice_rows + 1] * run
        back_in[strand, z_me] = scan_out[strand, z_me]
        waits["back", strand] = z_copies(
            lambda z: scan_out.at[strand, z], back_in.at[strand, z_me], z_sems.at[strand, 2], z_sems.at[strand, 3]
        )

    def pass_on(strand):
        waits["back", strand]()
        mine = pair_out.at[strand, core]
        for k in range(2):
            rows = slice(k * 128, (k + 1) * 128)
            enter = back_in[strand, k * half_slices : (k + 1) * half_slices].reshape(128, 128)
            entering[strand, core, rows] = enter
            next_out[strand, rows] = gain_of(mine, k) * enter + mine[rows]
        copy = remote(
            next_out.at[strand],
            entering.at[strand, core],
            pair_sems.at[strand, 4],
            pair_sems.at[strand, 5],
            "seq",
            core_peer,
        )
        copy.start()
        waits["pass", strand] = copy.wait

    def enter_chunks(strand, d):
        lanes = STRANDS[strand]
        w = kind(strand, d)
        run = jnp.concatenate([entering[strand, d, k * 128 : (k + 1) * 128] for k in range(2)], axis=1)
        for i in range(chunks):
            c = i + d * (chunks - 1 - 2 * i)
            meet[w, c, :, lanes] = run
            run = run * gain_ref[c, 0:1, lanes] + terms_ref[w, c, :, lanes]
        meet[w, chunks, :, lanes] = run

    def cross(strand, w):
        lanes = STRANDS[strand]
        for c in range(chunks):
            span = slice(c * Q, (c + 1) * Q)
            m_hi, m_lo = split2(meet[w, c, :, lanes])
            hi, lo = hi_ref[w, span, lanes], lo_ref[w, span, lanes]
            part[w, span, :] = part[w, span, :] + (dot_nt(hi, m_hi) + dot_nt(lo, m_hi) + dot_nt(hi, m_lo))

    def share(w, n):
        return head_copies(
            lambda peer: part.at[w, pl.ds(peer * part_rows, part_rows)],
            got.at[w, head_me],
            head_sems.at[0, n],
            head_sems.at[1, n],
        )

    for load in loads:
        load.wait()
    prepare(0)
    trade(0)
    gathered()
    spread_chip(0)
    prepare(1)
    trade(1)
    scan_half(0)
    inside(0, 0)
    spread_chip(1)
    inside(0, 1)
    inside(1, 0)
    inside(1, 1)
    scan_half(1)
    send_back(0)
    inside(2, 0)
    inside(2, 1)
    send_back(1)
    inside(3, 0)
    pass_on(0)
    inside(3, 1)
    waits["pass", 0]()
    for d in range(2):
        enter_chunks(0, d)
        cross(0, kind(0, d))
    pass_on(1)
    enter_chunks(1, core)
    cross(1, core)
    sent = [share(core, 0)]

    pick = jnp.where(iota((8, 512), 0) == iota((8, 512), 1) // 64, 1.0, 0.0)
    pick_bf = pick.astype(BF16)
    pick2_bf = jnp.where(iota((8, 256), 0) % 4 == iota((8, 256), 1) // 64, 1.0, 0.0).astype(BF16)
    ones_bf = jnp.ones((8, 128), BF16)

    def same_place(c, carry):
        span = pl.ds(pl.multiple_of(c * Q, Q), Q)
        bc_prod = split2(b_ref[span, :].astype(F32) * c_ref[span, :].astype(F32))
        score8 = dot_nt(ones_bf, bc_prod[0]) + dot_nt(ones_bf, bc_prod[1])
        xg = split2(x_ref[span, :].astype(F32) * g_ref[span, :].astype(F32))
        pair8 = dot_nt(pick2_bf, xg[0]) + dot_nt(pick2_bf, xg[1])
        other_ref[:, span] = score8 * pair8
        return carry

    waits["pass", 1]()
    enter_chunks(1, other)
    cross(1, other)
    sent.append(share(other, 1))
    lax.fori_loop(0, chunks, same_place, 0)

    def across(c, carry):
        span = pl.ds(pl.multiple_of(c * Q, Q), Q)
        state_hi, state_lo = split2(meet[1, c])
        adj_hi, adj_lo = split2(meet[0, c])
        bc, cc = b_ref[span, :], c_ref[span, :]
        v = dot(bc, adj_hi) + dot(bc, adj_lo)
        y = dot(cc, state_hi) + dot(cc, state_lo)
        scaled = el_ref[span, :] * v
        dx_ref[span, :] = dx_ref[span, :] + scaled[:, FRONT] + scaled[:, MIRROR]
        x_prod = split2((hi_ref[0, span, :].astype(F32) + lo_ref[0, span, :].astype(F32)) * v)
        g_prod = split2((hi_ref[1, span, :].astype(F32) + lo_ref[1, span, :].astype(F32)) * y)
        col8 = col_keep[c] + dot_nt(pick_bf, x_prod[0]) + dot_nt(pick_bf, x_prod[1])
        row8 = row_keep[c] + dot_nt(pick_bf, g_prod[0]) + dot_nt(pick_bf, g_prod[1])
        s8 = jnp.concatenate([rows_ref[c, 0, 12:16, :], rows_ref[c, 1, 12:16, :]], axis=0)
        step8 = col8 / s8 + other_ref[:, span]
        flow_f = jnp.sum(meet[1, c + 1, :, FRONT] * meet[0, c, :, FRONT], axis=0, keepdims=True)
        under = lax.rem(c + chunks, chunks + 1)
        flow_m = jnp.sum(meet[1, under, :, MIRROR] * meet[0, c, :, MIRROR], axis=0, keepdims=True)
        flow8 = jnp.sum(pick * jnp.concatenate([flow_f, flow_m], axis=1), axis=1, keepdims=True)
        diff = split3(row8 - col8)
        front8 = iota((8, Q), 0) < 4
        decay8 = jnp.where(front8, dot_sum(diff, low_one), dot_sum(diff, up_one)) + flow8
        own_ref[0:4, span] = step8[0:4]
        own_ref[4:8, span] = decay8[0:4]
        other_ref[0:4, span] = step8[4:8]
        other_ref[4:8, span] = decay8[4:8]
        return carry

    own_rows = pl.ds(head_me * part_rows, part_rows)

    def add_up(w, n):
        sent[n]()
        total = part[w, own_rows, :]
        for k in range(1, nh):
            total = total + got[w, lax.rem(head_me + k, nh)]
        sums_ref[w] = total
        own = pltpu.make_async_copy(sums_ref.at[w], sums_hbm.at[w, own_rows], local_sems.at[5 + n])
        own.start()
        stores.append(own)
        return head_copies(
            lambda peer: sums_ref.at[w], sums_hbm.at[w, own_rows], head_sems.at[2, n], head_sems.at[3, n]
        )

    lax.fori_loop(0, chunks, across, 0, unroll=True)
    stores = [pltpu.make_async_copy(dx_ref, dx_hbm, local_sems.at[4])]
    stores[0].start()
    ny = nh // 2
    y_me, side = lax.rem(head_me, ny), head_me // ny
    x_head = lax.rem(head_me + ny, nh)
    others[y_me] = other_ref[...]

    def y_copy(k):
        peer = side * ny + lax.rem(y_me + k, ny)
        return remote(other_ref, others.at[y_me], other_sems.at[0, k], other_sems.at[1, k], "head", peer)

    shared = every(ny, y_copy)

    def find(head):
        place = 0 * head
        for k in range(nh * 4):
            place = jnp.where(heads_ref[k] == head, k, place)
        return place

    def row_of(place, row):
        return others[lax.rem(place // 4, ny), pl.ds(lax.rem(place, 4) + row, 1), :]

    ended = [add_up(core, 0)]
    shared()
    for h in range(4):
        place = find(x_head * 4 + h)
        far_out[h : h + 1, :] = row_of(place, 0)
        far_out[4 + h : 5 + h, :] = row_of(place, 4)
    far = remote(far_out, far_in, other_sems.at[0, 0], other_sems.at[1, 0], "head", x_head)
    far.start()
    ended.append(add_up(other, 1))
    far.wait()
    for h in range(4):
        place = find(head_me * 4 + h)
        near = place // (4 * ny) == side
        for row, target in ((0, dstep_ref), (4, ddecay_ref)):
            back = jnp.where(near, row_of(place, row), far_in[row + h : row + h + 1, :])
            target[h : h + 1, :] = own_ref[row + h : row + h + 1, :] + back
    for wait in ended:
        wait()
    for store in stores:
        store.wait()


def hand_on(dx_ref, sums_ref, step_ref, decay_ref, dx_out, db_out, dc_out, step_out, decay_out, dx, sums, step, decay, sems):
    pieces = []
    for c in range(dx_ref.shape[0] // Q):
        rows = slice(c * Q, (c + 1) * Q)
        for w, out in enumerate((db_out, dc_out)):
            pieces.append((sums_ref.at[w, rows], sums.at[w, rows], out.at[rows]))
        pieces.append((dx_ref.at[rows], dx.at[rows], dx_out.at[rows]))
    pieces.append((step_ref, step, step_out))
    pieces.append((decay_ref, decay, decay_out))
    loads = [pltpu.make_async_copy(a, b, sems.at[0, i]) for i, (a, b, _) in enumerate(pieces)]
    for load in loads:
        load.start()
    stores = []
    for i, (_, a, b) in enumerate(pieces):
        loads[i].wait()
        stores.append(pltpu.make_async_copy(a, b, sems.at[1, i]))
        stores[-1].start()
    for store in stores:
        store.wait()


def on_device(signal, write_keys, read_queries, step_sizes, log_decay, mirror_heads, contig_starts, out_grad):
    nh, ns = lax.axis_size("head"), lax.axis_size("seq")
    length = signal.shape[0]
    chunks = length // Q
    zs = ns // 4
    slice_rows = 256 // zs
    part_rows = length // nh
    vmem = pl.BlockSpec(memory_space=pltpu.VMEM)
    smem = pl.BlockSpec(memory_space=pltpu.SMEM)
    hbm = pl.BlockSpec(memory_space=pl.ANY)

    def shape(*dims, dtype=F32):
        return jax.ShapeDtypeStruct(dims, dtype)

    def room(*dims, dtype=F32):
        return pltpu.VMEM(dims, dtype)

    dx, sums, dstep, ddecay = pl.pallas_call(
        functools.partial(kernel, nh, ns),
        out_shape=[shape(length, 256), shape(2, length, 128), shape(4, length), shape(4, length)],
        in_specs=[smem] * 2 + [hbm] * 4 + [vmem] * 2,
        out_specs=[hbm] * 2 + [vmem] * 2,
        scratch_shapes=[
            room(length, 256, dtype=BF16),
            room(length, 256, dtype=BF16),
            room(length, 128, dtype=BF16),
            room(length, 128, dtype=BF16),
            room(chunks, 128, Q, dtype=BF16),
            room(chunks, 128, Q, dtype=BF16),
            room(length, 256),
            room(2, part_rows, 128),
            pltpu.SemaphoreType.DMA((7,)),
            room(nh, 8, length),
            room(chunks, 2, 16, Q),
            room(2, length, 16),
            room(2, length, 512, dtype=BF16),
            room(2, length, 512, dtype=BF16),
            room(length, 512),
            room(2, chunks, 128, 512),
            room(chunks, 8, 512),
            room(2, 2, 272, 128),
            room(2, 272, 128),
            room(2, zs, slice_rows + 8, 128),
            room(2, zs, slice_rows + 8, 128),
            room(2, zs, slice_rows, 128),
            room(2, slice_rows, 128),
            room(2, slice_rows, 128),
            room(2, zs, slice_rows, 128),
            room(2, 256, 128),
            room(2, 2, 256, 128),
            room(2, chunks + 1, 128, 512),
            room(Q, Q),
            room(4, Q, Q),
            room(4, Q, Q, dtype=BF16),
            room(4, Q, Q, dtype=BF16),
            room(Q, Q, dtype=BF16),
            room(Q, Q, dtype=BF16),
            room(Q, 128),
            room(chunks, 8, Q),
            room(chunks, 8, Q),
            room(2, length, 128),
            room(2, nh, part_rows, 128),
            room(8, length),
            room(8, length),
            room(nh // 2, 8, length),
            room(8, length),
            room(8, length),
            pltpu.SemaphoreType.DMA((2, nh)),
            pltpu.SemaphoreType.DMA((2, 6)),
            pltpu.SemaphoreType.DMA((2, 4, zs)),
            pltpu.SemaphoreType.DMA((4, 2, nh)),
            pltpu.SemaphoreType.DMA((2, nh)),
        ],
        compiler_params=pltpu.CompilerParams(
            vmem_limit_bytes=VMEM_LIMIT, collective_id=0, has_side_effects=True
        ),
        name="mixer_backward",
    )(mirror_heads, contig_starts, signal, out_grad, write_keys, read_queries, step_sizes, log_decay)

    return pl.pallas_call(
        hand_on,
        out_shape=[shape(length, 256), shape(length, 128), shape(length, 128), shape(4, length), shape(4, length)],
        in_specs=[hbm] * 4,
        out_specs=[hbm] * 5,
        scratch_shapes=[
            room(length, 256),
            room(2, length, 128),
            room(4, length),
            room(4, length),
            pltpu.SemaphoreType.DMA((2, 3 * chunks + 2)),
        ],
        compiler_params=pltpu.CompilerParams(vmem_limit_bytes=VMEM_LIMIT),
        name="hand_on",
    )(dx, sums, dstep, ddecay)


def solution(mesh):
    return jax.shard_map(
        on_device,
        mesh=mesh,
        in_specs=(
            P("seq", "head"),
            P("seq", None),
            P("seq", None),
            P("head", "seq"),
            P("head", "seq"),
            P(),
            P(),
            P("seq", "head"),
        ),
        out_specs=(
            P("seq", "head"),
            P("seq", None),
            P("seq", None),
            P("head", "seq"),
            P("head", "seq"),
        ),
        check_vma=False,
    )
```
